32 devices in a mesh: tok: 8 (over z, core), ch: 4 (over y, x).
Axes of the slice: x: 2, y: 2, z: 4, core: 2. Of those that a mesh axis runs over, the one named last changes fastest.
Arguments:
- layer_in: bfloat16 [8192, 2048], P('tok', 'ch'), may hold values from -6 to 6
- positions: int32 [8192], P('tok'), may hold values from 0 to 3071, as said below
- norm_gain: float32 [2048], replicated, may hold values from 0.25 to 1.75
- w_branch: bfloat16 [2048, 2560], P(None, 'ch'), may hold values from -0.125 to 0.125
- w_gelu: bfloat16 [2048, 2560], P(None, 'ch'), may hold values from -0.125 to 0.125
- conv_w: float32 [4, 2560], P(None, 'ch'), may hold values from -3 to 3
- conv_b: float32 [2560], P('ch'), may hold values from -3 to 3
- w_rgate: bfloat16 [16, 160, 160], P('ch'), may hold values from -0.5 to 0.5
- b_rgate: float32 [2560], P('ch'), may hold values from -4 to 4
- w_igate: bfloat16 [16, 160, 160], P('ch'), may hold values from -0.5 to 0.5
- b_igate: float32 [2560], P('ch'), may hold values from -4 to 4
- decay_param: float32 [2560], P('ch'), may hold values from 3.5 to 11
- w_out: bfloat16 [2560, 2048], P('ch'), may hold values from -0.25 to 0.25
- mlp_gain: float32 [2048], replicated, may hold values from 0.25 to 1.75
- w_gate: bfloat16 [2048, 6144], P(None, 'ch'), may hold values from -0.125 to 0.125
- w_up: bfloat16 [2048, 6144], P(None, 'ch'), may hold values from -0.125 to 0.125
- w_down: bfloat16 [6144, 2048], P('ch'), may hold values from -0.15625 to 0.15625
- cotangent: bfloat16 [8192, 2048], P('tok', 'ch'), may hold values from -6 to 6
Outputs:
- layer_out: bfloat16 [8192, 2048], P('tok', 'ch')
- input_grad: float32 [8192, 2048], P('tok', 'ch')
- norm_gain_grad: float32 [2048], P('ch')
- w_branch_grad: float32 [2048, 2560], P('tok', 'ch')
- w_gelu_grad: float32 [2048, 2560], P('tok', 'ch')
- conv_w_grad: float32 [4, 2560], P(None, 'ch')
- conv_b_grad: float32 [2560], P('ch')
- w_rgate_grad: float32 [16, 160, 160], P('ch', 'tok')
- b_rgate_grad: float32 [2560], P('ch')
- w_igate_grad: float32 [16, 160, 160], P('ch', 'tok')
- b_igate_grad: float32 [2560], P('ch')
- decay_grad: float32 [2560], P('ch')
- w_out_grad: float32 [2560, 2048], P('ch', 'tok')
- mlp_gain_grad: float32 [2048], P('ch')
- w_gate_grad: float32 [2048, 6144], P('tok', 'ch')
- w_up_grad: float32 [2048, 6144], P('tok', 'ch')
- w_down_grad: float32 [6144, 2048], P('ch', 'tok')
The draws below stay inside these ranges and needn't reach their ends.
Inputs may be any that keep to these rules, and one draw needn't show every extreme that they name: positions count 0, 1, 2 and so on along each sequence; the sequences lie end to end from the first token to the last, each has 1024 tokens or more, and the longest reaches the largest position.
All inputs are finite; a program needn't handle non-finite values.
Results may differ from the reference program's by a relative error of at most 0.0093.
Values may be sent and summed in bfloat16 or wider, within the bound.
A program may use at most 256 MiB of HBM per device.

```python
import jax
import jax.numpy as jnp
from jax import lax

D = 2048
R = 2560
NB = 16
F = 6144
BW = 160
CONV_WIDTH = 4
MIN_LEN = 1024
TOKENS = 8192
SEQS = 4


def draw_positions(key, part):
    tokens_at = jnp.arange(TOKENS, dtype=jnp.int32)
    if SEQS == 1:
        return tokens_at
    spare_tokens = TOKENS - SEQS * MIN_LEN
    small_share = spare_tokens // 2
    large_share = spare_tokens - small_share
    cut_key = jax.random.fold_in(key, 11)
    slot_key = jax.random.fold_in(key, 23)
    cut_points = jnp.sort(jax.random.randint(cut_key, (SEQS - 2,), 0, small_share + 1).astype(jnp.int32))
    edges = jnp.concatenate([jnp.zeros((1,), jnp.int32), cut_points, jnp.full((1,), small_share, jnp.int32)])
    other_lengths = MIN_LEN + edges[1:] - edges[:-1]
    long_slot = jax.random.randint(slot_key, (), 0, SEQS).astype(jnp.int32)
    seq_ids = jnp.arange(SEQS, dtype=jnp.int32)
    lower_pick = other_lengths[jnp.clip(seq_ids, 0, SEQS - 2)]
    upper_pick = other_lengths[jnp.clip(seq_ids - 1, 0, SEQS - 2)]
    lengths = jnp.where(seq_ids < long_slot, lower_pick, jnp.where(seq_ids == long_slot, MIN_LEN + large_share, upper_pick)).astype(jnp.int32)
    starts = (jnp.cumsum(lengths) - lengths).astype(jnp.int32)
    seq_index = jnp.sum((starts[None, :] <= tokens_at[:, None]).astype(jnp.int32), axis=1) - 1
    return tokens_at - starts[seq_index]


def block_scale(rng, shape, split, smallest, largest):
    def one(axis_at, blocks):
        draws = jax.random.uniform(jax.random.fold_in(jax.random.fold_in(rng, 6), axis_at), (blocks,), jnp.float32, smallest / len(split), largest / len(split))
        return jnp.repeat(jnp.exp(draws), shape[axis_at] // blocks).reshape((-1,) + (1,) * (len(shape) - axis_at - 1))

    loudness = one(*split[0])
    for cut in split[1:]:
        loudness = loudness * one(*cut)
    return loudness


def gaussian(own_key, extent, spread, most, cuts=(), kind=jnp.bfloat16):
    values = jax.random.normal(own_key, extent, jnp.float32) * spread
    if len(cuts) > 0:
        values = block_scale(own_key, extent, cuts, -0.22, 0.18) * values
    return jnp.clip(values, min=-most, max=most).astype(kind)


def setup_inputs(seed: int = 0) -> dict:
    keys = jax.random.split(jax.random.key(seed), 19)
    return {
        "layer_in": gaussian(keys[0], (TOKENS, D), 1.0, 6.0, ((0, 8), (1, 4))),
        "positions": draw_positions(jax.random.fold_in(keys[18], 71), 0),
        "norm_gain": jnp.clip(1.0 + 0.15 * jax.random.normal(keys[2], (D,), jnp.float32), 0.25, 1.75),
        "w_branch": gaussian(keys[3], (D, R), D ** -0.5, 0.125, ((1, 4),)),
        "w_gelu": gaussian(keys[4], (D, R), D ** -0.5, 0.125, ((1, 4),)),
        "conv_w": gaussian(keys[5], (CONV_WIDTH, R), 0.5, 3.0, ((1, 4),), jnp.float32),
        "conv_b": gaussian(keys[6], (R,), 0.5, 3.0, ((0, 4),), jnp.float32),
        "w_rgate": gaussian(keys[7], (NB, BW, BW), BW ** -0.5, 0.5, ((0, 4),)),
        "b_rgate": gaussian(keys[8], (R,), 1.0, 4.0, ((0, 4),), jnp.float32),
        "w_igate": gaussian(keys[9], (NB, BW, BW), BW ** -0.5, 0.5, ((0, 4),)),
        "b_igate": gaussian(keys[10], (R,), 1.0, 4.0, ((0, 4),), jnp.float32),
        "decay_param": jnp.clip(3.5 + 7.5 * jax.random.uniform(keys[11], (R,), jnp.float32) ** block_scale(keys[11], (R,), ((0, 4),), -0.2, 0.2), 3.5, 11.0),
        "w_out": gaussian(keys[12], (R, D), (R // 4) ** -0.5, 0.25, ((0, 4),)),
        "mlp_gain": jnp.clip(1.0 + 0.15 * jax.random.normal(keys[13], (D,), jnp.float32), 0.25, 1.75),
        "w_gate": gaussian(keys[14], (D, F), D ** -0.5, 0.125, ((1, 4),)),
        "w_up": gaussian(keys[15], (D, F), D ** -0.5, 0.125, ((1, 4),)),
        "w_down": gaussian(keys[16], (F, D), (F // 4) ** -0.5, 0.15625, ((0, 4),)),
        "cotangent": gaussian(keys[17], (TOKENS, D), 1.0, 6.0, ((0, 8), (1, 4))),
    }


@jax.custom_vjp
def low(v):
    return lax.optimization_barrier(v.astype(jnp.bfloat16)).astype(jnp.float32)

@jax.custom_vjp
def low_back(v):
    return v

def low_keep(v):
    return (low(v), None)

def low_pass(kept, grad):
    return (grad,)

def back_keep(v):
    return (v, None)

def back_low(kept, grad):
    return (low(grad),)
low.defvjp(low_keep, low_pass)
low_back.defvjp(back_keep, back_low)
PRECISE = lax.Precision.HIGHEST

def matmul(first_in, second_in):
    return jnp.dot(first_in, second_in, precision=PRECISE, preferred_element_type=jnp.float32)

def rms_norm(values, gain_vec):
    return values * lax.rsqrt(lax.optimization_barrier(jnp.mean(values * values, axis=-1, keepdims=True)) + 1e-06) * gain_vec

def block_product(values, blocks):
    shaped = values.reshape(values.shape[0], blocks.shape[0], blocks.shape[1])
    return jnp.einsum('tnb,nbc->tnc', shaped, blocks, precision=PRECISE).reshape(values.shape[0], -1)

def combine(earlier, latter):
    return (earlier[0] * latter[0], latter[0] * earlier[1] + latter[1])

def gate_terms(pre_rate, pre_input, conv_out, decay_param, keep_mask):
    rate_gate = jax.nn.sigmoid(pre_rate)
    input_gate = jax.nn.sigmoid(pre_input)
    log_decay = -8.0 * rate_gate * jax.nn.softplus(-decay_param)
    decay_val = jnp.exp(log_decay)
    norm_scale = jnp.where(keep_mask > 0, jnp.sqrt(-jnp.expm1(2.0 * log_decay)), 1.0)
    return (decay_val * keep_mask, input_gate * conv_out * norm_scale)

def layer_forward(layer_in, positions, keep_mask, norm_gain, w_branch, w_gelu, conv_w, conv_b, w_rgate, b_rgate, w_igate, b_igate, decay_param, w_out, mlp_gain, w_gate, w_up, w_down):
    normed = low(rms_norm(layer_in, norm_gain))
    rec_in = low_back(matmul(normed, w_branch))
    gate_pre = low_back(matmul(normed, w_gelu))
    conv_out = conv_b + conv_w[0] * rec_in
    for offset in range(1, CONV_WIDTH):
        shifted = jnp.concatenate([jnp.zeros((offset, rec_in.shape[1]), jnp.float32), rec_in[:-offset]], axis=0)
        conv_out = conv_out + conv_w[offset] * shifted * (positions >= offset).astype(jnp.float32)[:, None]
    conv_low = low(conv_out)
    pre_rate = low_back(block_product(conv_low, w_rgate) + b_rgate)
    pre_input = low_back(block_product(conv_low, w_igate) + b_igate)
    step_decay, gated_in = gate_terms(pre_rate, pre_input, conv_out, decay_param, keep_mask)
    decays, lru_state = lax.associative_scan(combine, (step_decay, gated_in), axis=0)
    branch = low(lru_state * jax.nn.gelu(gate_pre))
    block_out = low_back(matmul(branch, w_out))
    middle = layer_in + block_out
    normed_mid = low(rms_norm(middle, mlp_gain))
    gate_val = low_back(matmul(normed_mid, w_gate))
    up_val = low_back(matmul(normed_mid, w_up))
    hidden = low(jax.nn.gelu(gate_val) * up_val)
    mlp_out = low_back(matmul(hidden, w_down))
    return middle + mlp_out

def reference(layer_in, positions, norm_gain, w_branch, w_gelu, conv_w, conv_b, w_rgate, b_rgate, w_igate, b_igate, decay_param, w_out, mlp_gain, w_gate, w_up, w_down, cotangent):
    keep_mask = (positions > 0).astype(jnp.float32)[:, None]
    weights_f32 = [weight.astype(jnp.float32) for weight in (norm_gain, w_branch, w_gelu, conv_w, conv_b, w_rgate, b_rgate, w_igate, b_igate, decay_param, w_out, mlp_gain, w_gate, w_up, w_down)]

    def forward(inputs, gain_one, branch_w, gelu_w, taps_w, taps_b, rgate_w, rgate_b, igate_w, igate_b, decay_in, out_w, gain_two, gate_w, up_w, down_w):
        return layer_forward(inputs, positions, keep_mask, gain_one, branch_w, gelu_w, taps_w, taps_b, rgate_w, rgate_b, igate_w, igate_b, decay_in, out_w, gain_two, gate_w, up_w, down_w)
    result, pullback = jax.vjp(forward, layer_in.astype(jnp.float32), weights_f32[0], weights_f32[1], weights_f32[2], weights_f32[3], weights_f32[4], weights_f32[5], weights_f32[6], weights_f32[7], weights_f32[8], weights_f32[9], weights_f32[10], weights_f32[11], weights_f32[12], weights_f32[13], weights_f32[14])
    gradients = pullback(cotangent.astype(jnp.float32))
    return (result.astype(jnp.bfloat16), gradients[0], gradients[1], gradients[2], gradients[3], gradients[4], gradients[5], gradients[6], gradients[7], gradients[8], gradients[9], gradients[10], gradients[11], gradients[12], gradients[13], gradients[14], gradients[15])
```

```python
import functools

import jax
import jax.numpy as jnp
from jax import lax
from jax.experimental import pallas as pl
from jax.experimental.pallas import tpu as pltpu
from jax.sharding import PartitionSpec as P

MESH = pl.DeviceIdType.MESH
F32 = jnp.float32
BF16 = jnp.bfloat16
SEGS = 8
GELU_A = 0.7978845608028654
GELU_B = 0.044715


def low_bit(mask):
    return (mask & -mask).bit_length() - 1


def high_bit(mask):
    return mask.bit_length() - 1


def gelu_parts(x):
    inner = jnp.tanh(GELU_A * (x + GELU_B * x * x * x))
    act = 0.5 * x * (1.0 + inner)
    slope = 0.5 * (1.0 + inner) + 0.5 * x * (1.0 - inner * inner) * GELU_A * (
        1.0 + 3.0 * GELU_B * x * x
    )
    return act, slope


def gelu_value(x):
    return 0.5 * x * (1.0 + jnp.tanh(GELU_A * (x + GELU_B * x * x * x)))


def minus_expm1(y, exp_y):
    series = 1.0 + y * (1.0 / 7.0)
    for k in (6, 5, 4, 3, 2):
        series = 1.0 + y * (1.0 / k) * series
    return jnp.where(y > -0.35, -y * series, 1.0 - exp_y)


def nt_dot(a, b):
    return lax.dot_general(a, b, (((1,), (1,)), ((), ())), preferred_element_type=F32)


def tn_dot(a, b):
    return lax.dot_general(a, b, (((0,), (0,)), ((), ())), preferred_element_type=F32)


def lane_tiles(chans):
    return [(j, min(128, chans - 128 * j)) for j in range(-(-chans // 128))]


def put_tiles(ref, span, value):
    for j, lanes in lane_tiles(value.shape[1]):
        ref[j, span, :lanes] = value[:, 128 * j : 128 * j + lanes]


def get_tiles(ref, span, chans):
    return jnp.concatenate(
        [ref[j, span, :lanes] for j, lanes in lane_tiles(chans)], axis=1
    )


def join_tiles(parts, chans):
    return jnp.concatenate(
        [part[:, :lanes] for part, (_, lanes) in zip(parts, lane_tiles(chans), strict=True)],
        axis=1,
    )


def whole_vmem(count):
    return [pl.BlockSpec(memory_space=pltpu.VMEM)] * count


def greet(targets):
    barrier = pltpu.get_barrier_semaphore()
    for target in targets:
        pl.semaphore_signal(barrier, inc=1, device_id=target, device_id_type=MESH)
    pl.semaphore_wait(barrier, len(targets))


def gather_kernel(n, chunks, x, out, send, recv, send_f, recv_f, here):
    tok, me = lax.axis_index("tok"), lax.axis_index("ch")
    bits = n.bit_length() - 1
    rows, width = x.shape
    size, half = rows // chunks, width // 2
    greet([(tok, me ^ (1 << b)) for b in range(bits)])

    def place(owner, part, c):
        span = pl.ds(c * size, size)
        if part is None:
            return out.at[span, pl.ds(pl.multiple_of(owner * width, 128), width)]
        return out.at[span, pl.ds(pl.multiple_of(owner * width + part * half, 128), half)]

    own = pltpu.make_async_copy(
        x, out.at[:, pl.ds(pl.multiple_of(me * width, 128), width)], here
    )
    own.start()
    started = []
    for c in range(chunks):
        for b in range(bits):
            copy = pltpu.make_async_remote_copy(
                x.at[pl.ds(c * size, size)],
                place(me, None, c),
                send.at[b, c],
                recv.at[b, c],
                (tok, me ^ (1 << b)),
                MESH,
            )
            copy.start()
            started.append(copy)
    for c in range(chunks):
        for count in range(1, bits):
            for mask in [m for m in range(1, n) if m.bit_count() == count]:
                if count == 1:
                    b = low_bit(mask)
                    pltpu.make_async_remote_copy(
                        x.at[pl.ds(c * size, size)],
                        place(me ^ mask, None, c),
                        send.at[b, c],
                        recv.at[b, c],
                        (tok, me ^ (1 << b)),
                        MESH,
                    ).wait_recv()
                for part in range(2):
                    nexts = (
                        range(high_bit(mask) + 1, bits) if part == 0 else range(low_bit(mask))
                    )
                    block = place(me ^ mask, part, c)
                    if count > 1:
                        pltpu.make_async_remote_copy(
                            block, block, send_f.at[part, mask, c], recv_f.at[part, mask, c],
                            (tok, me ^ 1), MESH,
                        ).wait_recv()
                    for b in nexts:
                        got = mask | (1 << b)
                        copy = pltpu.make_async_remote_copy(
                            block,
                            block,
                            send_f.at[part, got, c],
                            recv_f.at[part, got, c],
                            (tok, me ^ (1 << b)),
                            MESH,
                        )
                        copy.start()
                        started.append(copy)
    for c in range(chunks):
        mask = n - 1
        for part in range(2):
            block = place(me ^ mask, part, c)
            pltpu.make_async_remote_copy(
                block, block, send_f.at[part, mask, c], recv_f.at[part, mask, c],
                (tok, me ^ 1), MESH,
            ).wait_recv()
    for copy in started:
        copy.wait_send()
    own.wait()


def gather_columns(x, ident, chunks=4):
    n = lax.axis_size("ch")
    bits = n.bit_length() - 1
    rows, width = x.shape
    return pl.pallas_call(
        functools.partial(gather_kernel, n, chunks),
        out_shape=jax.ShapeDtypeStruct((rows, n * width), x.dtype),
        in_specs=[pl.BlockSpec(memory_space=pl.ANY)],
        out_specs=pl.BlockSpec(memory_space=pl.ANY),
        scratch_shapes=[
            pltpu.SemaphoreType.DMA((bits, chunks)),
            pltpu.SemaphoreType.DMA((bits, chunks)),
            pltpu.SemaphoreType.DMA((2, n, chunks)),
            pltpu.SemaphoreType.DMA((2, n, chunks)),
            pltpu.SemaphoreType.DMA,
        ],
        compiler_params=pltpu.CompilerParams(collective_id=ident, has_side_effects=True),
    )(x)


def tok_targets():
    count = lax.axis_size("tok")
    tok, ch = lax.axis_index("tok"), lax.axis_index("ch")
    return [(lax.rem(tok + o, count), ch) for o in range(1, count)]


def share_rows(buffer, send, recv):
    tok = lax.axis_index("tok")
    copies = []
    for o, target in enumerate(tok_targets()):
        copy = pltpu.make_async_remote_copy(
            buffer.at[tok], buffer.at[tok], send.at[o], recv.at[o], target, MESH
        )
        copy.start()
        copies.append(copy)
    count = lax.axis_size("tok")
    for o in range(count - 1):
        source = lax.rem(tok + count - 1 - o, count)
        pltpu.make_async_remote_copy(
            buffer.at[source], buffer.at[source], send.at[o], recv.at[o], tok_targets()[o], MESH
        ).wait_recv()
    return copies


def recur_fwd_kernel(
    rec, gpre, pos, cw, cb, wr, br, wi, bi, sp,
    ext, conv, rate, igate, lru, branch,
    low, a_s, h_s, halo, seg, ends, halo_send, halo_recv, send, recv,
):
    rows, chans = rec.shape
    taps = cw.shape[0]
    tok, ch = lax.axis_index("tok"), lax.axis_index("ch")
    count = lax.axis_size("tok")
    greet(tok_targets())
    halo_copy = pltpu.make_async_remote_copy(
        rec.at[pl.ds(rows - 8, 8)], halo, halo_send, halo_recv,
        (lax.rem(tok + 1, count), ch), MESH,
    )
    halo_copy.start()

    step = 16

    def spread(i, _):
        ext[pl.ds(8 + i * step, step), :] = rec[pl.ds(i * step, step), :]
        return 0

    lax.fori_loop(0, rows // step, spread, 0, unroll=4)
    halo_copy.wait()
    ext[0:8, :] = jnp.where(tok > 0, halo[...], 0.0)

    def conv_rows(i, _):
        window = ext[pl.ds(i * step, step + 8), :]
        at = pos[pl.ds(i * step, step), :]
        total = cb[...] + cw[0:1, :] * window[8 : 8 + step]
        for k in range(1, taps):
            total = total + jnp.where(at >= k, cw[k : k + 1, :] * window[8 - k : 8 - k + step], 0.0)
        conv[pl.ds(i * step, step), :] = total
        low[pl.ds(i * step, step), :] = total.astype(BF16)
        return 0

    lax.fori_loop(0, rows // step, conv_rows, 0, unroll=2)

    big = min(256, rows)

    def products(i, _):
        span = pl.ds(i * big, big)
        rate[span, :] = jnp.dot(low[span, :], wr[...], preferred_element_type=F32) + br[...]
        igate[span, :] = jnp.dot(low[span, :], wi[...], preferred_element_type=F32) + bi[...]
        return 0

    lax.fori_loop(0, rows // big, products, 0)

    def gates(i, _):
        span = pl.ds(i * step, step)
        at = pos[span, :]
        r = jax.nn.sigmoid(rate[span, :])
        g = jax.nn.sigmoid(igate[span, :])
        rate[span, :] = r
        igate[span, :] = g
        log_decay = -8.0 * r * sp[...]
        decay = jnp.exp(log_decay)
        mult = jnp.sqrt(minus_expm1(2.0 * log_decay, decay * decay))
        mult = jnp.where(at > 0, mult, 1.0)
        put_tiles(a_s, span, jnp.where(at > 0, decay, 0.0))
        put_tiles(h_s, span, g * conv[span, :] * mult)
        return 0

    lax.fori_loop(0, rows // step, gates, 0, unroll=2)

    length = rows // SEGS

    def scan(t, carry):
        span = pl.ds(t, SEGS, stride=length)
        after = []
        for j, (h, p) in enumerate(carry):
            a = a_s[j, span, :]
            h = a * h + h_s[j, span, :]
            p = a * p
            h_s[j, span, :] = h
            a_s[j, span, :] = p
            after.append((h, p))
        return tuple(after)

    nothing = tuple(
        (jnp.zeros((SEGS, 128), F32), jnp.ones((SEGS, 128), F32)) for _ in lane_tiles(chans)
    )
    found = lax.fori_loop(0, length, scan, nothing, unroll=8)
    h_end = join_tiles([h for h, _ in found], chans)
    p_end = join_tiles([p for _, p in found], chans)
    total_h, total_p = jnp.zeros((1, chans), F32), jnp.ones((1, chans), F32)
    for s in range(SEGS):
        total_h = p_end[s : s + 1] * total_h + h_end[s : s + 1]
        total_p = p_end[s : s + 1] * total_p
    ends[tok, 0:1, :] = total_h
    ends[tok, 1:2, :] = total_p
    sends = share_rows(ends, send, recv)
    state = jnp.zeros((1, chans), F32)
    for source in range(count - 1):
        after = ends[source, 1:2, :] * state + ends[source, 0:1, :]
        state = jnp.where(source < tok, after, state)
    lru[0:8, :] = jnp.broadcast_to(state, (8, chans))
    for s in range(SEGS):
        seg[s : s + 1, :] = state
        state = p_end[s : s + 1] * state + h_end[s : s + 1]

    per = length // step

    def finish(i, _):
        span = pl.ds(i * step, step)
        entering = seg[pl.ds(i // per, 1), :]
        value = get_tiles(h_s, span, chans) + get_tiles(a_s, span, chans) * entering
        lru[pl.ds(8 + i * step, step), :] = value
        branch[span, :] = (value * gelu_value(gpre[span, :])).astype(BF16)
        return 0

    lax.fori_loop(0, rows // step, finish, 0, unroll=2)
    for copy in sends:
        copy.wait_send()


def recur_fwd(rec, gpre, pos, cw, cb, wr, br, wi, bi, sp, ident):
    rows, chans = rec.shape
    count = lax.axis_size("tok")
    grid = jax.ShapeDtypeStruct((rows, chans), F32)
    tall = jax.ShapeDtypeStruct((rows + 8, chans), F32)
    return pl.pallas_call(
        recur_fwd_kernel,
        out_shape=[tall, grid, grid, grid, tall, jax.ShapeDtypeStruct((rows, chans), BF16)],
        in_specs=whole_vmem(10),
        out_specs=whole_vmem(6),
        scratch_shapes=[
            pltpu.VMEM((rows, chans), BF16),
            pltpu.VMEM((len(lane_tiles(chans)), rows, 128), F32),
            pltpu.VMEM((len(lane_tiles(chans)), rows, 128), F32),
            pltpu.VMEM((8, chans), F32),
            pltpu.VMEM((SEGS, chans), F32),
            pltpu.VMEM((count, 8, chans), F32),
            pltpu.SemaphoreType.DMA,
            pltpu.SemaphoreType.DMA,
            pltpu.SemaphoreType.DMA((count - 1,)),
            pltpu.SemaphoreType.DMA((count - 1,)),
        ],
        compiler_params=pltpu.CompilerParams(
            collective_id=ident, has_side_effects=True, vmem_limit_bytes=56 << 20
        ),
    )(rec, gpre, pos, cw, cb, wr, br, wi, bi, sp)


def recur_bwd_kernel(
    gb, gpre, ext, conv, rate, igate, lru, pos, cw, wr, wi, sp, sg,
    grec, ggp, grate, ginput, sums, row_term,
    g_s, a_s, gc, seg, ends, edge, landed, acc, edge_send, edge_recv, send, recv,
):
    rows, chans = gb.shape
    taps = cw.shape[0]
    tok, ch = lax.axis_index("tok"), lax.axis_index("ch")
    count = lax.axis_size("tok")
    greet(tok_targets())
    step = 16
    length = rows // SEGS
    per = length // step

    def begin(i, _):
        span = pl.ds(i * step, step)
        act, slope = gelu_parts(gpre[span, :])
        grad = gb[span, :]
        put_tiles(g_s, span, grad * act)
        ggp[span, :] = (grad * lru[pl.ds(8 + i * step, step), :] * slope).astype(BF16)
        at = pos[span, :]
        put_tiles(a_s, span, jnp.where(at > 0, jnp.exp(-8.0 * rate[span, :] * sp[...]), 0.0))
        return 0

    lax.fori_loop(0, rows // step, begin, 0, unroll=2)

    def scan(t, carry):
        span = pl.ds(length - 1 - t, SEGS, stride=length)
        after = []
        for j, (v, q) in enumerate(carry):
            a = a_s[j, span, :]
            c = g_s[j, span, :] + v
            g_s[j, span, :] = c
            a_s[j, span, :] = q
            after.append((a * c, a * q))
        return tuple(after)

    nothing = tuple(
        (jnp.zeros((SEGS, 128), F32), jnp.ones((SEGS, 128), F32)) for _ in lane_tiles(chans)
    )
    found = lax.fori_loop(0, length, scan, nothing, unroll=8)
    v_end = join_tiles([v for v, _ in found], chans)
    q_end = join_tiles([q for _, q in found], chans)
    total_v, total_q = jnp.zeros((1, chans), F32), jnp.ones((1, chans), F32)
    for s in reversed(range(SEGS)):
        total_v = q_end[s : s + 1] * total_v + v_end[s : s + 1]
        total_q = q_end[s : s + 1] * total_q
    ends[tok, 0:1, :] = total_v
    ends[tok, 1:2, :] = total_q
    sends = share_rows(ends, send, recv)
    state = jnp.zeros((1, chans), F32)
    for source in reversed(range(1, count)):
        after = ends[source, 1:2, :] * state + ends[source, 0:1, :]
        state = jnp.where(source > tok, after, state)
    for s in reversed(range(SEGS)):
        seg[s : s + 1, :] = state
        state = q_end[s : s + 1] * state + v_end[s : s + 1]

    acc[...] = jnp.zeros_like(acc)

    def folded(x):
        return jnp.sum(x.reshape(-1, 8, chans), axis=0)

    def middle(i, _):
        span = pl.ds(i * step, step)
        carried = get_tiles(g_s, span, chans)
        carried = carried + get_tiles(a_s, span, chans) * seg[pl.ds(i // per, 1), :]
        before = lru[pl.ds(i * step, step + 8), :][7 : 7 + step]
        keep = pos[span, :] > 0
        r, g, out = rate[span, :], igate[span, :], conv[span, :]
        log_decay = -8.0 * r * sp[...]
        decay = jnp.exp(log_decay)
        square = decay * decay
        mult = jnp.where(keep, jnp.sqrt(minus_expm1(2.0 * log_decay, square)), 1.0)
        scaled = carried * g
        grad_log = jnp.where(
            keep, decay * carried * before - scaled * out * square / mult, 0.0
        )
        slope = 8.0 * r * grad_log
        grad_rate = (-slope * sp[...] * (1.0 - r)).astype(BF16)
        grad_input = (scaled * out * mult * (1.0 - g)).astype(BF16)
        grate[span, :] = grad_rate
        ginput[span, :] = grad_input
        gc[span, :] = scaled * mult
        acc[0] += folded(slope * sg[...])
        acc[1] += folded(grad_rate.astype(F32))
        acc[2] += folded(grad_input.astype(F32))
        return 0

    lax.fori_loop(0, rows // step, middle, 0)
    big = min(256, rows)

    def products(i, _):
        span = pl.ds(i * big, big)
        gc[span, :] += nt_dot(grate[span, :], wr[...]) + nt_dot(ginput[span, :], wi[...])
        return 0

    lax.fori_loop(0, rows // big, products, 0)
    gc[pl.ds(rows, 8), :] = jnp.zeros((8, chans), F32)

    first = gc[0:8, :]
    first_at = pos[0:8, :]
    total = jnp.zeros((8, chans), F32)
    for k in range(1, taps):
        masked = jnp.where(first_at >= k, cw[k : k + 1, :] * first, 0.0)
        total = total + jnp.concatenate([jnp.zeros((8, chans), F32), masked], axis=0)[k : k + 8]
    edge[...] = total
    edge_copy = pltpu.make_async_remote_copy(
        edge, landed, edge_send, edge_recv, (lax.rem(tok + count - 1, count), ch), MESH
    )
    edge_copy.start()

    def last(i, _):
        span = pl.ds(i * step, step)
        window = gc[pl.ds(i * step, step + 8), :]
        at = pos[pl.ds(i * step, step + 8), :]
        source = ext[pl.ds(i * step, step + 8), :]
        here = window[:step]
        total = cw[0:1, :] * here
        acc[3] += folded(here)
        acc[4] += folded(here * source[8 : 8 + step])
        for k in range(1, taps):
            masked = jnp.where(at >= k, window, 0.0)
            total = total + cw[k : k + 1, :] * masked[k : k + step]
            acc[4 + k] += folded(masked[:step] * source[8 - k : 8 - k + step])
        grec[span, :] = total.astype(BF16)
        return 0

    lax.fori_loop(0, rows // step, last, 0)
    edge_copy.wait()
    tail = jnp.concatenate([jnp.zeros((8, chans), F32), landed[...]], axis=0)
    span = pl.ds(rows - 16, 16)
    window = gc[pl.ds(rows - 16, 24), :]
    at = pos[pl.ds(rows - 16, 24), :]
    total = cw[0:1, :] * window[:16] + jnp.where(tok < count - 1, tail, 0.0)
    for k in range(1, taps):
        masked = jnp.where(at >= k, window, 0.0)
        total = total + cw[k : k + 1, :] * masked[k : k + 16]
    grec[span, :] = total.astype(BF16)

    def stat(i, _):
        span = pl.ds(i * step, step)
        both = grec[span, :].astype(F32) * ext[pl.ds(8 + i * step, step), :]
        both = both + ggp[span, :].astype(F32) * gpre[span, :]
        row_term[span, :] = jnp.sum(both, axis=1, keepdims=True)
        return 0

    lax.fori_loop(0, rows // step, stat, 0, unroll=2)
    for k in range(8):
        sums[k : k + 1, :] = jnp.sum(acc[k], axis=0, keepdims=True)
    for copy in sends:
        copy.wait_send()


def recur_bwd(gb, gpre, ext, conv, rate, igate, lru, pos, cw, wr, wi, sp, sg, ident):
    rows, chans = gb.shape
    count = lax.axis_size("tok")
    half = jax.ShapeDtypeStruct((rows, chans), BF16)
    return pl.pallas_call(
        recur_bwd_kernel,
        out_shape=[
            half, half, half, half,
            jax.ShapeDtypeStruct((8, chans), F32),
            jax.ShapeDtypeStruct((rows, 1), F32),
        ],
        in_specs=whole_vmem(13),
        out_specs=whole_vmem(6),
        scratch_shapes=[
            pltpu.VMEM((len(lane_tiles(chans)), rows, 128), F32),
            pltpu.VMEM((len(lane_tiles(chans)), rows, 128), F32),
            pltpu.VMEM((rows + 8, chans), F32),
            pltpu.VMEM((SEGS, chans), F32),
            pltpu.VMEM((count, 8, chans), F32),
            pltpu.VMEM((8, chans), F32),
            pltpu.VMEM((8, chans), F32),
            pltpu.VMEM((8, 8, chans), F32),
            pltpu.SemaphoreType.DMA,
            pltpu.SemaphoreType.DMA,
            pltpu.SemaphoreType.DMA((count - 1,)),
            pltpu.SemaphoreType.DMA((count - 1,)),
        ],
        compiler_params=pltpu.CompilerParams(
            collective_id=ident, has_side_effects=True, vmem_limit_bytes=60 << 20
        ),
    )(gb, gpre, ext, conv, rate, igate, lru, pos, cw, wr, wi, sp, sg)


class Exchange:
    def __init__(self, n, rows, width, chunks, gather):
        self.n, self.rows, self.width, self.chunks, self.gather = n, rows, width, chunks, gather
        self.bits = n.bit_length() - 1
        self.half = width // 2
        self.size = rows // chunks
        self.keeps = [(part, m) for part in range(2) for m in range(n) if self.incoming(part, m)]

    def scratch(self):
        n, rows, half, chunks = self.n, self.rows, self.half, self.chunks
        shapes = [
            pltpu.VMEM((2, n, rows, half), BF16),
            pltpu.VMEM((2, n, rows, half), BF16),
            pltpu.VMEM((len(self.keeps), rows, half), F32),
            pltpu.SemaphoreType.DMA((2, n, chunks)),
            pltpu.SemaphoreType.DMA((2, n, chunks)),
        ]
        if self.gather:
            shapes += [
                pltpu.VMEM((n, 2, rows, half), BF16),
                pltpu.SemaphoreType.DMA((self.bits, 2, chunks)),
                pltpu.SemaphoreType.DMA((self.bits, 2, chunks)),
                pltpu.SemaphoreType.DMA((2, n, chunks)),
                pltpu.SemaphoreType.DMA((2, n, chunks)),
            ]
        return shapes

    def bind(self, refs):
        if self.gather:
            (self.out, self.into, self.acc, self.ss, self.rs,
             self.full, self.gs, self.gr, self.fs, self.fr) = refs
        else:
            self.out, self.into, self.acc, self.ss, self.rs = refs
        self.tok, self.me = lax.axis_index("tok"), lax.axis_index("ch")

    def neighbours(self):
        return [self.peer(b) for b in range(self.bits)]

    def peer(self, b):
        return (self.tok, self.me ^ (1 << b))

    def bit_of(self, part, mask):
        return low_bit(mask) if part == 0 else high_bit(mask)

    def incoming(self, part, mask):
        if mask == 0:
            return list(range(self.bits)) if part == 0 else list(reversed(range(self.bits)))
        if part == 0:
            return list(range(low_bit(mask)))
        return list(reversed(range(high_bit(mask) + 1, self.bits)))

    def stage_of(self, part, mask):
        return low_bit(mask) if part == 0 else self.bits - 1 - high_bit(mask)

    def span(self, c):
        return pl.ds(pl.multiple_of(c * self.size, self.size), self.size)

    def reduce_copy(self, part, mask, c):
        return pltpu.make_async_remote_copy(
            self.out.at[part, mask, self.span(c)],
            self.into.at[part, mask, self.span(c)],
            self.ss.at[part, mask, c],
            self.rs.at[part, mask, c],
            self.peer(self.bit_of(part, mask)),
            MESH,
        )

    def produce(self, c, block):
        span = self.span(c)
        for mask in sorted(range(self.n), key=lambda m: -m.bit_count()):
            value = block(mask)
            for part in range(2):
                piece = value[:, part * self.half : (part + 1) * self.half]
                if (part, mask) in self.keeps:
                    self.acc[self.keeps.index((part, mask)), span, :] = piece
                else:
                    self.out[part, mask, span, :] = piece.astype(BF16)
                    self.reduce_copy(part, mask, c).start()

    def summed(self, part, mask, c):
        span = self.span(c)
        value = self.acc[self.keeps.index((part, mask)), span, :]
        for b in self.incoming(part, mask):
            came = mask | (1 << b)
            self.reduce_copy(part, came, c).wait_recv()
            value = value + self.into[part, came, span, :].astype(F32)
        return value

    def pass_on(self, stage, c):
        for part in range(2):
            for mask in range(1, self.n):
                if self.stage_of(part, mask) == stage:
                    value = self.summed(part, mask, c)
                    self.out[part, mask, self.span(c), :] = value.astype(BF16)
                    self.reduce_copy(part, mask, c).start()

    def close_reduce(self, c):
        for part in range(2):
            for mask in range(1, self.n):
                self.reduce_copy(part, mask, c).wait_send()

    def gather_copy(self, part, mask, b, c):
        block = self.full.at[self.me ^ mask, part, self.span(c)]
        if mask == 0:
            return pltpu.make_async_remote_copy(
                block, block, self.gs.at[b, part, c], self.gr.at[b, part, c], self.peer(b), MESH
            )
        got = mask | (1 << b)
        return pltpu.make_async_remote_copy(
            block, block, self.fs.at[part, got, c], self.fr.at[part, got, c], self.peer(b), MESH
        )

    def arrived(self, part, mask, c):
        block = self.full.at[self.me ^ mask, part, self.span(c)]
        if mask.bit_count() == 1:
            b = low_bit(mask)
            sems = (self.gs.at[b, part, c], self.gr.at[b, part, c])
        else:
            sems = (self.fs.at[part, mask, c], self.fr.at[part, mask, c])
        pltpu.make_async_remote_copy(block, block, *sems, self.peer(0), MESH).wait_recv()

    def gather_start(self, c, halves):
        for part in range(2):
            self.full[self.me, part, self.span(c), :] = halves[part].astype(BF16)
            for b in range(self.bits):
                self.gather_copy(part, 0, b, c).start()

    def nexts(self, part, mask):
        return range(high_bit(mask) + 1, self.bits) if part == 0 else range(low_bit(mask))

    def gather_pass(self, stage, c):
        for mask in [m for m in range(1, self.n) if m.bit_count() == stage]:
            for part in range(2):
                self.arrived(part, mask, c)
                for b in self.nexts(part, mask):
                    self.gather_copy(part, mask, b, c).start()

    def gather_close(self, c):
        for part in range(2):
            self.arrived(part, self.n - 1, c)
        for part in range(2):
            for b in range(self.bits):
                self.gather_copy(part, 0, b, c).wait_send()
            for mask in range(1, self.n):
                for b in self.nexts(part, mask):
                    self.gather_copy(part, mask, b, c).wait_send()

    def piece(self, owner, c):
        span = self.span(c)
        return jnp.concatenate([self.full[owner, 0, span, :], self.full[owner, 1, span, :]], axis=1)

    def own_sum(self, c):
        return [self.summed(part, 0, c) for part in range(2)]

    def run(self, stages):
        depth = len(stages)

        def turn(t, _):
            for s in reversed(range(depth)):
                c = t - s

                @pl.when(jnp.logical_and(c >= 0, c < self.chunks))
                def _():
                    stages[s](c)

            return 0

        lax.fori_loop(0, self.chunks + depth - 1, turn, 0)


def mid_kernel(ex, branch, w_out, x_own, gain, normed, full_o, own_o, scale_o, *refs):
    ex.bind(refs)
    n, width = ex.n, ex.width
    greet(ex.neighbours())

    def first(c):
        rows = branch[ex.span(c), :]

        def block(mask):
            at = pl.multiple_of((ex.me ^ mask) * width, 128)
            return jnp.dot(rows, w_out[:, pl.ds(at, width)], preferred_element_type=F32)

        ex.produce(c, block)

    def own(c):
        span = ex.span(c)
        value = jnp.concatenate(ex.own_sum(c), axis=1) + x_own[span, :].astype(F32)
        own_o[span, :] = value
        ex.gather_start(c, [value[:, : ex.half], value[:, ex.half :]])
        ex.close_reduce(c)

    def final(c):
        ex.gather_close(c)
        span = ex.span(c)
        total = jnp.zeros((ex.size, 1), F32)
        for d in range(n):
            value = ex.piece(d, c).astype(F32)
            total = total + jnp.sum(value * value, axis=1, keepdims=True)
        scale = lax.rsqrt(total * (1.0 / (n * width)) + 1e-06)
        scale_o[span, :] = scale
        for d in range(n):
            columns = slice(d * width, (d + 1) * width)
            value = ex.piece(d, c)
            full_o[span, columns] = value
            normed[span, columns] = (value.astype(F32) * scale * gain[:, columns]).astype(BF16)

    stages = [first]
    stages += [functools.partial(ex.pass_on, s) for s in range(1, ex.bits)]
    stages += [own]
    stages += [functools.partial(ex.gather_pass, s) for s in range(1, ex.bits)]
    stages += [final]
    ex.run(stages)


def mid_exchange(branch, w_out, x_own, gain, ident, chunks=8):
    n = lax.axis_size("ch")
    rows, width = x_own.shape
    ex = Exchange(n, rows, width, chunks, True)
    full = jax.ShapeDtypeStruct((rows, n * width), BF16)
    return pl.pallas_call(
        functools.partial(mid_kernel, ex),
        out_shape=[
            full, full,
            jax.ShapeDtypeStruct((rows, width), F32),
            jax.ShapeDtypeStruct((rows, 1), F32),
        ],
        in_specs=whole_vmem(4),
        out_specs=whole_vmem(4),
        scratch_shapes=ex.scratch(),
        compiler_params=pltpu.CompilerParams(
            collective_id=ident, has_side_effects=True, vmem_limit_bytes=60 << 20
        ),
    )(branch, w_out, x_own, gain)


def back_kernel(
    ex, grad_gate, grad_up, w_gate, w_up, full, mid_own, cot, cot_own, scale, gain_own,
    block_o, own_o, gain_o, *refs,
):
    ex.bind(refs)
    n, width = ex.n, ex.width
    greet(ex.neighbours())
    gain_o[...] = jnp.zeros_like(gain_o)

    def first(c):
        span = ex.span(c)
        left, right = grad_gate[span, :], grad_up[span, :]

        def block(mask):
            at = pl.ds(pl.multiple_of((ex.me ^ mask) * width, 128), width)
            return nt_dot(left, w_gate[at, :]) + nt_dot(right, w_up[at, :])

        ex.produce(c, block)

    def own(c):
        span = ex.span(c)
        s = scale[span, :]
        grad = jnp.concatenate(ex.own_sum(c), axis=1)
        value = cot_own[span, :].astype(F32) + grad * gain_own[...] * s
        own_o[span, :] = value
        ex.gather_start(c, [value[:, : ex.half], value[:, ex.half :]])
        ex.close_reduce(c)
        product = grad * mid_own[span, :] * s
        gain_o[...] += jnp.sum(product.reshape(-1, 8, width), axis=0)

    def final(c):
        ex.gather_close(c)
        span = ex.span(c)
        s = scale[span, :]
        total = jnp.zeros((ex.size, 1), F32)
        for d in range(n):
            columns = slice(d * width, (d + 1) * width)
            delta = ex.piece(d, c).astype(F32) - cot[span, columns].astype(F32)
            total = total + jnp.sum(delta * full[span, columns].astype(F32), axis=1, keepdims=True)
        factor = s * s * total * (1.0 / (n * width))
        own_o[span, :] = own_o[span, :] - factor * mid_own[span, :]
        for d in range(n):
            columns = slice(d * width, (d + 1) * width)
            value = ex.piece(d, c).astype(F32) - factor * full[span, columns].astype(F32)
            block_o[span, columns] = value.astype(BF16)

    stages = [first]
    stages += [functools.partial(ex.pass_on, s) for s in range(1, ex.bits)]
    stages += [own]
    stages += [functools.partial(ex.gather_pass, s) for s in range(1, ex.bits)]
    stages += [final]
    ex.run(stages)


def back_exchange(
    grad_gate, grad_up, w_gate, w_up, full, mid_own, cot, cot_own, scale, gain_own, ident, chunks=8
):
    n = lax.axis_size("ch")
    rows, width = mid_own.shape
    ex = Exchange(n, rows, width, chunks, True)
    return pl.pallas_call(
        functools.partial(back_kernel, ex),
        out_shape=[
            jax.ShapeDtypeStruct((rows, n * width), BF16),
            jax.ShapeDtypeStruct((rows, width), F32),
            jax.ShapeDtypeStruct((8, width), F32),
        ],
        in_specs=whole_vmem(10),
        out_specs=whole_vmem(3),
        scratch_shapes=ex.scratch(),
        compiler_params=pltpu.CompilerParams(
            collective_id=ident, has_side_effects=True, vmem_limit_bytes=63 << 20
        ),
    )(grad_gate, grad_up, w_gate, w_up, full, mid_own, cot, cot_own, scale, gain_own)


def end_kernel(
    ex, g_rec, g_pre, w_branch, w_gelu, stat, small,
    own_o, stat_o, small_o, stats, smalls, st_s, st_r, sm_s, sm_r, *refs,
):
    ex.bind(refs)
    n, width = ex.n, ex.width
    count = lax.axis_size("tok")
    across = [(ex.tok, ex.me ^ m) for m in range(1, n)]
    greet(across + tok_targets())
    stats[ex.me] = stat[...]
    copies = []
    for m in range(1, n):
        copy = pltpu.make_async_remote_copy(
            stats.at[ex.me], stats.at[ex.me], st_s.at[m - 1], st_r.at[m - 1], across[m - 1], MESH
        )
        copy.start()
        copies.append(copy)
    smalls[ex.tok] = small[...]
    for o, target in enumerate(tok_targets()):
        copy = pltpu.make_async_remote_copy(
            smalls.at[ex.tok], smalls.at[ex.tok], sm_s.at[o], sm_r.at[o], target, MESH
        )
        copy.start()
        copies.append(copy)

    def first(c):
        span = ex.span(c)
        left, right = g_rec[span, :], g_pre[span, :]

        def block(mask):
            at = pl.ds(pl.multiple_of((ex.me ^ mask) * width, 128), width)
            return nt_dot(left, w_branch[at, :]) + nt_dot(right, w_gelu[at, :])

        ex.produce(c, block)

    def own(c):
        own_o[ex.span(c), :] = jnp.concatenate(ex.own_sum(c), axis=1)
        ex.close_reduce(c)

    stages = [first]
    stages += [functools.partial(ex.pass_on, s) for s in range(1, ex.bits)]
    stages += [own]
    ex.run(stages)
    for m in range(1, n):
        block = stats.at[ex.me ^ m]
        pltpu.make_async_remote_copy(
            block, block, st_s.at[m - 1], st_r.at[m - 1], across[m - 1], MESH
        ).wait_recv()
    for o in range(count - 1):
        source = lax.rem(ex.tok + count - 1 - o, count)
        block = smalls.at[source]
        pltpu.make_async_remote_copy(
            block, block, sm_s.at[o], sm_r.at[o], tok_targets()[o], MESH
        ).wait_recv()
    stat_o[...] = jnp.sum(stats[...], axis=0)
    small_o[...] = jnp.sum(smalls[...], axis=0)
    for copy in copies:
        copy.wait_send()


def end_exchange(g_rec, g_pre, w_branch, w_gelu, stat, small, width, ident, chunks=8):
    n, count = lax.axis_size("ch"), lax.axis_size("tok")
    rows = g_rec.shape[0]
    ex = Exchange(n, rows, width, chunks, False)
    return pl.pallas_call(
        functools.partial(end_kernel, ex),
        out_shape=[
            jax.ShapeDtypeStruct((rows, width), F32),
            jax.ShapeDtypeStruct(stat.shape, F32),
            jax.ShapeDtypeStruct(small.shape, F32),
        ],
        in_specs=whole_vmem(6),
        out_specs=whole_vmem(3),
        scratch_shapes=[
            pltpu.VMEM((n, *stat.shape), F32),
            pltpu.VMEM((count, *small.shape), F32),
            pltpu.SemaphoreType.DMA((n - 1,)),
            pltpu.SemaphoreType.DMA((n - 1,)),
            pltpu.SemaphoreType.DMA((count - 1,)),
            pltpu.SemaphoreType.DMA((count - 1,)),
        ]
        + ex.scratch(),
        compiler_params=pltpu.CompilerParams(
            collective_id=ident, has_side_effects=True, vmem_limit_bytes=60 << 20
        ),
    )(g_rec, g_pre, w_branch, w_gelu, stat, small)


def dense_blocks(blocks):
    count, size = blocks.shape[0], blocks.shape[1]
    rows = [
        jnp.pad(blocks[i], ((0, 0), (i * size, (count - 1 - i) * size))) for i in range(count)
    ]
    return jnp.concatenate(rows, axis=0)


def diagonal_blocks(full, count, size):
    return jnp.stack(
        [full[i * size : (i + 1) * size, i * size : (i + 1) * size] for i in range(count)]
    )


def tok_scatter(full, dim):
    summed = lax.psum_scatter(full.astype(BF16), "tok", scatter_dimension=dim, tiled=True)
    return summed.astype(F32)


def local(
    layer_in,
    positions,
    norm_gain,
    w_branch,
    w_gelu,
    conv_w,
    conv_b,
    w_rgate,
    b_rgate,
    w_igate,
    b_igate,
    decay_param,
    w_out,
    mlp_gain,
    w_gate,
    w_up,
    w_down,
    cotangent,
):
    rows, width = layer_in.shape
    ch_index = lax.axis_index("ch")
    column = ch_index * width
    chans = decay_param.shape[0]
    gates, gate_width = w_rgate.shape[0], w_rgate.shape[1]
    pos = positions[:, None]
    pos_tall = jnp.pad(positions, (0, 8))[:, None]
    sp = jax.nn.softplus(-decay_param)[None]
    sg = jax.nn.sigmoid(-decay_param)[None]
    dense_r, dense_i = dense_blocks(w_rgate), dense_blocks(w_igate)

    full_in = gather_columns(layer_in, 0)
    total = full_in.shape[1]
    tied_cot, full_in = lax.optimization_barrier((cotangent, full_in))
    cot = lax.all_gather(tied_cot, "ch", axis=1, tiled=True)
    full_f = full_in.astype(F32)
    scale_in = lax.rsqrt(jnp.mean(full_f * full_f, axis=1, keepdims=True) + 1e-06)
    normed = (full_f * scale_in * norm_gain).astype(BF16)
    rec_in = jnp.dot(normed, w_branch, preferred_element_type=F32)
    gate_pre = jnp.dot(normed, w_gelu, preferred_element_type=F32)
    ext, conv, rate, igate, lru, branch = recur_fwd(
        rec_in, gate_pre, pos, conv_w, conv_b[None], dense_r, b_rgate[None], dense_i,
        b_igate[None], sp, 1,
    )
    normed_mid, mid_full, mid_own, scale_mid = mid_exchange(
        branch, w_out, layer_in, mlp_gain[None], 2
    )
    gate_val = jnp.dot(normed_mid, w_gate, preferred_element_type=F32)
    up_val = jnp.dot(normed_mid, w_up, preferred_element_type=F32)
    act, slope = gelu_parts(gate_val)
    hidden = (act * up_val).astype(BF16)
    down = jnp.dot(hidden, w_down, preferred_element_type=F32).astype(BF16)
    mlp_out = lax.psum_scatter(down, "ch", scatter_dimension=1, tiled=True)
    layer_out = (mid_own + mlp_out.astype(F32)).astype(BF16)
    grad_hidden = nt_dot(cot, w_down)
    grad_gate = (grad_hidden * up_val * slope).astype(BF16)
    grad_up = (grad_hidden * act).astype(BF16)
    grad_wdown = tok_scatter(tn_dot(hidden, cot), 1)
    gain_mid_own = lax.dynamic_slice_in_dim(mlp_gain, column, width, 0)[None]
    grad_block, grad_mid_own, gain_sum = back_exchange(
        grad_gate, grad_up, w_gate, w_up, mid_full, mid_own, cot, cotangent, scale_mid,
        gain_mid_own, 3,
    )
    grad_wgate = tok_scatter(tn_dot(normed_mid, grad_gate), 0)
    grad_wup = tok_scatter(tn_dot(normed_mid, grad_up), 0)
    grad_branch = nt_dot(grad_block, w_out)
    grad_wout = tok_scatter(tn_dot(branch, grad_block), 1)
    grad_rec, grad_gate_pre, grad_rate, grad_input, sums, row_term = recur_bwd(
        grad_branch, gate_pre, ext, conv, rate, igate, lru, pos_tall, conv_w, dense_r, dense_i,
        sp, sg, 4,
    )
    conv_low = conv.astype(BF16)
    grad_wr = diagonal_blocks(tn_dot(conv_low, grad_rate), gates, gate_width)
    grad_wi = diagonal_blocks(tn_dot(conv_low, grad_input), gates, gate_width)
    stat = row_term.reshape(8, rows // 8)
    small_width = max(chans, width)
    small = jnp.concatenate(
        [
            jnp.pad(sums, ((0, 0), (0, small_width - chans))),
            jnp.pad(
                jnp.sum(gain_sum, axis=0, keepdims=True), ((0, 7), (0, small_width - width))
            ),
        ],
        axis=0,
    )
    own_normed, stat_sum, small_sum = end_exchange(
        grad_rec, grad_gate_pre, w_branch, w_gelu, stat, small, width, 5
    )
    grad_wbranch = tok_scatter(tn_dot(normed, grad_rec), 0)
    grad_wgelu = tok_scatter(tn_dot(normed, grad_gate_pre), 0)
    grad_wr = tok_scatter(grad_wr, 1)
    grad_wi = tok_scatter(grad_wi, 1)
    own_in = layer_in.astype(F32)
    own_gain = lax.dynamic_slice_in_dim(norm_gain, column, width, 0)
    row_stat = stat_sum.reshape(rows, 1)
    input_grad = (
        grad_mid_own
        + scale_in * own_gain * own_normed
        - scale_in * scale_in * own_in * (row_stat / total)
    )
    own_norm_gain = lax.psum(jnp.sum(own_normed * own_in * scale_in, axis=0), "tok")
    return (
        layer_out,
        input_grad,
        own_norm_gain,
        grad_wbranch,
        grad_wgelu,
        small_sum[4:8, :chans],
        small_sum[3, :chans],
        grad_wr,
        small_sum[1, :chans],
        grad_wi,
        small_sum[2, :chans],
        small_sum[0, :chans],
        grad_wout,
        small_sum[8, :width],
        grad_wgate,
        grad_wup,
        grad_wdown,
    )


def solution(mesh):
    placed = (
        P("tok", "ch"),
        P("tok"),
        P(),
        P(None, "ch"),
        P(None, "ch"),
        P(None, "ch"),
        P("ch"),
        P("ch", None, None),
        P("ch"),
        P("ch", None, None),
        P("ch"),
        P("ch"),
        P("ch", None),
        P(),
        P(None, "ch"),
        P(None, "ch"),
        P("ch", None),
        P("tok", "ch"),
    )
    return jax.shard_map(
        local,
        mesh=mesh,
        in_specs=placed,
        out_specs=(
            P("tok", "ch"),
            P("tok", "ch"),
            P("ch"),
            P("tok", "ch"),
            P("tok", "ch"),
            P(None, "ch"),
            P("ch"),
            P("ch", "tok", None),
            P("ch"),
            P("ch", "tok", None),
            P("ch"),
            P("ch"),
            P("ch", "tok"),
            P("ch"),
            P("tok", "ch"),
            P("tok", "ch"),
            P("ch", "tok"),
        ),
        check_vma=False,
    )
```

```python
import functools

import jax
import jax.numpy as jnp
from jax import lax
from jax.experimental import pallas as pl
from jax.experimental.pallas import tpu as pltpu
from jax.sharding import PartitionSpec as P

MESH = pl.DeviceIdType.MESH
F32 = jnp.float32
BF16 = jnp.bfloat16
SEGS = 8
GELU_A = 0.7978845608028654
GELU_B = 0.044715


def low_bit(mask):
    return (mask & -mask).bit_length() - 1


def high_bit(mask):
    return mask.bit_length() - 1


def gelu_parts(x):
    inner = jnp.tanh(GELU_A * (x + GELU_B * x * x * x))
    act = 0.5 * x * (1.0 + inner)
    slope = 0.5 * (1.0 + inner) + 0.5 * x * (1.0 - inner * inner) * GELU_A * (
        1.0 + 3.0 * GELU_B * x * x
    )
    return act, slope


def gelu_value(x):
    return 0.5 * x * (1.0 + jnp.tanh(GELU_A * (x + GELU_B * x * x * x)))


def minus_expm1(y, exp_y):
    series = 1.0 + y * (1.0 / 7.0)
    for k in (6, 5, 4, 3, 2):
        series = 1.0 + y * (1.0 / k) * series
    return jnp.where(y > -0.35, -y * series, 1.0 - exp_y)


def nt_dot(a, b):
    return lax.dot_general(a, b, (((1,), (1,)), ((), ())), preferred_element_type=F32)


def tn_dot(a, b):
    return lax.dot_general(a, b, (((0,), (0,)), ((), ())), preferred_element_type=F32)


def whole_vmem(count):
    return [pl.BlockSpec(memory_space=pltpu.VMEM)] * count


def greet(targets):
    barrier = pltpu.get_barrier_semaphore()
    for target in targets:
        pl.semaphore_signal(barrier, inc=1, device_id=target, device_id_type=MESH)
    pl.semaphore_wait(barrier, len(targets))


class Routes:
    def __init__(self, n, rows, width):
        self.n, self.rows, self.width = n, rows, width
        self.bits = n.bit_length() - 1
        self.half = width // 2
        self.keeps = [(part, m) for part in range(2) for m in range(n) if self.incoming(part, m)]

    def peer(self, b):
        return (self.tok, self.me ^ (1 << b))

    def neighbours(self):
        return [self.peer(b) for b in range(self.bits)]

    def bit_of(self, part, mask):
        return low_bit(mask) if part == 0 else high_bit(mask)

    def incoming(self, part, mask):
        if mask == 0:
            return list(range(self.bits)) if part == 0 else list(reversed(range(self.bits)))
        if part == 0:
            return list(range(low_bit(mask)))
        return list(reversed(range(high_bit(mask) + 1, self.bits)))

    def stage_of(self, part, mask):
        return low_bit(mask) if part == 0 else self.bits - 1 - high_bit(mask)


class Spread(Routes):
    def scratch(self):
        shape = (2, self.n, self.rows, self.half)
        keeps = (len(self.keeps), self.rows, self.half)
        return [
            pltpu.VMEM(shape, BF16),
            pltpu.VMEM(keeps, BF16),
            pltpu.SemaphoreType.DMA((2, self.n)),
            pltpu.SemaphoreType.DMA((2, self.n)),
            pltpu.SemaphoreType.DMA((len(self.keeps),)),
        ]

    def bind(self, refs, source):
        self.into, self.own, self.ss, self.rs, self.ls = refs
        self.source = source
        self.tok, self.me = lax.axis_index("tok"), lax.axis_index("ch")

    def view(self, part, mask):
        at = (self.me ^ mask) * self.width + part * self.half
        return self.source.at[:, pl.ds(pl.multiple_of(at, 128), self.half)]

    def copy(self, part, mask):
        held = (part, mask) in self.keeps
        block = self.own.at[self.keeps.index((part, mask))] if held else self.view(part, mask)
        return pltpu.make_async_remote_copy(
            block,
            self.into.at[part, mask],
            self.ss.at[part, mask],
            self.rs.at[part, mask],
            self.peer(self.bit_of(part, mask)),
            MESH,
        )

    def fetch(self, at):
        return pltpu.make_async_copy(self.view(*self.keeps[at]), self.own.at[at], self.ls.at[at])

    def launch(self):
        for part in range(2):
            for mask in range(1, self.n):
                if (part, mask) not in self.keeps:
                    self.copy(part, mask).start()
        for at in range(len(self.keeps)):
            self.fetch(at).start()

    def gather_in(self, part, mask, write):
        at = self.keeps.index((part, mask))
        self.fetch(at).wait()
        came = [mask | (1 << b) for b in self.incoming(part, mask)]
        for m in came:
            self.copy(part, m).wait_recv()

        def add(i, _):
            span = pl.ds(i * 32, 32)
            value = self.own[at, span, :].astype(F32)
            for m in came:
                value = value + self.into[part, m, span, :].astype(F32)
            write(at, span, value)
            return 0

        lax.fori_loop(0, self.rows // 32, add, 0, unroll=2)

    def relay(self, stage):
        def write(at, span, value):
            self.own[at, span, :] = value.astype(BF16)

        for part in range(2):
            for mask in range(1, self.n):
                if self.stage_of(part, mask) == stage:
                    self.gather_in(part, mask, write)
                    self.copy(part, mask).start()

    def settle(self, result):
        for part in range(2):

            def write(at, span, value, part=part):
                result[span, part * self.half : (part + 1) * self.half] = value

            self.gather_in(part, 0, write)
        for part in range(2):
            for mask in range(1, self.n):
                self.copy(part, mask).wait_send()


def tok_targets():
    count = lax.axis_size("tok")
    tok, ch = lax.axis_index("tok"), lax.axis_index("ch")
    return [(lax.rem(tok + o, count), ch) for o in range(1, count)]


def share_rows(buffer, send, recv):
    tok = lax.axis_index("tok")
    copies = []
    for o, target in enumerate(tok_targets()):
        copy = pltpu.make_async_remote_copy(
            buffer.at[tok], buffer.at[tok], send.at[o], recv.at[o], target, MESH
        )
        copy.start()
        copies.append(copy)
    count = lax.axis_size("tok")
    for o in range(count - 1):
        source = lax.rem(tok + count - 1 - o, count)
        pltpu.make_async_remote_copy(
            buffer.at[source], buffer.at[source], send.at[o], recv.at[o], tok_targets()[o], MESH
        ).wait_recv()
    return copies


class Gather(Routes):
    def __init__(self, n, rows, width, chunks):
        super().__init__(n, rows, width)
        self.chunks, self.size = chunks, rows // chunks

    def scratch(self):
        sem = pltpu.SemaphoreType.DMA
        near, far = (self.bits, self.chunks), (2, self.n, self.chunks)
        return [sem(near), sem(near), sem(far), sem(far), sem]

    def bind(self, refs, x, full):
        self.gs, self.gr, self.fs, self.fr, self.here = refs
        self.x, self.full = x, full
        self.tok, self.me = lax.axis_index("tok"), lax.axis_index("ch")

    def place(self, owner, part, c):
        span = pl.ds(c * self.size, self.size)
        if part is None:
            return self.full.at[span, pl.ds(pl.multiple_of(owner * self.width, 128), self.width)]
        at = owner * self.width + part * self.half
        return self.full.at[span, pl.ds(pl.multiple_of(at, 128), self.half)]

    def near_copy(self, b, c, owner):
        return pltpu.make_async_remote_copy(
            self.x.at[pl.ds(c * self.size, self.size)],
            self.place(owner, None, c),
            self.gs.at[b, c],
            self.gr.at[b, c],
            self.peer(b),
            MESH,
        )

    def far_copy(self, part, mask, b, c):
        block, got = self.place(self.me ^ mask, part, c), mask | (1 << b)
        return pltpu.make_async_remote_copy(
            block, block, self.fs.at[part, got, c], self.fr.at[part, got, c], self.peer(b), MESH
        )

    def own_copy(self):
        at = pl.ds(pl.multiple_of(self.me * self.width, 128), self.width)
        return pltpu.make_async_copy(self.x, self.full.at[:, at], self.here)

    def launch(self, order):
        for c in order:
            for b in range(self.bits):
                self.near_copy(b, c, self.me).start()
        self.own_copy().start()

    def nexts(self, part, mask):
        return range(high_bit(mask) + 1, self.bits) if part == 0 else range(low_bit(mask))

    def far_arrived(self, part, mask, c):
        block = self.place(self.me ^ mask, part, c)
        pltpu.make_async_remote_copy(
            block, block, self.fs.at[part, mask, c], self.fr.at[part, mask, c], self.peer(0), MESH
        ).wait_recv()

    def forward(self, c):
        for count in range(1, self.bits):
            for mask in [m for m in range(1, self.n) if m.bit_count() == count]:
                if count == 1:
                    self.near_copy(low_bit(mask), c, self.me ^ mask).wait_recv()
                for part in range(2):
                    if count > 1:
                        self.far_arrived(part, mask, c)
                    for b in self.nexts(part, mask):
                        self.far_copy(part, mask, b, c).start()

    def finish(self, c):
        for part in range(2):
            self.far_arrived(part, self.n - 1, c)

    def close(self):
        for c in range(self.chunks):
            for b in range(self.bits):
                self.near_copy(b, c, self.me).wait_send()
            for mask in range(1, self.n):
                for part in range(2):
                    for b in self.nexts(part, mask):
                        self.far_copy(part, mask, b, c).wait_send()


def over_rows(start, rows, step, body, unroll=1):
    def one(i, _):
        body(pl.multiple_of(start + i * step, 8))
        return 0

    lax.fori_loop(0, rows // step, one, 0, unroll=unroll)


def eight(value):
    return value.reshape(-1, SEGS, value.shape[-1])


def with_segments(value, seg):
    return (eight(value) * seg[None]).reshape(value.shape)


def front_kernel(
    ga, late, x, gain, pos, wb_h, wg_h, cw, cb, wr_h, br, wi_h, bi, sp, cot,
    normed_h, scale, gpre_h, ext_h, conv_h, rate_h, igate_h, lru, branch, cot_full,
    full, normed, wb, wg, wr, wi, gpre, ext, conv, rate, igate, low, a_s, h_s, carry, halo, ends,
    wsem, osem, halo_send, halo_recv, send, recv, *refs,
):
    held = len(ga.scratch())
    ga.bind(refs[:held], x, full)
    late.bind(refs[held:], cot, cot_full)
    rows, chans = gpre.shape
    taps = cw.shape[0]
    pad = 8 * (taps - 1)
    tok, ch = lax.axis_index("tok"), lax.axis_index("ch")
    count = lax.axis_size("tok")
    total_width = full.shape[1]
    greet(tok_targets() + ga.neighbours())
    order = [ga.chunks - 1] + list(range(ga.chunks - 1))
    ga.launch(order)
    loads = [
        pltpu.make_async_copy(a, b, wsem.at[i])
        for i, (a, b) in enumerate(((wb_h, wb), (wg_h, wg), (wr_h, wr), (wi_h, wi)))
    ]
    for load in loads:
        load.start()
    step = 16
    size = ga.size
    stores = []

    def store(source, target):
        copy = pltpu.make_async_copy(source, target, osem.at[len(stores)])
        copy.start()
        stores.append(copy)

    halo_copy = pltpu.make_async_remote_copy(
        ext.at[pl.ds(rows, pad)], halo, halo_send, halo_recv,
        (lax.rem(tok + 1, count), ch), MESH,
    )

    def norm_rows(at):
        span = pl.ds(at, step)
        value = full[span, :].astype(F32)
        s = lax.rsqrt(
            jnp.sum(value * value, axis=1, keepdims=True) * (1.0 / total_width) + 1e-06
        )
        scale[span, :] = s
        normed[span, :] = (value * s * gain[...]).astype(BF16)

    def enter(c):
        over_rows(c * size, size, step, norm_rows)
        span = pl.ds(c * size, size)
        ext[pl.ds(pad + c * size, size), :] = jnp.dot(
            normed[span, :], wb[...], preferred_element_type=F32
        )
        gpre[span, :] = jnp.dot(normed[span, :], wg[...], preferred_element_type=F32)

    def conv_rows(at):
        span = pl.ds(at, step)
        window = ext[pl.ds(at, step + pad), :]
        where = pos[span, :]
        value = cb[...] + cw[0:1, :] * window[pad : pad + step]
        for k in range(1, taps):
            shifted = window[pad - 8 * k : pad - 8 * k + step]
            value = value + jnp.where(where >= k, cw[k : k + 1, :] * shifted, 0.0)
        conv[span, :] = value
        low[span, :] = value.astype(BF16)

    def gate_rows(at):
        span = pl.ds(at, step)
        where = pos[span, :]
        r = jax.nn.sigmoid(rate[span, :])
        g = jax.nn.sigmoid(igate[span, :])
        rate[span, :] = r
        igate[span, :] = g
        log_decay = -8.0 * r * sp[...]
        decay = jnp.exp(log_decay)
        mult = jnp.sqrt(minus_expm1(2.0 * log_decay, decay * decay))
        mult = jnp.where(where > 0, mult, 1.0)
        a_s[span, :] = jnp.where(where > 0, decay, 0.0)
        h_s[span, :] = g * conv[span, :] * mult

    def scan_rows(c):
        def one(t, state):
            h, p = state
            span = pl.ds(pl.multiple_of(c * size + t * SEGS, SEGS), SEGS)
            a = a_s[span, :]
            h = a * h + h_s[span, :]
            p = a * p
            h_s[span, :] = h
            a_s[span, :] = p
            return h, p

        h, p = lax.fori_loop(0, size // SEGS, one, (carry[0], carry[1]), unroll=4)
        carry[0] = h
        carry[1] = p

    def recur(c):
        over_rows(c * size, size, step, conv_rows, 2)
        span = pl.ds(c * size, size)
        rate[span, :] = jnp.dot(low[span, :], wr[...], preferred_element_type=F32) + br[...]
        igate[span, :] = jnp.dot(low[span, :], wi[...], preferred_element_type=F32) + bi[...]
        over_rows(c * size, size, step, gate_rows, 2)
        scan_rows(c)

    carry[0] = jnp.zeros((SEGS, chans), F32)
    carry[1] = jnp.ones((SEGS, chans), F32)
    for i, c in enumerate(order):
        if i == 0:
            ga.forward(c)
        if i + 1 < len(order):
            ga.forward(order[i + 1])
        if i + 2 == len(order):
            late.launch(range(late.chunks))
        ga.finish(c)
        if i == 0:
            ga.own_copy().wait()
            for load in loads:
                load.wait()
        enter(c)
        if i == 0:
            halo_copy.start()
        if i == 1:
            halo_copy.wait()
            last_row = lax.broadcasted_iota(jnp.int32, (SEGS, chans), 0) == SEGS - 1
            for j in range(taps - 1):
                here = ext[pl.ds(rows + 8 * j, 8), :]
                joined = jnp.where(last_row, halo[8 * j : 8 * j + 8, :], here)
                ext[8 * j : 8 * j + 8, :] = pltpu.roll(joined, 1, 0)
        if i + 1 == len(order):
            late.forward(0)
        if i >= 1:
            recur(c)
    late.forward(1)
    store(normed, normed_h)
    store(gpre, gpre_h)
    store(ext, ext_h)
    recur(ga.chunks - 1)
    late.forward(2)
    store(conv, conv_h)
    store(rate, rate_h)
    store(igate, igate_h)
    h_end, p_end = carry[0], carry[1]
    total_h, total_p = jnp.zeros((1, chans), F32), jnp.ones((1, chans), F32)
    for s in range(SEGS):
        total_h = p_end[s : s + 1] * total_h + h_end[s : s + 1]
        total_p = p_end[s : s + 1] * total_p
    ends[tok, 0:1, :] = total_h
    ends[tok, 1:2, :] = total_p
    sends = share_rows(ends, send, recv)
    state = jnp.zeros((1, chans), F32)
    for source in range(count - 1):
        after = ends[source, 1:2, :] * state + ends[source, 0:1, :]
        state = jnp.where(source < tok, after, state)
    for s in range(SEGS):
        lru[s : s + 1, :] = state
        state = p_end[s : s + 1] * state + h_end[s : s + 1]
    seg = lru[0:8, :]
    late.forward(3)

    def finish_rows(at):
        span = pl.ds(at, step)
        value = h_s[span, :] + with_segments(a_s[span, :], seg)
        lru[pl.ds(8 + at, step), :] = value
        branch[span, :] = (value * gelu_value(gpre[span, :])).astype(BF16)

    over_rows(0, rows, step, finish_rows, 2)
    for copy in sends:
        copy.wait_send()
    ga.close()
    for c in range(late.chunks):
        late.finish(c)
    late.close()
    late.own_copy().wait()
    for copy in stores:
        copy.wait()


def front(x, gain, pos, w_branch, w_gelu, cw, cb, wr, br, wi, bi, sp, cot, ident, chunks=4):
    n, count = lax.axis_size("ch"), lax.axis_size("tok")
    rows, width = x.shape
    total, chans = w_branch.shape
    taps = cw.shape[0]
    pad = 8 * (taps - 1)
    ga, late = Gather(n, rows, width, chunks), Gather(n, rows, width, 4)
    sem = pltpu.SemaphoreType.DMA
    grid = (rows, chans)
    anywhere = pl.BlockSpec(memory_space=pl.ANY)
    vmem = pl.BlockSpec(memory_space=pltpu.VMEM)
    return pl.pallas_call(
        functools.partial(front_kernel, ga, late),
        out_shape=[
            jax.ShapeDtypeStruct((rows, total), BF16),
            jax.ShapeDtypeStruct((rows, 1), F32),
            jax.ShapeDtypeStruct(grid, F32),
            jax.ShapeDtypeStruct((rows + pad, chans), F32),
            jax.ShapeDtypeStruct(grid, F32),
            jax.ShapeDtypeStruct(grid, F32),
            jax.ShapeDtypeStruct(grid, F32),
            jax.ShapeDtypeStruct((rows + 8, chans), F32),
            jax.ShapeDtypeStruct(grid, BF16),
            jax.ShapeDtypeStruct((rows, total), BF16),
        ],
        in_specs=[
            anywhere, vmem, vmem, anywhere, anywhere, vmem, vmem, anywhere, vmem, anywhere, vmem,
            vmem, anywhere,
        ],
        out_specs=[
            anywhere, vmem, anywhere, anywhere, anywhere, anywhere, anywhere, vmem, vmem,
            anywhere,
        ],
        scratch_shapes=[
            pltpu.VMEM((rows, total), BF16),
            pltpu.VMEM((rows, total), BF16),
            pltpu.VMEM(w_branch.shape, BF16),
            pltpu.VMEM(w_gelu.shape, BF16),
            pltpu.VMEM(wr.shape, BF16),
            pltpu.VMEM(wi.shape, BF16),
            pltpu.VMEM(grid, F32),
            pltpu.VMEM((rows + pad, chans), F32),
            pltpu.VMEM(grid, F32),
            pltpu.VMEM(grid, F32),
            pltpu.VMEM(grid, F32),
            pltpu.VMEM(grid, BF16),
            pltpu.VMEM(grid, F32),
            pltpu.VMEM(grid, F32),
            pltpu.VMEM((2, SEGS, chans), F32),
            pltpu.VMEM((pad, chans), F32),
            pltpu.VMEM((count, 8, chans), F32),
            sem((4,)), sem((6,)), sem, sem, sem((count - 1,)), sem((count - 1,)),
        ]
        + ga.scratch()
        + late.scratch(),
        compiler_params=pltpu.CompilerParams(
            collective_id=ident, has_side_effects=True, vmem_limit_bytes=60 << 20
        ),
    )(x, gain, pos, w_branch, w_gelu, cw, cb, wr, br, wi, bi, sp, cot)


def recur_bwd_kernel(
    ex, g_block_h, w_out_h, gpre_h, ext_h, conv_h, rate_h, igate_h, lru_h, pos, cw, wr_h, wi_h, sp,
    sg, down,
    grec, ggp, grate, ginput, sums, row_term, down_sum,
    g_block, w_out, gpre, ext, conv, rate, igate, lru, wr, wi,
    g_s, a_s, gc, ends, edge, landed, acc, lsem, edge_send, edge_recv, send, recv, *refs,
):
    ex.bind(refs, down)
    rows, chans = conv.shape
    taps = cw.shape[0]
    pad = 8 * (taps - 1)
    tok, ch = lax.axis_index("tok"), lax.axis_index("ch")
    count = lax.axis_size("tok")
    pairs = (
        (g_block_h, g_block), (w_out_h, w_out), (gpre_h, gpre), (lru_h, lru), (rate_h, rate),
        (igate_h, igate), (conv_h, conv), (wr_h, wr), (wi_h, wi), (ext_h, ext),
    )
    loads = [pltpu.make_async_copy(a, b, lsem.at[i]) for i, (a, b) in enumerate(pairs)]
    for load in loads:
        load.start()
    greet(tok_targets() + ex.neighbours())
    ex.launch()
    step = 16
    big = min(256, rows)
    for load in loads[:5]:
        load.wait()

    def begin_rows(at):
        span = pl.ds(at, step)
        act, slope = gelu_parts(gpre[span, :])
        grad = g_s[span, :]
        g_s[span, :] = grad * act
        ggp[span, :] = (grad * lru[pl.ds(8 + at, step), :] * slope).astype(BF16)
        a_s[span, :] = jnp.where(pos[span, :] > 0, jnp.exp(-8.0 * rate[span, :] * sp[...]), 0.0)

    def begin(i, state):
        at = pl.multiple_of(rows - (i + 1) * big, 8)
        g_s[pl.ds(at, big), :] = nt_dot(g_block[pl.ds(at, big), :], w_out[...])
        over_rows(at, big, step, begin_rows, 2)

        def one(t, state):
            v, q = state
            span = pl.ds(pl.multiple_of(at + big - (t + 1) * SEGS, SEGS), SEGS)
            a = a_s[span, :]
            c = g_s[span, :] + v
            g_s[span, :] = c
            a_s[span, :] = q
            return a * c, a * q

        return lax.fori_loop(0, big // SEGS, one, state, unroll=4)

    v_end, q_end = lax.fori_loop(
        0, rows // big, begin, (jnp.zeros((SEGS, chans), F32), jnp.ones((SEGS, chans), F32))
    )
    total_v, total_q = jnp.zeros((1, chans), F32), jnp.ones((1, chans), F32)
    for s in reversed(range(SEGS)):
        total_v = q_end[s : s + 1] * total_v + v_end[s : s + 1]
        total_q = q_end[s : s + 1] * total_q
    ends[tok, 0:1, :] = total_v
    ends[tok, 1:2, :] = total_q
    sends = share_rows(ends, send, recv)
    state = jnp.zeros((1, chans), F32)
    for source in reversed(range(1, count)):
        after = ends[source, 1:2, :] * state + ends[source, 0:1, :]
        state = jnp.where(source > tok, after, state)
    entering = [None] * SEGS
    for s in reversed(range(SEGS)):
        entering[s] = state
        state = q_end[s : s + 1] * state + v_end[s : s + 1]
    for s in range(SEGS):
        edge[s : s + 1, :] = entering[s]
    seg = edge[0:8, :]
    acc[...] = jnp.zeros_like(acc)
    for load in loads[5:]:
        load.wait()

    def folded(x):
        return jnp.sum(eight(x), axis=0)

    def middle_rows(at):
        span = pl.ds(at, step)
        carried = g_s[span, :] + with_segments(a_s[span, :], seg)
        before = lru[span, :]
        keep = pos[span, :] > 0
        r, g, out = rate[span, :], igate[span, :], conv[span, :]
        log_decay = -8.0 * r * sp[...]
        decay = jnp.exp(log_decay)
        square = decay * decay
        mult = jnp.where(keep, jnp.sqrt(minus_expm1(2.0 * log_decay, square)), 1.0)
        scaled = carried * g
        grad_log = jnp.where(keep, decay * carried * before - scaled * out * square / mult, 0.0)
        slope = 8.0 * r * grad_log
        grad_rate = (-slope * sp[...] * (1.0 - r)).astype(BF16)
        grad_input = (scaled * out * mult * (1.0 - g)).astype(BF16)
        grate[span, :] = grad_rate
        ginput[span, :] = grad_input
        gc[span, :] = scaled * mult
        acc[0] += folded(slope * sg[...])
        acc[1] += folded(grad_rate.astype(F32))
        acc[2] += folded(grad_input.astype(F32))

    def middle(i, _):
        at = pl.multiple_of(i * big, 8)
        over_rows(at, big, step, middle_rows)
        span = pl.ds(at, big)
        gc[span, :] += nt_dot(grate[span, :], wr[...]) + nt_dot(ginput[span, :], wi[...])
        return 0

    lax.fori_loop(0, rows // big, middle, 0)
    gc[pl.ds(rows, pad), :] = jnp.zeros((pad, chans), F32)
    for j in range(1, taps):
        value = jnp.zeros((8, chans), F32)
        for k in range(j, taps):
            e = 8 * (k - j)
            masked = jnp.where(pos[e : e + 8, :] >= k, gc[e : e + 8, :], 0.0)
            value = value + cw[k : k + 1, :] * masked
        edge[pad - 8 * j : pad - 8 * j + 8, :] = value
    edge_copy = pltpu.make_async_remote_copy(
        edge, landed, edge_send, edge_recv, (lax.rem(tok + count - 1, count), ch), MESH
    )
    edge_copy.start()
    for stage in range(1, ex.bits):
        ex.relay(stage)

    def last_rows(at):
        span = pl.ds(at, step)
        window = gc[pl.ds(at, step + pad), :]
        where = pos[pl.ds(at, step + pad), :]
        source = ext[pl.ds(at, step + pad), :]
        here = window[:step]
        total = cw[0:1, :] * here
        acc[3] += folded(here)
        acc[4] += folded(here * source[pad : pad + step])
        for k in range(1, taps):
            masked = jnp.where(where >= k, window, 0.0)
            total = total + cw[k : k + 1, :] * masked[8 * k : 8 * k + step]
            acc[4 + k] += folded(masked[:step] * source[pad - 8 * k : pad - 8 * k + step])
        gc[span, :] = total
        grec[span, :] = total.astype(BF16)
        both = total.astype(BF16).astype(F32) * source[pad : pad + step]
        both = both + ggp[span, :].astype(F32) * gpre[span, :]
        row_term[span, :] = jnp.sum(both, axis=1, keepdims=True)

    over_rows(0, rows, step, last_rows)
    edge_copy.wait()
    first_row = lax.broadcasted_iota(jnp.int32, (SEGS, chans), 0) == 0
    for j in range(0, pad, 8):
        joined = jnp.where(first_row, landed[j : j + 8, :], edge[j : j + 8, :])
        at = pl.ds(rows - pad + j, 8)
        gc[at, :] = gc[at, :] + pltpu.roll(joined, SEGS - 1, 0)
    tail = -(-pad // 16) * 16
    span = pl.ds(rows - tail, tail)
    total = gc[span, :].astype(BF16)
    grec[span, :] = total
    both = total.astype(F32) * ext[pl.ds(pad + rows - tail, tail), :]
    both = both + ggp[span, :].astype(F32) * gpre[span, :]
    row_term[span, :] = jnp.sum(both, axis=1, keepdims=True)
    for k in range(8):
        sums[k : k + 1, :] = jnp.sum(acc[k], axis=0, keepdims=True)
    ex.settle(down_sum)
    for copy in sends:
        copy.wait_send()


def recur_bwd(
    g_block, w_out, gpre, ext, conv, rate, igate, lru, pos, cw, wr, wi, sp, sg, down, ident
):
    rows, chans = conv.shape
    n, count = lax.axis_size("ch"), lax.axis_size("tok")
    width = down.shape[1] // n
    pad = 8 * (cw.shape[0] - 1)
    ex = Spread(n, rows, width)
    half = jax.ShapeDtypeStruct((rows, chans), BF16)
    sem = pltpu.SemaphoreType.DMA
    anywhere = pl.BlockSpec(memory_space=pl.ANY)
    vmem = pl.BlockSpec(memory_space=pltpu.VMEM)
    loaded = (g_block, w_out, gpre, ext, conv, rate, igate, lru, wr, wi)
    return pl.pallas_call(
        functools.partial(recur_bwd_kernel, ex),
        out_shape=[
            half, half, half, half,
            jax.ShapeDtypeStruct((8, chans), F32),
            jax.ShapeDtypeStruct((rows, 1), F32),
            jax.ShapeDtypeStruct((rows, width), F32),
        ],
        in_specs=[anywhere] * 8 + [vmem] * 2 + [anywhere] * 2 + [vmem] * 2 + [anywhere],
        out_specs=[vmem] * 7,
        scratch_shapes=[pltpu.VMEM(array.shape, array.dtype) for array in loaded]
        + [
            pltpu.VMEM((rows, chans), F32),
            pltpu.VMEM((rows, chans), F32),
            pltpu.VMEM((rows + pad, chans), F32),
            pltpu.VMEM((count, 8, chans), F32),
            pltpu.VMEM((pad, chans), F32),
            pltpu.VMEM((pad, chans), F32),
            pltpu.VMEM((8, 8, chans), F32),
            sem((len(loaded),)), sem, sem, sem((count - 1,)), sem((count - 1,)),
        ]
        + ex.scratch(),
        compiler_params=pltpu.CompilerParams(
            collective_id=ident, has_side_effects=True, vmem_limit_bytes=62 << 20
        ),
    )(g_block, w_out, gpre, ext, conv, rate, igate, lru, pos, cw, wr, wi, sp, sg, down)


class Exchange(Routes):
    def __init__(self, n, rows, width, chunks, gather):
        super().__init__(n, rows, width)
        self.chunks, self.gather = chunks, gather
        self.size = rows // chunks

    def scratch(self):
        n, rows, half, chunks = self.n, self.rows, self.half, self.chunks
        shapes = [
            pltpu.VMEM((2, n - 1, rows, half), BF16),
            pltpu.VMEM((2, n - 1, rows, half), BF16),
            pltpu.VMEM((len(self.keeps), rows, half), F32),
            pltpu.SemaphoreType.DMA((2, n, chunks)),
            pltpu.SemaphoreType.DMA((2, n, chunks)),
        ]
        if self.gather:
            shapes += [
                pltpu.VMEM((n, 2, rows, half), BF16),
                pltpu.SemaphoreType.DMA((self.bits, 2, chunks)),
                pltpu.SemaphoreType.DMA((self.bits, 2, chunks)),
                pltpu.SemaphoreType.DMA((2, n, chunks)),
                pltpu.SemaphoreType.DMA((2, n, chunks)),
            ]
        return shapes

    def bind(self, refs):
        if self.gather:
            (self.out, self.into, self.acc, self.ss, self.rs,
             self.full, self.gs, self.gr, self.fs, self.fr) = refs
        else:
            self.out, self.into, self.acc, self.ss, self.rs = refs
        self.tok, self.me = lax.axis_index("tok"), lax.axis_index("ch")

    def span(self, c):
        return pl.ds(pl.multiple_of(c * self.size, self.size), self.size)

    def reduce_copy(self, part, mask, c):
        return pltpu.make_async_remote_copy(
            self.out.at[part, mask - 1, self.span(c)],
            self.into.at[part, mask - 1, self.span(c)],
            self.ss.at[part, mask, c],
            self.rs.at[part, mask, c],
            self.peer(self.bit_of(part, mask)),
            MESH,
        )

    def produce(self, c, block):
        span = self.span(c)
        for mask in sorted(range(self.n), key=lambda m: -m.bit_count()):
            value = block(mask)
            for part in range(2):
                piece = value[:, part * self.half : (part + 1) * self.half]
                if (part, mask) in self.keeps:
                    self.acc[self.keeps.index((part, mask)), span, :] = piece
                else:
                    self.out[part, mask - 1, span, :] = piece.astype(BF16)
                    self.reduce_copy(part, mask, c).start()

    def summed(self, part, mask, c):
        span = self.span(c)
        value = self.acc[self.keeps.index((part, mask)), span, :]
        for b in self.incoming(part, mask):
            came = mask | (1 << b)
            self.reduce_copy(part, came, c).wait_recv()
            value = value + self.into[part, came - 1, span, :].astype(F32)
        return value

    def pass_on(self, stage, c):
        for part in range(2):
            for mask in range(1, self.n):
                if self.stage_of(part, mask) == stage:
                    value = self.summed(part, mask, c)
                    self.out[part, mask - 1, self.span(c), :] = value.astype(BF16)
                    self.reduce_copy(part, mask, c).start()

    def close_reduce(self, c):
        for part in range(2):
            for mask in range(1, self.n):
                self.reduce_copy(part, mask, c).wait_send()

    def gather_copy(self, part, mask, b, c):
        block = self.full.at[self.me ^ mask, part, self.span(c)]
        if mask == 0:
            return pltpu.make_async_remote_copy(
                block, block, self.gs.at[b, part, c], self.gr.at[b, part, c], self.peer(b), MESH
            )
        got = mask | (1 << b)
        return pltpu.make_async_remote_copy(
            block, block, self.fs.at[part, got, c], self.fr.at[part, got, c], self.peer(b), MESH
        )

    def arrived(self, part, mask, c):
        block = self.full.at[self.me ^ mask, part, self.span(c)]
        if mask.bit_count() == 1:
            b = low_bit(mask)
            sems = (self.gs.at[b, part, c], self.gr.at[b, part, c])
        else:
            sems = (self.fs.at[part, mask, c], self.fr.at[part, mask, c])
        pltpu.make_async_remote_copy(block, block, *sems, self.peer(0), MESH).wait_recv()

    def gather_start(self, c, halves):
        for part in range(2):
            self.full[self.me, part, self.span(c), :] = halves[part].astype(BF16)
            for b in range(self.bits):
                self.gather_copy(part, 0, b, c).start()

    def nexts(self, part, mask):
        return range(high_bit(mask) + 1, self.bits) if part == 0 else range(low_bit(mask))

    def gather_pass(self, stage, c):
        for mask in [m for m in range(1, self.n) if m.bit_count() == stage]:
            for part in range(2):
                self.arrived(part, mask, c)
                for b in self.nexts(part, mask):
                    self.gather_copy(part, mask, b, c).start()

    def gather_close(self, c):
        for part in range(2):
            self.arrived(part, self.n - 1, c)
        for part in range(2):
            for b in range(self.bits):
                self.gather_copy(part, 0, b, c).wait_send()
            for mask in range(1, self.n):
                for b in self.nexts(part, mask):
                    self.gather_copy(part, mask, b, c).wait_send()

    def piece(self, owner, c):
        span = self.span(c)
        return jnp.concatenate([self.full[owner, 0, span, :], self.full[owner, 1, span, :]], axis=1)

    def own_sum(self, c):
        return [self.summed(part, 0, c) for part in range(2)]

    def run(self, stages, extra=None, after=None):
        depth = len(stages)

        def turn(t, _):
            if extra is not None:
                extra(t)
            for s in reversed(range(depth)):
                c = t - s

                @pl.when(jnp.logical_and(c >= 0, c < self.chunks))
                def _():
                    stages[s](c)

            if after is not None:
                after(t)
            return 0

        lax.fori_loop(0, self.chunks + depth - 1, turn, 0)


def tile_of(size):
    return next(t for t in (512, 384, 256, 128, size) if size % t == 0)


def mid_kernel(
    ex, branch, w_out, x_own, gain, wg_h, wu_h, wd_h, cot_h,
    normed_h, full_h, own_o, scale_o, hidden_h, gg_h, gu_h, down_h,
    wg, wu, wd, cot, normed, hidden, gg, gu, down, wsem, csem, osem, fsem, *refs,
):
    ex.bind(refs)
    n, width = ex.n, ex.width
    units = wg.shape[1]
    tile = tile_of(units)
    greet(ex.neighbours())
    loads = [
        pltpu.make_async_copy(a, b, wsem.at[i])
        for i, (a, b) in enumerate(((wg_h, wg), (wu_h, wu), (wd_h, wd)))
    ]
    for load in loads:
        load.start()

    def cot_load(c):
        return pltpu.make_async_copy(cot_h.at[ex.span(c)], cot, csem)

    outs = ((normed, normed_h), (hidden, hidden_h), (gg, gg_h), (gu, gu_h), (down, down_h))

    def store(i, c):
        source, target = outs[i]
        return pltpu.make_async_copy(source, target.at[ex.span(c)], osem.at[i])

    def full_store(c):
        span = ex.span(c)
        return pltpu.make_async_copy(
            ex.full.at[:, :, span], full_h.at[:, :, span], fsem.at[c]
        )

    cot_load(0).start()

    def first(c):
        rows = branch[ex.span(c), :]

        def block(mask):
            at = pl.multiple_of((ex.me ^ mask) * width, 128)
            return jnp.dot(rows, w_out[:, pl.ds(at, width)], preferred_element_type=F32)

        ex.produce(c, block)

    def own(c):
        span = ex.span(c)
        value = jnp.concatenate(ex.own_sum(c), axis=1) + x_own[span, :].astype(F32)
        own_o[span, :] = value
        ex.gather_start(c, [value[:, : ex.half], value[:, ex.half :]])
        ex.close_reduce(c)

    def final(c):
        ex.gather_close(c)
        full_store(c).start()

        @pl.when(c > 0)
        def _():
            store(0, c - 1).wait()

        def norm_rows(at):
            span = pl.ds(pl.multiple_of(c * ex.size + at, 16), 16)
            pieces = [
                ex.full[d, part, span, :].astype(F32) for d in range(n) for part in range(2)
            ]
            total = sum(jnp.sum(p * p, axis=1, keepdims=True) for p in pieces)
            scale = lax.rsqrt(total * (1.0 / (n * width)) + 1e-06)
            scale_o[span, :] = scale
            for i, p in enumerate(pieces):
                columns = slice(i * ex.half, (i + 1) * ex.half)
                normed[pl.ds(at, 16), columns] = (p * scale * gain[:, columns]).astype(BF16)

        over_rows(0, ex.size, 16, norm_rows)
        store(0, c).start()

    def feed(c):
        @pl.when(c == 0)
        def _():
            for load in loads:
                load.wait()

        cot_load(c).wait()

        @pl.when(c > 0)
        def _():
            for i in range(1, 5):
                store(i, c - 1).wait()

        for j in range(units // tile):
            columns = slice(j * tile, (j + 1) * tile)
            act, slope = gelu_parts(
                jnp.dot(normed[...], wg[:, columns], preferred_element_type=F32)
            )
            up = jnp.dot(normed[...], wu[:, columns], preferred_element_type=F32)
            grad = nt_dot(cot[...], wd[columns, :])
            hidden[:, columns] = (act * up).astype(BF16)
            gg[:, columns] = (grad * up * slope).astype(BF16)
            gu[:, columns] = (grad * act).astype(BF16)

        @pl.when(c + 1 < ex.chunks)
        def _():
            cot_load(c + 1).start()

        for i in range(1, 4):
            store(i, c).start()
        down[...] = jnp.dot(hidden[...], wd[...], preferred_element_type=F32).astype(BF16)
        store(4, c).start()

    stages = [first]
    stages += [functools.partial(ex.pass_on, s) for s in range(1, ex.bits)]
    stages += [own]
    stages += [functools.partial(ex.gather_pass, s) for s in range(1, ex.bits)]
    stages += [final]
    depth = len(stages)

    def after(t):
        c = t - (depth - 1)

        @pl.when(c >= 0)
        def _():
            feed(c)

    ex.run(stages, after=after)
    for i in range(5):
        store(i, ex.chunks - 1).wait()
    for c in range(ex.chunks):
        full_store(c).wait()


def mid_exchange(branch, w_out, x_own, gain, w_gate, w_up, w_down, cot, ident, chunks=4):
    n = lax.axis_size("ch")
    rows, width = x_own.shape
    units = w_gate.shape[1]
    ex = Exchange(n, rows, width, chunks, True)
    whole = jax.ShapeDtypeStruct((rows, n * width), BF16)
    inner = jax.ShapeDtypeStruct((rows, units), BF16)
    wide, narrow = pltpu.VMEM((ex.size, n * width), BF16), pltpu.VMEM((ex.size, units), BF16)
    sem = pltpu.SemaphoreType.DMA
    anywhere = pl.BlockSpec(memory_space=pl.ANY)
    vmem = pl.BlockSpec(memory_space=pltpu.VMEM)
    return pl.pallas_call(
        functools.partial(mid_kernel, ex),
        out_shape=[
            whole,
            jax.ShapeDtypeStruct((n, 2, rows, ex.half), BF16),
            jax.ShapeDtypeStruct((rows, width), F32),
            jax.ShapeDtypeStruct((rows, 1), F32),
            inner, inner, inner, whole,
        ],
        in_specs=[vmem] * 4 + [anywhere] * 4,
        out_specs=[anywhere, anywhere, vmem, vmem] + [anywhere] * 4,
        scratch_shapes=[
            pltpu.VMEM(w_gate.shape, BF16),
            pltpu.VMEM(w_up.shape, BF16),
            pltpu.VMEM(w_down.shape, BF16),
            wide, wide, narrow, narrow, narrow, wide,
            sem((3,)), sem, sem((5,)), sem((chunks,)),
        ]
        + ex.scratch(),
        compiler_params=pltpu.CompilerParams(
            collective_id=ident, has_side_effects=True, vmem_limit_bytes=62 << 20
        ),
    )(branch, w_out, x_own, gain, w_gate, w_up, w_down, cot)


def back_kernel(
    ex, grad_gate, grad_up, w_gate, w_up, full, mid_own, cot, cot_own, scale, gain_own,
    block_o, own_o, gain_o, *refs,
):
    ex.bind(refs)
    n, width = ex.n, ex.width
    greet(ex.neighbours())
    gain_o[...] = jnp.zeros_like(gain_o)

    def whole(d, c):
        span = ex.span(c)
        return jnp.concatenate([full[d, 0, span, :], full[d, 1, span, :]], axis=1).astype(F32)

    def first(c):
        span = ex.span(c)
        left, right = grad_gate[span, :], grad_up[span, :]

        def block(mask):
            at = pl.ds(pl.multiple_of((ex.me ^ mask) * width, 128), width)
            return nt_dot(left, w_gate[at, :]) + nt_dot(right, w_up[at, :])

        ex.produce(c, block)

    def own(c):
        span = ex.span(c)
        s = scale[span, :]
        grad = jnp.concatenate(ex.own_sum(c), axis=1)
        value = cot_own[span, :].astype(F32) + grad * gain_own[...] * s
        own_o[span, :] = value
        ex.gather_start(c, [value[:, : ex.half], value[:, ex.half :]])
        ex.close_reduce(c)
        product = grad * mid_own[span, :] * s
        gain_o[...] += jnp.sum(product.reshape(-1, 8, width), axis=0)

    def final(c):
        ex.gather_close(c)
        span = ex.span(c)
        s = scale[span, :]
        total = jnp.zeros((ex.size, 1), F32)
        for d in range(n):
            columns = slice(d * width, (d + 1) * width)
            delta = ex.piece(d, c).astype(F32) - cot[span, columns].astype(F32)
            total = total + jnp.sum(delta * whole(d, c), axis=1, keepdims=True)
        factor = s * s * total * (1.0 / (n * width))
        own_o[span, :] = own_o[span, :] - factor * mid_own[span, :]
        for d in range(n):
            columns = slice(d * width, (d + 1) * width)
            value = ex.piece(d, c).astype(F32) - factor * whole(d, c)
            block_o[span, columns] = value.astype(BF16)

    stages = [first]
    stages += [functools.partial(ex.pass_on, s) for s in range(1, ex.bits)]
    stages += [own]
    stages += [functools.partial(ex.gather_pass, s) for s in range(1, ex.bits)]
    stages += [final]
    ex.run(stages)


def back_exchange(
    grad_gate, grad_up, w_gate, w_up, full, mid_own, cot, cot_own, scale, gain_own, ident, chunks=4
):
    n = lax.axis_size("ch")
    rows, width = mid_own.shape
    ex = Exchange(n, rows, width, chunks, True)
    return pl.pallas_call(
        functools.partial(back_kernel, ex),
        out_shape=[
            jax.ShapeDtypeStruct((rows, n * width), BF16),
            jax.ShapeDtypeStruct((rows, width), F32),
            jax.ShapeDtypeStruct((8, width), F32),
        ],
        in_specs=whole_vmem(10),
        out_specs=whole_vmem(3),
        scratch_shapes=ex.scratch(),
        compiler_params=pltpu.CompilerParams(
            collective_id=ident, has_side_effects=True, vmem_limit_bytes=63 << 20
        ),
    )(grad_gate, grad_up, w_gate, w_up, full, mid_own, cot, cot_own, scale, gain_own)


class Line:
    def __init__(self, count, shape):
        self.count, self.shape, self.chips = count, shape, count // 2

    def scratch(self):
        blocks = (self.chips, *self.shape)
        hops = (max(self.chips - 1, 1), *self.shape)
        sems = [pltpu.SemaphoreType.DMA((self.chips,))] * 6
        return [pltpu.VMEM(blocks, BF16)] * 3 + [pltpu.VMEM(hops, BF16)] * 4 + sems

    def bind(self, refs):
        (self.pair_out, self.pair_in, self.home, self.up_out, self.up_in, self.dn_out, self.dn_in,
         self.ps, self.pr, self.us, self.ur, self.ds, self.dr) = refs
        self.tok, self.ch = lax.axis_index("tok"), lax.axis_index("ch")
        self.place, self.core = self.tok // 2, self.tok % 2

    def pair_copy(self, z):
        return pltpu.make_async_remote_copy(
            self.pair_out.at[z], self.pair_in.at[z], self.ps.at[z], self.pr.at[z],
            (self.tok + 1 - 2 * self.core, self.ch), MESH,
        )

    def away(self, z):
        return 2 * z + 1 - self.core

    def kept(self, z):
        return 2 * z + self.core

    def put_away(self, z, value):
        self.pair_out[z] = value.astype(BF16)
        self.pair_copy(z).start()

    def put_home(self, z, value):
        self.home[z] = value.astype(BF16)

    def over_rows(self, body):
        size = 32

        def one(i, _):
            body(pl.ds(i * size, size))
            return 0

        lax.fori_loop(0, self.shape[0] // size, one, 0, unroll=2)

    def join(self):
        for z in range(self.chips):
            self.pair_copy(z).wait_recv()

            def add(span, z=z):
                total = self.home[z, span, :].astype(F32) + self.pair_in[z, span, :].astype(F32)
                self.home[z, span, :] = total.astype(BF16)

            self.over_rows(add)

    def ways(self):
        last = self.chips - 1
        rising = (self.up_out, self.up_in, self.us, self.ur, self.place, 1)
        falling = (self.dn_out, self.dn_in, self.ds, self.dr, last - self.place, -1)
        return rising, falling

    def hop(self, way, far):
        out, into, ss, rs, _, sign = way
        count = self.count
        return pltpu.make_async_remote_copy(
            out.at[far - 1], into.at[far - 1], ss.at[far - 1], rs.at[far - 1],
            ((self.tok + 2 * sign + count) % count, self.ch), MESH,
        )

    def step(self, far):
        for way in self.ways():
            out, into, _, _, rank, sign = way

            @pl.when(rank + far <= self.chips - 1)
            def _():
                if far < self.chips - 1:

                    @pl.when(rank >= 1)
                    def _():
                        self.hop(way, far + 1).wait_recv()

                def add(span):
                    value = self.home[self.place + sign * far, span, :].astype(F32)
                    if far < self.chips - 1:
                        came = into[far, span, :].astype(F32)
                        value = value + jnp.where(rank >= 1, came, 0.0)
                    out[far - 1, span, :] = value.astype(BF16)

                self.over_rows(add)
                self.hop(way, far).start()

    def settle(self, result):
        if self.chips > 1:
            for way in self.ways():

                @pl.when(way[4] >= 1)
                def _():
                    self.hop(way, 1).wait_recv()

        def add(span):
            value = self.home[self.place, span, :].astype(F32)
            for way in self.ways() if self.chips > 1 else ():
                value = value + jnp.where(way[4] >= 1, way[1][0, span, :].astype(F32), 0.0)
            result[span, :] = value

        self.over_rows(add)

    def close(self):
        for z in range(self.chips):
            self.pair_copy(z).wait_send()
        for far in range(1, self.chips):
            for way in self.ways():

                @pl.when(way[4] + far <= self.chips - 1)
                def _():
                    self.hop(way, far).wait_send()


def end_kernel(
    ex, lines,
    g_rec, g_pre, w_branch, w_gelu, stat, small, normed, branch, g_block, gate_blocks, x_own,
    scale, gain_own, mid_own,
    input_o, small_o, gain_o, wb_o, wg_o, wo_o, gate_o,
    stats, stat_sum, smalls, gains, gain_acc, st_s, st_r, sm_s, sm_r, gn_s, gn_r, *refs,
):
    held = len(lines[0].scratch())
    for i, line in enumerate(lines):
        line.bind(refs[i * held : (i + 1) * held])
    ex.bind(refs[len(lines) * held :])
    n, width = ex.n, ex.width
    count = lax.axis_size("tok")
    across = [(ex.tok, ex.me ^ m) for m in range(1, n)]
    greet(across + tok_targets())
    stats[ex.me] = stat[...]
    copies = []
    for m in range(1, n):
        copy = pltpu.make_async_remote_copy(
            stats.at[ex.me], stats.at[ex.me], st_s.at[m - 1], st_r.at[m - 1], across[m - 1], MESH
        )
        copy.start()
        copies.append(copy)

    def spread(buffer, send, recv):
        for o, target in enumerate(tok_targets()):
            copy = pltpu.make_async_remote_copy(
                buffer.at[ex.tok], buffer.at[ex.tok], send.at[o], recv.at[o], target, MESH
            )
            copy.start()
            copies.append(copy)

    def collect(buffer, send, recv):
        for o in range(count - 1):
            block = buffer.at[lax.rem(ex.tok + count - 1 - o, count)]
            pltpu.make_async_remote_copy(
                block, block, send.at[o], recv.at[o], tok_targets()[o], MESH
            ).wait_recv()

    smalls[ex.tok] = small[...]
    spread(smalls, sm_s, sm_r)
    wo_line, wb_line, wg_line, gate_line = lines

    def columns(source, block, line):
        size = source.shape[1] // count
        return source[:, pl.ds(pl.multiple_of(block * size, 128), size)]

    def fill(line, product):
        def far_side(z, _):
            line.put_away(z, product(line.away(z)))
            return 0

        def near_side(z, _):
            line.put_home(z, product(line.kept(z)))
            return 0

        lax.fori_loop(0, line.chips, far_side, 0)
        lax.fori_loop(0, line.chips, near_side, 0)

    def start(line):
        line.join()
        if line.chips > 1:
            line.step(line.chips - 1)

    fill(gate_line, lambda d: gate_blocks[d].astype(F32))
    fill(wo_line, lambda d: tn_dot(branch[...], columns(g_block, d, wo_line)))
    start(wo_line)
    fill(wb_line, lambda d: tn_dot(columns(normed, d, wb_line), g_rec[...]))
    start(gate_line)
    start(wb_line)
    fill(wg_line, lambda d: tn_dot(columns(normed, d, wg_line), g_pre[...]))
    start(wg_line)
    for m in range(1, n):
        block = stats.at[ex.me ^ m]
        pltpu.make_async_remote_copy(
            block, block, st_s.at[m - 1], st_r.at[m - 1], across[m - 1], MESH
        ).wait_recv()
    stat_sum[...] = jnp.sum(stats[...], axis=0)
    gain_acc[...] = jnp.zeros_like(gain_acc)

    def first(c):
        span = ex.span(c)
        left, right = g_rec[span, :], g_pre[span, :]

        def block(mask):
            at = pl.ds(pl.multiple_of((ex.me ^ mask) * width, 128), width)
            return nt_dot(left, w_branch[at, :]) + nt_dot(right, w_gelu[at, :])

        ex.produce(c, block)

    def own(c):
        span = ex.span(c)
        grad = jnp.concatenate(ex.own_sum(c), axis=1)
        along = stat_sum[pl.ds(c, 1), :]
        square = (ex.size, ex.size)
        same = lax.broadcasted_iota(jnp.int32, square, 0) == lax.broadcasted_iota(
            jnp.int32, square, 1
        )
        term = jnp.sum(jnp.where(same, along, 0.0), axis=1, keepdims=True)
        s = scale[span, :]
        mine = x_own[span, :].astype(F32)
        input_o[span, :] = (
            mid_own[span, :]
            + s * gain_own[...] * grad
            - s * s * mine * (term * (1.0 / (n * width)))
        )
        gain_acc[...] += jnp.sum((grad * mine * s).reshape(-1, 8, width), axis=0)
        ex.close_reduce(c)

    stages = [first]
    stages += [functools.partial(ex.pass_on, s) for s in range(1, ex.bits)]
    stages += [own]
    turns = ex.chunks + len(stages) - 1
    acts = [
        functools.partial(line.step, far)
        for far in range(wo_line.chips - 2, 0, -1)
        for line in (wo_line, gate_line, wb_line, wg_line)
    ]

    def extra(t):
        for i, act in enumerate(acts):
            when = 2 + i * (turns - 2) // max(len(acts), 1)

            @pl.when(t == when)
            def _():
                act()

    ex.run(stages, extra)
    gains[ex.tok] = jnp.broadcast_to(jnp.sum(gain_acc[...], axis=0, keepdims=True), (8, width))
    spread(gains, gn_s, gn_r)
    collect(smalls, sm_s, sm_r)
    small_o[...] = jnp.sum(smalls[...], axis=0)
    wo_line.settle(wo_o)
    gate_line.settle(gate_o)
    wb_line.settle(wb_o)
    wg_line.settle(wg_o)
    collect(gains, gn_s, gn_r)
    gain_o[...] = jnp.sum(gains[...], axis=0)
    for copy in copies:
        copy.wait_send()
    for line in lines:
        line.close()


def end_exchange(
    g_rec, g_pre, w_branch, w_gelu, stat, small, normed, branch, g_block, gate_blocks, x_own,
    scale, gain_own, mid_own, ident,
):
    n, count = lax.axis_size("ch"), lax.axis_size("tok")
    rows, width = x_own.shape
    chans, total = g_rec.shape[1], normed.shape[1]
    chunks = stat.shape[0]
    ex = Exchange(n, rows, width, chunks, False)
    lines = [
        Line(count, (chans, total // count)),
        Line(count, (total // count, chans)),
        Line(count, (total // count, chans)),
        Line(count, gate_blocks.shape[1:]),
    ]
    sem = pltpu.SemaphoreType.DMA
    return pl.pallas_call(
        functools.partial(end_kernel, ex, lines),
        out_shape=[
            jax.ShapeDtypeStruct((rows, width), F32),
            jax.ShapeDtypeStruct(small.shape, F32),
            jax.ShapeDtypeStruct((8, width), F32),
            jax.ShapeDtypeStruct(lines[1].shape, F32),
            jax.ShapeDtypeStruct(lines[2].shape, F32),
            jax.ShapeDtypeStruct(lines[0].shape, F32),
            jax.ShapeDtypeStruct(lines[3].shape, F32),
        ],
        in_specs=whole_vmem(14),
        out_specs=whole_vmem(7),
        scratch_shapes=[
            pltpu.VMEM((n, *stat.shape), F32),
            pltpu.VMEM(stat.shape, F32),
            pltpu.VMEM((count, *small.shape), F32),
            pltpu.VMEM((count, 8, width), F32),
            pltpu.VMEM((8, width), F32),
            sem((n - 1,)), sem((n - 1,)),
            sem((count - 1,)), sem((count - 1,)),
            sem((count - 1,)), sem((count - 1,)),
        ]
        + [shape for line in lines for shape in line.scratch()]
        + ex.scratch(),
        compiler_params=pltpu.CompilerParams(
            collective_id=ident, has_side_effects=True, vmem_limit_bytes=63 << 20
        ),
    )(g_rec, g_pre, w_branch, w_gelu, stat, small, normed, branch, g_block, gate_blocks, x_own,
      scale, gain_own, mid_own)


def dense_blocks(blocks):
    count, size = blocks.shape[0], blocks.shape[1]
    whole = count * size
    column = lax.broadcasted_iota(jnp.int32, (size, whole), 1)
    copies = (column % size == lax.broadcasted_iota(jnp.int32, (size, whole), 0)).astype(BF16)
    tiled = jnp.dot(blocks.reshape(whole, size), copies, preferred_element_type=F32)
    shape = (whole, whole)
    row = lax.broadcasted_iota(jnp.int32, shape, 0) // size
    same = row == lax.broadcasted_iota(jnp.int32, shape, 1) // size
    return jnp.where(same, tiled, 0.0).astype(BF16)


def diagonal_blocks(full, count, size):
    return jnp.stack(
        [full[i * size : (i + 1) * size, i * size : (i + 1) * size] for i in range(count)]
    )


def to_major(rows):
    count, width = rows.shape
    return rows.reshape(SEGS, count // SEGS, width).swapaxes(0, 1).reshape(count, width)


def from_major(rows):
    count, width = rows.shape
    return rows.reshape(count // SEGS, SEGS, width).swapaxes(0, 1).reshape(count, width)


def tok_scatter(full, dim):
    summed = lax.psum_scatter(full.astype(BF16), "tok", scatter_dimension=dim, tiled=True)
    return summed.astype(F32)


def local(
    layer_in,
    positions,
    norm_gain,
    w_branch,
    w_gelu,
    conv_w,
    conv_b,
    w_rgate,
    b_rgate,
    w_igate,
    b_igate,
    decay_param,
    w_out,
    mlp_gain,
    w_gate,
    w_up,
    w_down,
    cotangent,
):
    rows, width = layer_in.shape
    ch_index = lax.axis_index("ch")
    column = ch_index * width
    chans = decay_param.shape[0]
    gates, gate_width = w_rgate.shape[0], w_rgate.shape[1]
    layer_in, cotangent = to_major(layer_in), to_major(cotangent)
    pos = to_major(positions[:, None])
    pos_tall = jnp.pad(pos, ((0, 8 * (conv_w.shape[0] - 1)), (0, 0)))
    sp = jax.nn.softplus(-decay_param)[None]
    sg = jax.nn.sigmoid(-decay_param)[None]
    dense_r, dense_i = dense_blocks(w_rgate), dense_blocks(w_igate)

    normed, scale_in, gate_pre, ext, conv, rate, igate, lru, branch, cot = front(
        layer_in, norm_gain[None], pos, w_branch, w_gelu, conv_w, conv_b[None], dense_r,
        b_rgate[None], dense_i, b_igate[None], sp, cotangent, 0,
    )
    normed_mid, mid_full, mid_own, scale_mid, hidden, grad_gate, grad_up, down = mid_exchange(
        branch, w_out, layer_in, mlp_gain[None], w_gate, w_up, w_down, cot, 2
    )
    grad_wdown = tok_scatter(tn_dot(hidden, cot), 1)
    grad_wgate = tok_scatter(tn_dot(normed_mid, grad_gate), 0)
    grad_wup = tok_scatter(tn_dot(normed_mid, grad_up), 0)
    gain_mid_own = lax.dynamic_slice_in_dim(mlp_gain, column, width, 0)[None]
    grad_block, grad_mid_own, gain_sum = back_exchange(
        grad_gate, grad_up, w_gate, w_up, mid_full, mid_own, cot, cotangent, scale_mid,
        gain_mid_own, 3,
    )
    count = lax.axis_size("tok")
    grad_rec, grad_gate_pre, grad_rate, grad_input, sums, row_term, mlp_out = recur_bwd(
        grad_block, w_out, gate_pre, ext, conv, rate, igate, lru, pos_tall, conv_w, dense_r,
        dense_i, sp, sg, down, 4,
    )
    layer_out = from_major((mid_own + mlp_out).astype(BF16))
    def gate_blocks(full):
        parts = diagonal_blocks(full, gates, gate_width).reshape(gates, count, -1, gate_width)
        return jnp.swapaxes(parts, 0, 1).reshape(count, -1, gate_width)

    conv_low = conv.astype(BF16)
    gate_parts = jnp.concatenate(
        [gate_blocks(tn_dot(conv_low, grad_rate)), gate_blocks(tn_dot(conv_low, grad_input))],
        axis=1,
    ).astype(BF16)
    stat = row_term.reshape(8, rows // 8)
    small_width = max(chans, width)
    small = jnp.concatenate(
        [
            jnp.pad(sums, ((0, 0), (0, small_width - chans))),
            jnp.pad(
                jnp.sum(gain_sum, axis=0, keepdims=True), ((0, 7), (0, small_width - width))
            ),
        ],
        axis=0,
    )
    own_gain = lax.dynamic_slice_in_dim(norm_gain, column, width, 0)[None]
    input_grad, small_sum, norm_gain_sum, grad_wbranch, grad_wgelu, grad_wout, gate_sum = (
        end_exchange(
            grad_rec, grad_gate_pre, w_branch, w_gelu, stat, small, normed, branch, grad_block,
            gate_parts, layer_in, scale_in, own_gain, grad_mid_own, 5,
        )
    )
    input_grad = from_major(input_grad)
    gate_grads = gate_sum.reshape(2, gates, -1, gate_width)
    own_norm_gain = norm_gain_sum[0]
    return (
        layer_out,
        input_grad,
        own_norm_gain,
        grad_wbranch,
        grad_wgelu,
        small_sum[4:8, :chans],
        small_sum[3, :chans],
        gate_grads[0],
        small_sum[1, :chans],
        gate_grads[1],
        small_sum[2, :chans],
        small_sum[0, :chans],
        grad_wout,
        small_sum[8, :width],
        grad_wgate,
        grad_wup,
        grad_wdown,
    )


def solution(mesh):
    placed = (
        P("tok", "ch"),
        P("tok"),
        P(),
        P(None, "ch"),
        P(None, "ch"),
        P(None, "ch"),
        P("ch"),
        P("ch", None, None),
        P("ch"),
        P("ch", None, None),
        P("ch"),
        P("ch"),
        P("ch", None),
        P(),
        P(None, "ch"),
        P(None, "ch"),
        P("ch", None),
        P("tok", "ch"),
    )
    return jax.shard_map(
        local,
        mesh=mesh,
        in_specs=placed,
        out_specs=(
            P("tok", "ch"),
            P("tok", "ch"),
            P("ch"),
            P("tok", "ch"),
            P("tok", "ch"),
            P(None, "ch"),
            P("ch"),
            P("ch", "tok", None),
            P("ch"),
            P("ch", "tok", None),
            P("ch"),
            P("ch"),
            P("ch", "tok"),
            P("ch"),
            P("tok", "ch"),
            P("tok", "ch"),
            P("ch", "tok"),
        ),
        check_vma=False,
    )
```

```python
import functools

import jax
import jax.numpy as jnp
from jax import lax
from jax.experimental import pallas as pl
from jax.experimental.pallas import tpu as pltpu
from jax.sharding import PartitionSpec as P

MESH = pl.DeviceIdType.MESH
F32 = jnp.float32
BF16 = jnp.bfloat16
SEGS = 8
GELU_A = 0.7978845608028654
GELU_B = 0.044715


def low_bit(mask):
    return (mask & -mask).bit_length() - 1


def high_bit(mask):
    return mask.bit_length() - 1


def gelu_parts(x):
    inner = jnp.tanh(GELU_A * (x + GELU_B * x * x * x))
    act = 0.5 * x * (1.0 + inner)
    slope = 0.5 * (1.0 + inner) + 0.5 * x * (1.0 - inner * inner) * GELU_A * (
        1.0 + 3.0 * GELU_B * x * x
    )
    return act, slope


def gelu_value(x):
    return 0.5 * x * (1.0 + jnp.tanh(GELU_A * (x + GELU_B * x * x * x)))


def minus_expm1(y, exp_y):
    series = 1.0 + y * (1.0 / 7.0)
    for k in (6, 5, 4, 3, 2):
        series = 1.0 + y * (1.0 / k) * series
    return jnp.where(y > -0.35, -y * series, 1.0 - exp_y)


def nt_dot(a, b):
    return lax.dot_general(a, b, (((1,), (1,)), ((), ())), preferred_element_type=F32)


def tn_dot(a, b):
    return lax.dot_general(a, b, (((0,), (0,)), ((), ())), preferred_element_type=F32)


def block_of(shape, axis, size):
    index = lax.broadcasted_iota(jnp.int32, shape, axis).astype(F32)
    return jnp.floor((index + 0.5) * (1.0 / size))


def tiled_ones(size, count):
    shape = (size, count * size)
    row = lax.broadcasted_iota(jnp.int32, shape, 0).astype(F32)
    column = lax.broadcasted_iota(jnp.int32, shape, 1).astype(F32)
    return (column - block_of(shape, 1, size) * size == row).astype(BF16)


def same_block(count, size):
    shape = (count * size, count * size)
    return block_of(shape, 0, size) == block_of(shape, 1, size)


def whole_vmem(count):
    return [pl.BlockSpec(memory_space=pltpu.VMEM)] * count


def greet(targets):
    barrier = pltpu.get_barrier_semaphore()
    for target in targets:
        pl.semaphore_signal(barrier, inc=1, device_id=target, device_id_type=MESH)
    pl.semaphore_wait(barrier, len(targets))


class Routes:
    def __init__(self, n, rows, width):
        self.n, self.rows, self.width = n, rows, width
        self.bits = n.bit_length() - 1
        self.half = width // 2
        self.keeps = [(part, m) for part in range(2) for m in range(n) if self.incoming(part, m)]

    def peer(self, b):
        return (self.tok, self.me ^ (1 << b))

    def neighbours(self):
        return [self.peer(b) for b in range(self.bits)]

    def bit_of(self, part, mask):
        return low_bit(mask) if part == 0 else high_bit(mask)

    def incoming(self, part, mask):
        if mask == 0:
            return list(range(self.bits)) if part == 0 else list(reversed(range(self.bits)))
        if part == 0:
            return list(range(low_bit(mask)))
        return list(reversed(range(high_bit(mask) + 1, self.bits)))

    def stage_of(self, part, mask):
        return low_bit(mask) if part == 0 else self.bits - 1 - high_bit(mask)


class Spread(Routes):
    def scratch(self):
        shape = (2, self.n, self.rows, self.half)
        keeps = (len(self.keeps), self.rows, self.half)
        return [
            pltpu.VMEM(shape, BF16),
            pltpu.VMEM(keeps, BF16),
            pltpu.SemaphoreType.DMA((2, self.n)),
            pltpu.SemaphoreType.DMA((2, self.n)),
            pltpu.SemaphoreType.DMA((len(self.keeps),)),
        ]

    def bind(self, refs, source):
        self.into, self.own, self.ss, self.rs, self.ls = refs
        self.source = source
        self.tok, self.me = lax.axis_index("tok"), lax.axis_index("ch")

    def view(self, part, mask):
        at = (self.me ^ mask) * self.width + part * self.half
        return self.source.at[:, pl.ds(pl.multiple_of(at, 128), self.half)]

    def copy(self, part, mask):
        held = (part, mask) in self.keeps
        block = self.own.at[self.keeps.index((part, mask))] if held else self.view(part, mask)
        return pltpu.make_async_remote_copy(
            block,
            self.into.at[part, mask],
            self.ss.at[part, mask],
            self.rs.at[part, mask],
            self.peer(self.bit_of(part, mask)),
            MESH,
        )

    def fetch(self, at):
        return pltpu.make_async_copy(self.view(*self.keeps[at]), self.own.at[at], self.ls.at[at])

    def launch(self):
        for part in range(2):
            for mask in range(1, self.n):
                if (part, mask) not in self.keeps:
                    self.copy(part, mask).start()
        for at in range(len(self.keeps)):
            self.fetch(at).start()

    def gather_in(self, part, mask, write):
        at = self.keeps.index((part, mask))
        self.fetch(at).wait()
        came = [mask | (1 << b) for b in self.incoming(part, mask)]
        for m in came:
            self.copy(part, m).wait_recv()

        def add(i, _):
            span = pl.ds(i * 32, 32)
            value = self.own[at, span, :].astype(F32)
            for m in came:
                value = value + self.into[part, m, span, :].astype(F32)
            write(at, span, value)
            return 0

        lax.fori_loop(0, self.rows // 32, add, 0, unroll=2)

    def relay(self, stage):
        def write(at, span, value):
            self.own[at, span, :] = value.astype(BF16)

        for part in range(2):
            for mask in range(1, self.n):
                if self.stage_of(part, mask) == stage:
                    self.gather_in(part, mask, write)
                    self.copy(part, mask).start()

    def settle(self, result):
        for part in range(2):

            def write(at, span, value, part=part):
                result[span, part * self.half : (part + 1) * self.half] = value

            self.gather_in(part, 0, write)
        for part in range(2):
            for mask in range(1, self.n):
                self.copy(part, mask).wait_send()


def tok_targets():
    count = lax.axis_size("tok")
    tok, ch = lax.axis_index("tok"), lax.axis_index("ch")
    return [(lax.rem(tok + o, count), ch) for o in range(1, count)]


def share_rows(buffer, send, recv):
    tok = lax.axis_index("tok")
    copies = []
    for o, target in enumerate(tok_targets()):
        copy = pltpu.make_async_remote_copy(
            buffer.at[tok], buffer.at[tok], send.at[o], recv.at[o], target, MESH
        )
        copy.start()
        copies.append(copy)
    count = lax.axis_size("tok")
    for o in range(count - 1):
        source = lax.rem(tok + count - 1 - o, count)
        pltpu.make_async_remote_copy(
            buffer.at[source], buffer.at[source], send.at[o], recv.at[o], tok_targets()[o], MESH
        ).wait_recv()
    return copies


class Gather(Routes):
    def __init__(self, n, rows, width, chunks):
        super().__init__(n, rows, width)
        self.chunks, self.size = chunks, rows // chunks

    def scratch(self):
        sem = pltpu.SemaphoreType.DMA
        near, far = (self.bits, self.chunks), (2, self.n, self.chunks)
        return [sem(near), sem(near), sem(far), sem(far), sem]

    def bind(self, refs, x, full):
        self.gs, self.gr, self.fs, self.fr, self.here = refs
        self.x, self.full = x, full
        self.tok, self.me = lax.axis_index("tok"), lax.axis_index("ch")

    def place(self, owner, part, c):
        span = pl.ds(c * self.size, self.size)
        if part is None:
            return self.full.at[span, pl.ds(pl.multiple_of(owner * self.width, 128), self.width)]
        at = owner * self.width + part * self.half
        return self.full.at[span, pl.ds(pl.multiple_of(at, 128), self.half)]

    def near_copy(self, b, c, owner):
        return pltpu.make_async_remote_copy(
            self.x.at[pl.ds(c * self.size, self.size)],
            self.place(owner, None, c),
            self.gs.at[b, c],
            self.gr.at[b, c],
            self.peer(b),
            MESH,
        )

    def far_copy(self, part, mask, b, c):
        block, got = self.place(self.me ^ mask, part, c), mask | (1 << b)
        return pltpu.make_async_remote_copy(
            block, block, self.fs.at[part, got, c], self.fr.at[part, got, c], self.peer(b), MESH
        )

    def own_copy(self):
        at = pl.ds(pl.multiple_of(self.me * self.width, 128), self.width)
        return pltpu.make_async_copy(self.x, self.full.at[:, at], self.here)

    def launch(self, order):
        for c in order:
            for b in range(self.bits):
                self.near_copy(b, c, self.me).start()
        self.own_copy().start()

    def nexts(self, part, mask):
        return range(high_bit(mask) + 1, self.bits) if part == 0 else range(low_bit(mask))

    def far_arrived(self, part, mask, c):
        block = self.place(self.me ^ mask, part, c)
        pltpu.make_async_remote_copy(
            block, block, self.fs.at[part, mask, c], self.fr.at[part, mask, c], self.peer(0), MESH
        ).wait_recv()

    def forward(self, c):
        for count in range(1, self.bits):
            for mask in [m for m in range(1, self.n) if m.bit_count() == count]:
                if count == 1:
                    self.near_copy(low_bit(mask), c, self.me ^ mask).wait_recv()
                for part in range(2):
                    if count > 1:
                        self.far_arrived(part, mask, c)
                    for b in self.nexts(part, mask):
                        self.far_copy(part, mask, b, c).start()

    def finish(self, c):
        for part in range(2):
            self.far_arrived(part, self.n - 1, c)

    def close(self):
        for c in range(self.chunks):
            for b in range(self.bits):
                self.near_copy(b, c, self.me).wait_send()
            for mask in range(1, self.n):
                for part in range(2):
                    for b in self.nexts(part, mask):
                        self.far_copy(part, mask, b, c).wait_send()


def over_rows(start, rows, step, body, unroll=1):
    def one(i, _):
        body(pl.multiple_of(start + i * step, 8))
        return 0

    lax.fori_loop(0, rows // step, one, 0, unroll=unroll)


def eight(value):
    return value.reshape(-1, SEGS, value.shape[-1])


def with_segments(value, seg):
    return (eight(value) * seg[None]).reshape(value.shape)


def front_kernel(
    ga, late, x, gain, pos_in, wb_h, wg_h, cw, cb_in, br_in, bi_in, dp_in, gate_r, gate_i, cot,
    normed_h, scale, gpre_h, ext_h, conv_h, rate_h, igate_h, lru, branch, cot_full, vectors, wr, wi,
    pos,
    full, normed, wb, wg, gpre, ext, conv, rate, igate, low, a_s, h_s, carry, halo, ends,
    wsem, osem, halo_send, halo_recv, send, recv, *refs,
):
    held = len(ga.scratch())
    ga.bind(refs[:held], x, full)
    late.bind(refs[held:], cot, cot_full)
    cb, br, bi, sp = (vectors.at[i : i + 1] for i in range(4))
    for i, vector in enumerate((cb_in, br_in, bi_in)):
        vectors[i : i + 1, :] = vector[...].reshape(1, -1)
    minus = -dp_in[...].reshape(1, -1)
    vectors[3:4, :] = jnp.maximum(minus, 0.0) + jnp.log1p(jnp.exp(-jnp.abs(minus)))
    vectors[4:5, :] = jax.nn.sigmoid(minus)
    rows, chans = gpre.shape
    taps = cw.shape[0]
    pad = 8 * (taps - 1)
    tok, ch = lax.axis_index("tok"), lax.axis_index("ch")
    count = lax.axis_size("tok")
    total_width = full.shape[1]
    greet(tok_targets() + ga.neighbours())
    order = [ga.chunks - 1] + list(range(ga.chunks - 1))
    ga.launch(order)
    loads = [
        pltpu.make_async_copy(a, b, wsem.at[i])
        for i, (a, b) in enumerate(((wb_h, wb), (wg_h, wg)))
    ]
    for load in loads:
        load.start()
    blocks, block = gate_r.shape[0] // gate_r.shape[1], gate_r.shape[1]
    for source, target in ((gate_r, wr), (gate_i, wi)):
        copies = jnp.dot(source[...], tiled_ones(block, blocks), preferred_element_type=F32)
        target[...] = jnp.where(same_block(blocks, block), copies, 0.0).astype(BF16)
    for t in range(rows // SEGS):
        pos[t * SEGS : (t + 1) * SEGS, :] = pos_in[:, t : t + 1]
    pos[rows:, :] = jnp.zeros((pos.shape[0] - rows, 1), jnp.int32)
    step = 16
    size = ga.size
    stores = []

    def store(source, target):
        copy = pltpu.make_async_copy(source, target, osem.at[len(stores)])
        copy.start()
        stores.append(copy)

    halo_copy = pltpu.make_async_remote_copy(
        ext.at[pl.ds(rows, pad)], halo, halo_send, halo_recv,
        (lax.rem(tok + 1, count), ch), MESH,
    )

    def norm_rows(at):
        span = pl.ds(at, step)
        value = full[span, :].astype(F32)
        s = lax.rsqrt(
            jnp.sum(value * value, axis=1, keepdims=True) * (1.0 / total_width) + 1e-06
        )
        scale[span, :] = s
        normed[span, :] = (value * s * gain[...]).astype(BF16)

    def enter(c):
        over_rows(c * size, size, step, norm_rows)
        span = pl.ds(c * size, size)
        ext[pl.ds(pad + c * size, size), :] = jnp.dot(
            normed[span, :], wb[...], preferred_element_type=F32
        )
        gpre[span, :] = jnp.dot(normed[span, :], wg[...], preferred_element_type=F32)

    def conv_rows(at):
        span = pl.ds(at, step)
        window = ext[pl.ds(at, step + pad), :]
        where = pos[span, :]
        value = cb[...] + cw[0:1, :] * window[pad : pad + step]
        for k in range(1, taps):
            shifted = window[pad - 8 * k : pad - 8 * k + step]
            value = value + jnp.where(where >= k, cw[k : k + 1, :] * shifted, 0.0)
        conv[span, :] = value
        low[span, :] = value.astype(BF16)

    def gate_rows(at):
        span = pl.ds(at, step)
        where = pos[span, :]
        r = jax.nn.sigmoid(rate[span, :])
        g = jax.nn.sigmoid(igate[span, :])
        rate[span, :] = r
        igate[span, :] = g
        log_decay = -8.0 * r * sp[...]
        decay = jnp.exp(log_decay)
        mult = jnp.sqrt(minus_expm1(2.0 * log_decay, decay * decay))
        mult = jnp.where(where > 0, mult, 1.0)
        a_s[span, :] = jnp.where(where > 0, decay, 0.0)
        h_s[span, :] = g * conv[span, :] * mult

    def scan_rows(c):
        def one(t, state):
            h, p = state
            span = pl.ds(pl.multiple_of(c * size + t * SEGS, SEGS), SEGS)
            a = a_s[span, :]
            h = a * h + h_s[span, :]
            p = a * p
            h_s[span, :] = h
            a_s[span, :] = p
            return h, p

        h, p = lax.fori_loop(0, size // SEGS, one, (carry[0], carry[1]), unroll=4)
        carry[0] = h
        carry[1] = p

    def recur(c):
        over_rows(c * size, size, step, conv_rows, 2)
        span = pl.ds(c * size, size)
        rate[span, :] = jnp.dot(low[span, :], wr[...], preferred_element_type=F32) + br[...]
        igate[span, :] = jnp.dot(low[span, :], wi[...], preferred_element_type=F32) + bi[...]
        over_rows(c * size, size, step, gate_rows, 2)
        scan_rows(c)

    carry[0] = jnp.zeros((SEGS, chans), F32)
    carry[1] = jnp.ones((SEGS, chans), F32)
    for i, c in enumerate(order):
        if i == 0:
            ga.forward(c)
        if i + 1 < len(order):
            ga.forward(order[i + 1])
        if i + 2 == len(order):
            late.launch(range(late.chunks))
        ga.finish(c)
        if i == 0:
            ga.own_copy().wait()
            for load in loads:
                load.wait()
        enter(c)
        if i == 0:
            halo_copy.start()
        if i == 1:
            halo_copy.wait()
            last_row = lax.broadcasted_iota(jnp.int32, (SEGS, chans), 0) == SEGS - 1
            for j in range(taps - 1):
                here = ext[pl.ds(rows + 8 * j, 8), :]
                joined = jnp.where(last_row, halo[8 * j : 8 * j + 8, :], here)
                ext[8 * j : 8 * j + 8, :] = pltpu.roll(joined, 1, 0)
        if i + 1 == len(order):
            late.forward(0)
        if i >= 1:
            recur(c)
    late.forward(1)
    store(normed, normed_h)
    store(gpre, gpre_h)
    store(ext, ext_h)
    recur(ga.chunks - 1)
    late.forward(2)
    store(conv, conv_h)
    store(rate, rate_h)
    store(igate, igate_h)
    h_end, p_end = carry[0], carry[1]
    total_h, total_p = jnp.zeros((1, chans), F32), jnp.ones((1, chans), F32)
    for s in range(SEGS):
        total_h = p_end[s : s + 1] * total_h + h_end[s : s + 1]
        total_p = p_end[s : s + 1] * total_p
    ends[tok, 0:1, :] = total_h
    ends[tok, 1:2, :] = total_p
    sends = share_rows(ends, send, recv)
    state = jnp.zeros((1, chans), F32)
    for source in range(count - 1):
        after = ends[source, 1:2, :] * state + ends[source, 0:1, :]
        state = jnp.where(source < tok, after, state)
    for s in range(SEGS):
        lru[s : s + 1, :] = state
        state = p_end[s : s + 1] * state + h_end[s : s + 1]
    seg = lru[0:8, :]
    late.forward(3)

    def finish_rows(at):
        span = pl.ds(at, step)
        value = h_s[span, :] + with_segments(a_s[span, :], seg)
        lru[pl.ds(8 + at, step), :] = value
        branch[span, :] = (value * gelu_value(gpre[span, :])).astype(BF16)

    over_rows(0, rows, step, finish_rows, 2)
    for copy in sends:
        copy.wait_send()
    ga.close()
    for c in range(late.chunks):
        late.finish(c)
    late.close()
    late.own_copy().wait()
    for copy in stores:
        copy.wait()


def front(x, gain, pos, w_branch, w_gelu, cw, cb, br, bi, dp, gate_r, gate_i, cot, ident, chunks=4):
    n, count = lax.axis_size("ch"), lax.axis_size("tok")
    rows, width = x.shape
    total, chans = w_branch.shape
    taps = cw.shape[0]
    pad = 8 * (taps - 1)
    ga, late = Gather(n, rows, width, chunks), Gather(n, rows, width, 4)
    sem = pltpu.SemaphoreType.DMA
    grid = (rows, chans)
    anywhere = pl.BlockSpec(memory_space=pl.ANY)
    vmem = pl.BlockSpec(memory_space=pltpu.VMEM)
    return pl.pallas_call(
        functools.partial(front_kernel, ga, late),
        out_shape=[
            jax.ShapeDtypeStruct((rows, total), BF16),
            jax.ShapeDtypeStruct((rows, 1), F32),
            jax.ShapeDtypeStruct(grid, F32),
            jax.ShapeDtypeStruct((rows + pad, chans), F32),
            jax.ShapeDtypeStruct(grid, F32),
            jax.ShapeDtypeStruct(grid, F32),
            jax.ShapeDtypeStruct(grid, F32),
            jax.ShapeDtypeStruct((rows + 8, chans), F32),
            jax.ShapeDtypeStruct(grid, BF16),
            jax.ShapeDtypeStruct((rows, total), BF16),
            jax.ShapeDtypeStruct((8, chans), F32),
            jax.ShapeDtypeStruct((chans, chans), BF16),
            jax.ShapeDtypeStruct((chans, chans), BF16),
            jax.ShapeDtypeStruct((rows + pad, 1), jnp.int32),
        ],
        in_specs=[anywhere, vmem, vmem, anywhere, anywhere] + [vmem] * 7 + [anywhere],
        out_specs=[
            anywhere, vmem, anywhere, anywhere, anywhere, anywhere, anywhere, vmem, vmem,
            anywhere, vmem, vmem, vmem, vmem,
        ],
        scratch_shapes=[
            pltpu.VMEM((rows, total), BF16),
            pltpu.VMEM((rows, total), BF16),
            pltpu.VMEM(w_branch.shape, BF16),
            pltpu.VMEM(w_gelu.shape, BF16),
            pltpu.VMEM(grid, F32),
            pltpu.VMEM((rows + pad, chans), F32),
            pltpu.VMEM(grid, F32),
            pltpu.VMEM(grid, F32),
            pltpu.VMEM(grid, F32),
            pltpu.VMEM(grid, BF16),
            pltpu.VMEM(grid, F32),
            pltpu.VMEM(grid, F32),
            pltpu.VMEM((2, SEGS, chans), F32),
            pltpu.VMEM((pad, chans), F32),
            pltpu.VMEM((count, 8, chans), F32),
            sem((2,)), sem((6,)), sem, sem, sem((count - 1,)), sem((count - 1,)),
        ]
        + ga.scratch()
        + late.scratch(),
        compiler_params=pltpu.CompilerParams(
            collective_id=ident, has_side_effects=True, vmem_limit_bytes=60 << 20
        ),
    )(x, gain, pos, w_branch, w_gelu, cw, cb, br, bi, dp, gate_r, gate_i, cot)


def recur_bwd_kernel(
    ex, g_block_h, w_out_h, gpre_h, ext_h, conv_h, rate_h, igate_h, lru_h, pos, cw, wr_h, wi_h, vectors,
    down,
    grec, ggp_h, gate_o, sums, row_term, down_sum,
    g_block, w_out, gpre, ext, conv, rate, igate, lru, wr, wi,
    ggp, grate, ginput, low,
    g_s, a_s, gc, ends, edge, landed, acc, lsem, osem, edge_send, edge_recv, send, recv, *refs,
):
    ex.bind(refs, down)
    sp, sg = vectors.at[3:4], vectors.at[4:5]
    rows, chans = conv.shape
    taps = cw.shape[0]
    pad = 8 * (taps - 1)
    tok, ch = lax.axis_index("tok"), lax.axis_index("ch")
    count = lax.axis_size("tok")
    pairs = (
        (g_block_h, g_block), (w_out_h, w_out), (gpre_h, gpre), (lru_h, lru), (rate_h, rate),
        (igate_h, igate), (conv_h, conv), (wr_h, wr), (wi_h, wi), (ext_h, ext),
    )
    loads = [pltpu.make_async_copy(a, b, lsem.at[i]) for i, (a, b) in enumerate(pairs)]
    for load in loads:
        load.start()
    greet(tok_targets() + ex.neighbours())
    ex.launch()
    step = 16
    big = min(256, rows)
    for load in loads[:5]:
        load.wait()

    def begin_rows(at):
        span = pl.ds(at, step)
        act, slope = gelu_parts(gpre[span, :])
        grad = g_s[span, :]
        g_s[span, :] = grad * act
        ggp[span, :] = (grad * lru[pl.ds(8 + at, step), :] * slope).astype(BF16)
        a_s[span, :] = jnp.where(pos[span, :] > 0, jnp.exp(-8.0 * rate[span, :] * sp[...]), 0.0)

    def begin(i, state):
        at = pl.multiple_of(rows - (i + 1) * big, 8)
        g_s[pl.ds(at, big), :] = nt_dot(g_block[pl.ds(at, big), :], w_out[...])
        over_rows(at, big, step, begin_rows, 2)

        def one(t, state):
            v, q = state
            span = pl.ds(pl.multiple_of(at + big - (t + 1) * SEGS, SEGS), SEGS)
            a = a_s[span, :]
            c = g_s[span, :] + v
            g_s[span, :] = c
            a_s[span, :] = q
            return a * c, a * q

        return lax.fori_loop(0, big // SEGS, one, state, unroll=4)

    v_end, q_end = lax.fori_loop(
        0, rows // big, begin, (jnp.zeros((SEGS, chans), F32), jnp.ones((SEGS, chans), F32))
    )
    total_v, total_q = jnp.zeros((1, chans), F32), jnp.ones((1, chans), F32)
    for s in reversed(range(SEGS)):
        total_v = q_end[s : s + 1] * total_v + v_end[s : s + 1]
        total_q = q_end[s : s + 1] * total_q
    ends[tok, 0:1, :] = total_v
    ends[tok, 1:2, :] = total_q
    ggp_store = pltpu.make_async_copy(ggp, ggp_h, osem)
    ggp_store.start()
    sends = share_rows(ends, send, recv)
    state = jnp.zeros((1, chans), F32)
    for source in reversed(range(1, count)):
        after = ends[source, 1:2, :] * state + ends[source, 0:1, :]
        state = jnp.where(source > tok, after, state)
    entering = [None] * SEGS
    for s in reversed(range(SEGS)):
        entering[s] = state
        state = q_end[s : s + 1] * state + v_end[s : s + 1]
    for s in range(SEGS):
        edge[s : s + 1, :] = entering[s]
    seg = edge[0:8, :]
    acc[...] = jnp.zeros_like(acc)
    for load in loads[5:]:
        load.wait()

    def folded(x):
        return jnp.sum(eight(x), axis=0)

    def middle_rows(at):
        span = pl.ds(at, step)
        carried = g_s[span, :] + with_segments(a_s[span, :], seg)
        before = lru[span, :]
        keep = pos[span, :] > 0
        r, g, out = rate[span, :], igate[span, :], conv[span, :]
        log_decay = -8.0 * r * sp[...]
        decay = jnp.exp(log_decay)
        square = decay * decay
        mult = jnp.where(keep, jnp.sqrt(minus_expm1(2.0 * log_decay, square)), 1.0)
        scaled = carried * g
        grad_log = jnp.where(keep, decay * carried * before - scaled * out * square / mult, 0.0)
        slope = 8.0 * r * grad_log
        grad_rate = (-slope * sp[...] * (1.0 - r)).astype(BF16)
        grad_input = (scaled * out * mult * (1.0 - g)).astype(BF16)
        grate[span, :] = grad_rate
        ginput[span, :] = grad_input
        low[span, :] = out.astype(BF16)
        gc[span, :] = scaled * mult
        acc[0] += folded(slope * sg[...])
        acc[1] += folded(grad_rate.astype(F32))
        acc[2] += folded(grad_input.astype(F32))

    def middle(i, _):
        at = pl.multiple_of(i * big, 8)
        over_rows(at, big, step, middle_rows)
        span = pl.ds(at, big)
        gc[span, :] += nt_dot(grate[span, :], wr[...]) + nt_dot(ginput[span, :], wi[...])
        return 0

    lax.fori_loop(0, rows // big, middle, 0)
    gc[pl.ds(rows, pad), :] = jnp.zeros((pad, chans), F32)
    for j in range(1, taps):
        value = jnp.zeros((8, chans), F32)
        for k in range(j, taps):
            e = 8 * (k - j)
            masked = jnp.where(pos[e : e + 8, :] >= k, gc[e : e + 8, :], 0.0)
            value = value + cw[k : k + 1, :] * masked
        edge[pad - 8 * j : pad - 8 * j + 8, :] = value
    edge_copy = pltpu.make_async_remote_copy(
        edge, landed, edge_send, edge_recv, (lax.rem(tok + count - 1, count), ch), MESH
    )
    edge_copy.start()
    for stage in range(1, ex.bits):
        ex.relay(stage)

    block = gate_o.shape[2]
    blocks = chans // block
    each = block // count
    shape = (chans, chans)
    row = lax.broadcasted_iota(jnp.int32, shape, 0).astype(F32)
    part = block_of(shape, 0, blocks * each)
    which = block_of(shape, 0, each) - part * blocks
    within = row - block_of(shape, 0, each) * each
    wanted = which * block + part * each + within
    column = lax.broadcasted_iota(jnp.int32, shape, 1).astype(F32)
    order = (column == wanted).astype(BF16)
    same = same_block(blocks, block)
    for i, grads in enumerate((grate, ginput)):
        kept = jnp.where(same, tn_dot(low[...], grads[...]), 0.0).astype(BF16)
        folded_in = nt_dot(kept, tiled_ones(block, blocks)).astype(BF16)
        value = jnp.dot(order, folded_in, preferred_element_type=F32)
        height = blocks * each
        for d in range(count):
            gate_o[d, i * height : (i + 1) * height, :] = value[d * height : (d + 1) * height]

    def last_rows(at):
        step = 32
        span = pl.ds(at, step)
        window = gc[pl.ds(at, step + pad), :]
        where = pos[pl.ds(at, step + pad), :]
        source = ext[pl.ds(at, step + pad), :]
        here = window[:step]
        total = cw[0:1, :] * here
        acc[3] += folded(here)
        acc[4] += folded(here * source[pad : pad + step])
        for k in range(1, taps):
            masked = jnp.where(where >= k, window, 0.0)
            total = total + cw[k : k + 1, :] * masked[8 * k : 8 * k + step]
            acc[4 + k] += folded(masked[:step] * source[pad - 8 * k : pad - 8 * k + step])
        gc[span, :] = total
        grec[span, :] = total.astype(BF16)
        both = total.astype(BF16).astype(F32) * source[pad : pad + step]
        both = both + ggp[span, :].astype(F32) * gpre[span, :]
        row_term[span, :] = jnp.sum(both, axis=1, keepdims=True)

    over_rows(0, rows, 32, last_rows)
    edge_copy.wait()
    first_row = lax.broadcasted_iota(jnp.int32, (SEGS, chans), 0) == 0
    for j in range(0, pad, 8):
        joined = jnp.where(first_row, landed[j : j + 8, :], edge[j : j + 8, :])
        at = pl.ds(rows - pad + j, 8)
        gc[at, :] = gc[at, :] + pltpu.roll(joined, SEGS - 1, 0)
    tail = -(-pad // 16) * 16
    span = pl.ds(rows - tail, tail)
    total = gc[span, :].astype(BF16)
    grec[span, :] = total
    both = total.astype(F32) * ext[pl.ds(pad + rows - tail, tail), :]
    both = both + ggp[span, :].astype(F32) * gpre[span, :]
    row_term[span, :] = jnp.sum(both, axis=1, keepdims=True)
    for k in range(8):
        sums[k : k + 1, :] = jnp.sum(acc[k], axis=0, keepdims=True)
    ex.settle(down_sum)
    ggp_store.wait()
    for copy in sends:
        copy.wait_send()


def recur_bwd(
    g_block, w_out, gpre, ext, conv, rate, igate, lru, pos, cw, wr, wi, vectors, down, block, ident
):
    rows, chans = conv.shape
    n, count = lax.axis_size("ch"), lax.axis_size("tok")
    width = down.shape[1] // n
    pad = 8 * (cw.shape[0] - 1)
    ex = Spread(n, rows, width)
    half = jax.ShapeDtypeStruct((rows, chans), BF16)
    sem = pltpu.SemaphoreType.DMA
    anywhere = pl.BlockSpec(memory_space=pl.ANY)
    vmem = pl.BlockSpec(memory_space=pltpu.VMEM)
    loaded = (g_block, w_out, gpre, ext, conv, rate, igate, lru, wr, wi)
    return pl.pallas_call(
        functools.partial(recur_bwd_kernel, ex),
        out_shape=[
            half, half,
            jax.ShapeDtypeStruct((count, 2 * chans // count, block), F32),
            jax.ShapeDtypeStruct((8, chans), F32),
            jax.ShapeDtypeStruct((rows, 1), F32),
            jax.ShapeDtypeStruct((rows, width), F32),
        ],
        in_specs=[anywhere] * 8 + [vmem] * 2 + [anywhere] * 2 + [vmem, anywhere],
        out_specs=[vmem, anywhere] + [vmem] * 4,
        scratch_shapes=[pltpu.VMEM(array.shape, array.dtype) for array in loaded]
        + [pltpu.VMEM((rows, chans), BF16)] * 4
        + [
            pltpu.VMEM((rows, chans), F32),
            pltpu.VMEM((rows, chans), F32),
            pltpu.VMEM((rows + pad, chans), F32),
            pltpu.VMEM((count, 8, chans), F32),
            pltpu.VMEM((pad, chans), F32),
            pltpu.VMEM((pad, chans), F32),
            pltpu.VMEM((8, 8, chans), F32),
            sem((len(loaded),)), sem, sem, sem, sem((count - 1,)), sem((count - 1,)),
        ]
        + ex.scratch(),
        compiler_params=pltpu.CompilerParams(
            collective_id=ident, has_side_effects=True, vmem_limit_bytes=62 << 20
        ),
    )(g_block, w_out, gpre, ext, conv, rate, igate, lru, pos, cw, wr, wi, vectors, down)


class Exchange(Routes):
    def __init__(self, n, rows, width, chunks, gather):
        super().__init__(n, rows, width)
        self.chunks, self.gather = chunks, gather
        self.size = rows // chunks
        self.ring = min(chunks, self.bits + 2)

    def scratch(self):
        n, rows, half, chunks = self.n, self.rows, self.half, self.chunks
        shapes = [
            pltpu.VMEM((2, n - 1, rows, half), BF16),
            pltpu.VMEM((2, n - 1, rows, half), BF16),
            pltpu.VMEM((len(self.keeps), self.ring * self.size, half), F32),
            pltpu.SemaphoreType.DMA((2, n, chunks)),
            pltpu.SemaphoreType.DMA((2, n, chunks)),
        ]
        if self.gather:
            shapes += [
                pltpu.VMEM((n, 2, rows, half), BF16),
                pltpu.SemaphoreType.DMA((self.bits, 2, chunks)),
                pltpu.SemaphoreType.DMA((self.bits, 2, chunks)),
                pltpu.SemaphoreType.DMA((2, n, chunks)),
                pltpu.SemaphoreType.DMA((2, n, chunks)),
            ]
        return shapes

    def bind(self, refs):
        if self.gather:
            (self.out, self.into, self.acc, self.ss, self.rs,
             self.full, self.gs, self.gr, self.fs, self.fr) = refs
        else:
            self.out, self.into, self.acc, self.ss, self.rs = refs
        self.tok, self.me = lax.axis_index("tok"), lax.axis_index("ch")

    def span(self, c):
        return pl.ds(pl.multiple_of(c * self.size, self.size), self.size)

    def acc_span(self, c):
        at = lax.rem(c, self.ring) * self.size
        return pl.ds(pl.multiple_of(at, self.size), self.size)

    def reduce_copy(self, part, mask, c):
        return pltpu.make_async_remote_copy(
            self.out.at[part, mask - 1, self.span(c)],
            self.into.at[part, mask - 1, self.span(c)],
            self.ss.at[part, mask, c],
            self.rs.at[part, mask, c],
            self.peer(self.bit_of(part, mask)),
            MESH,
        )

    def produce(self, c, block):
        span = self.span(c)
        for mask in sorted(range(self.n), key=lambda m: -m.bit_count()):
            value = block(mask)
            for part in range(2):
                piece = value[:, part * self.half : (part + 1) * self.half]
                if (part, mask) in self.keeps:
                    self.acc[self.keeps.index((part, mask)), self.acc_span(c), :] = piece
                else:
                    self.out[part, mask - 1, span, :] = piece.astype(BF16)
                    self.reduce_copy(part, mask, c).start()

    def summed(self, part, mask, c):
        span = self.span(c)
        value = self.acc[self.keeps.index((part, mask)), self.acc_span(c), :]
        for b in self.incoming(part, mask):
            came = mask | (1 << b)
            self.reduce_copy(part, came, c).wait_recv()
            value = value + self.into[part, came - 1, span, :].astype(F32)
        return value

    def pass_on(self, stage, c):
        for part in range(2):
            for mask in range(1, self.n):
                if self.stage_of(part, mask) == stage:
                    value = self.summed(part, mask, c)
                    self.out[part, mask - 1, self.span(c), :] = value.astype(BF16)
                    self.reduce_copy(part, mask, c).start()

    def close_reduce(self, c):
        for part in range(2):
            for mask in range(1, self.n):
                self.reduce_copy(part, mask, c).wait_send()

    def gather_copy(self, part, mask, b, c):
        block = self.full.at[self.me ^ mask, part, self.span(c)]
        if mask == 0:
            return pltpu.make_async_remote_copy(
                block, block, self.gs.at[b, part, c], self.gr.at[b, part, c], self.peer(b), MESH
            )
        got = mask | (1 << b)
        return pltpu.make_async_remote_copy(
            block, block, self.fs.at[part, got, c], self.fr.at[part, got, c], self.peer(b), MESH
        )

    def arrived(self, part, mask, c):
        block = self.full.at[self.me ^ mask, part, self.span(c)]
        if mask.bit_count() == 1:
            b = low_bit(mask)
            sems = (self.gs.at[b, part, c], self.gr.at[b, part, c])
        else:
            sems = (self.fs.at[part, mask, c], self.fr.at[part, mask, c])
        pltpu.make_async_remote_copy(block, block, *sems, self.peer(0), MESH).wait_recv()

    def gather_start(self, c, halves):
        for part in range(2):
            self.full[self.me, part, self.span(c), :] = halves[part].astype(BF16)
            for b in range(self.bits):
                self.gather_copy(part, 0, b, c).start()

    def nexts(self, part, mask):
        return range(high_bit(mask) + 1, self.bits) if part == 0 else range(low_bit(mask))

    def gather_pass(self, stage, c):
        for mask in [m for m in range(1, self.n) if m.bit_count() == stage]:
            for part in range(2):
                self.arrived(part, mask, c)
                for b in self.nexts(part, mask):
                    self.gather_copy(part, mask, b, c).start()

    def gather_close(self, c):
        for part in range(2):
            self.arrived(part, self.n - 1, c)
        for part in range(2):
            for b in range(self.bits):
                self.gather_copy(part, 0, b, c).wait_send()
            for mask in range(1, self.n):
                for b in self.nexts(part, mask):
                    self.gather_copy(part, mask, b, c).wait_send()

    def piece(self, owner, c):
        span = self.span(c)
        return jnp.concatenate([self.full[owner, 0, span, :], self.full[owner, 1, span, :]], axis=1)

    def own_sum(self, c):
        return [self.summed(part, 0, c) for part in range(2)]

    def run(self, stages, extra=None, after=None):
        depth = len(stages)

        def turn(t, _):
            if extra is not None:
                extra(t)
            for s in reversed(range(depth)):
                c = t - s

                @pl.when(jnp.logical_and(c >= 0, c < self.chunks))
                def _():
                    stages[s](c)

            if after is not None:
                after(t)
            return 0

        lax.fori_loop(0, self.chunks + depth - 1, turn, 0)


def own_part(gain, ex):
    return gain[:, pl.ds(pl.multiple_of(ex.me * ex.width, 128), ex.width)]


def tile_of(size):
    return next(t for t in (512, 384, 256, 128, size) if size % t == 0)


def mid_kernel(
    ex, branch, w_out, x_own, gain, wg_h, wu_h, wd_h, cot_h,
    normed_h, full_h, own_o, scale_o, hidden_h, gg_h, gu_h,
    wg, wu, wd, cot, normed, hidden, gg, gu, wsem, csem, osem, fsem, *refs,
):
    ex.bind(refs)
    n, width = ex.n, ex.width
    units = wg.shape[1]
    tile = tile_of(units)
    greet(ex.neighbours())
    loads = [
        pltpu.make_async_copy(a, b, wsem.at[i])
        for i, (a, b) in enumerate(((wg_h, wg), (wu_h, wu), (wd_h, wd)))
    ]
    for load in loads:
        load.start()

    def cot_load(c):
        return pltpu.make_async_copy(cot_h.at[ex.span(c)], cot, csem)

    outs = ((normed, normed_h), (hidden, hidden_h), (gg, gg_h), (gu, gu_h))

    def store(i, c):
        source, target = outs[i]
        return pltpu.make_async_copy(source, target.at[ex.span(c)], osem.at[i])

    def full_store(c):
        span = ex.span(c)
        return pltpu.make_async_copy(
            ex.full.at[:, :, span], full_h.at[:, :, span], fsem.at[c]
        )

    cot_load(0).start()

    def first(c):
        rows = branch[ex.span(c), :]

        def block(mask):
            at = pl.multiple_of((ex.me ^ mask) * width, 128)
            return jnp.dot(rows, w_out[:, pl.ds(at, width)], preferred_element_type=F32)

        ex.produce(c, block)

    def own(c):
        span = ex.span(c)
        value = jnp.concatenate(ex.own_sum(c), axis=1) + x_own[span, :].astype(F32)
        own_o[span, :] = value
        ex.gather_start(c, [value[:, : ex.half], value[:, ex.half :]])
        ex.close_reduce(c)

    def final(c):
        ex.gather_close(c)
        full_store(c).start()

        @pl.when(c > 0)
        def _():
            store(0, c - 1).wait()

        def norm_rows(at):
            span = pl.ds(pl.multiple_of(c * ex.size + at, 16), 16)
            pieces = [
                ex.full[d, part, span, :].astype(F32) for d in range(n) for part in range(2)
            ]
            total = sum(jnp.sum(p * p, axis=1, keepdims=True) for p in pieces)
            scale = lax.rsqrt(total * (1.0 / (n * width)) + 1e-06)
            scale_o[span, :] = scale
            for i, p in enumerate(pieces):
                columns = slice(i * ex.half, (i + 1) * ex.half)
                normed[pl.ds(at, 16), columns] = (p * scale * gain[:, columns]).astype(BF16)

        over_rows(0, ex.size, 16, norm_rows)
        store(0, c).start()

    def feed(c):
        @pl.when(c == 0)
        def _():
            for load in loads:
                load.wait()

        cot_load(c).wait()

        @pl.when(c > 0)
        def _():
            for i in range(1, 4):
                store(i, c - 1).wait()

        for j in range(units // tile):
            columns = slice(j * tile, (j + 1) * tile)
            act, slope = gelu_parts(
                jnp.dot(normed[...], wg[:, columns], preferred_element_type=F32)
            )
            up = jnp.dot(normed[...], wu[:, columns], preferred_element_type=F32)
            grad = nt_dot(cot[...], wd[columns, :])
            hidden[:, columns] = (act * up).astype(BF16)
            gg[:, columns] = (grad * up * slope).astype(BF16)
            gu[:, columns] = (grad * act).astype(BF16)

        @pl.when(c + 1 < ex.chunks)
        def _():
            cot_load(c + 1).start()

        for i in range(1, 4):
            store(i, c).start()

    stages = [first]
    stages += [functools.partial(ex.pass_on, s) for s in range(1, ex.bits)]
    stages += [own]
    stages += [functools.partial(ex.gather_pass, s) for s in range(1, ex.bits)]
    stages += [final]
    depth = len(stages)

    def after(t):
        c = t - (depth - 1)

        @pl.when(c >= 0)
        def _():
            feed(c)

    ex.run(stages, after=after)
    for i in range(4):
        store(i, ex.chunks - 1).wait()
    for c in range(ex.chunks):
        full_store(c).wait()


def mid_exchange(branch, w_out, x_own, gain, w_gate, w_up, w_down, cot, ident, chunks=4):
    n = lax.axis_size("ch")
    rows, width = x_own.shape
    units = w_gate.shape[1]
    ex = Exchange(n, rows, width, chunks, True)
    whole = jax.ShapeDtypeStruct((rows, n * width), BF16)
    inner = jax.ShapeDtypeStruct((rows, units), BF16)
    wide, narrow = pltpu.VMEM((ex.size, n * width), BF16), pltpu.VMEM((ex.size, units), BF16)
    sem = pltpu.SemaphoreType.DMA
    anywhere = pl.BlockSpec(memory_space=pl.ANY)
    vmem = pl.BlockSpec(memory_space=pltpu.VMEM)
    return pl.pallas_call(
        functools.partial(mid_kernel, ex),
        out_shape=[
            whole,
            jax.ShapeDtypeStruct((n, 2, rows, ex.half), BF16),
            jax.ShapeDtypeStruct((rows, width), F32),
            jax.ShapeDtypeStruct((rows, 1), F32),
            inner, inner, inner,
        ],
        in_specs=[vmem] * 4 + [anywhere] * 4,
        out_specs=[anywhere, anywhere, vmem, vmem] + [anywhere] * 3,
        scratch_shapes=[
            pltpu.VMEM(w_gate.shape, BF16),
            pltpu.VMEM(w_up.shape, BF16),
            pltpu.VMEM(w_down.shape, BF16),
            wide, wide, narrow, narrow, narrow,
            sem((3,)), sem, sem((4,)), sem((chunks,)),
        ]
        + ex.scratch(),
        compiler_params=pltpu.CompilerParams(
            collective_id=ident, has_side_effects=True, vmem_limit_bytes=62 << 20
        ),
    )(branch, w_out, x_own, gain, w_gate, w_up, w_down, cot)


class Halving:
    def __init__(self, count, rows, columns):
        self.count, self.chips = count, count // 2
        self.bits = self.chips.bit_length() - 1
        self.rows, self.columns = rows // count, columns

    def scratch(self):
        block = (self.rows, self.columns)
        sem = pltpu.SemaphoreType.DMA
        steps = max(self.bits, 1)
        return [
            pltpu.VMEM((self.chips, *block), BF16),
            pltpu.VMEM((self.chips, *block), BF16),
            pltpu.VMEM((max(self.chips - 1, 1), *block), BF16),
            sem((self.chips,)), sem((self.chips,)), sem((self.chips,)),
            sem((max(self.chips - 1, 1),)), sem((max(self.chips - 1, 1),)),
        ]

    def bind(self, refs, source):
        (self.home, self.pair, self.into, self.ls, self.ps, self.pr, self.ss, self.rs) = refs
        self.source = source
        self.tok, self.ch = lax.axis_index("tok"), lax.axis_index("ch")
        self.place, self.core = self.tok // 2, self.tok % 2

    def targets(self):
        found = [(self.tok + 1 - 2 * self.core, self.ch)]
        for step in range(self.bits):
            bit = (self.place // (1 << step)) % 2
            found.append((self.tok + (2 << step) * (1 - 2 * bit), self.ch))
        return found

    def rows_of(self, block):
        return self.source.at[pl.ds(pl.multiple_of(block * self.rows, self.rows), self.rows)]

    def chip_at(self, i):
        return self.place + sum(
            (1 << b) * (1 - 2 * ((self.place // (1 << b)) % 2)) for b in range(self.bits) if i >> b & 1
        )

    def load(self, i):
        return pltpu.make_async_copy(
            self.rows_of(2 * self.chip_at(i) + self.core), self.home.at[i], self.ls.at[i]
        )

    def pair_copy(self, i):
        away = self.rows_of(2 * self.chip_at(i) + 1 - self.core)
        return pltpu.make_async_remote_copy(
            away, self.pair.at[i], self.ps.at[i], self.pr.at[i], self.targets()[0], MESH
        )

    def sent_at(self, step):
        return [i for i in range(1, self.chips) if low_bit(i) == step]

    def hop(self, i):
        return pltpu.make_async_remote_copy(
            self.home.at[i], self.into.at[i - 1], self.ss.at[i - 1], self.rs.at[i - 1],
            self.targets()[1 + low_bit(i)], MESH,
        )

    def launch(self):
        for i in reversed(range(self.chips)):
            self.pair_copy(i).start()
        for i in reversed(range(self.chips)):
            self.load(i).start()

    def add(self, i, came):
        def rows(at):
            span = pl.ds(pl.multiple_of(at, 16), 16)
            total = self.home[i, span, :].astype(F32)
            for ref, j in came:
                total = total + ref[j, span, :].astype(F32)
            self.home[i, span, :] = total.astype(BF16)

        over_rows(0, self.rows, 16, rows, 2)

    def join(self):
        for i in sorted(range(self.chips), key=lambda i: i % 2 == 0):
            self.load(i).wait()
            self.pair_copy(i).wait_recv()
            self.add(i, [(self.pair, i)])
            if i in self.sent_at(0):
                self.hop(i).start()

    def step(self, step):
        for i in self.sent_at(step):
            came = [i | (1 << b) for b in range(step)]
            for j in came:
                self.hop(j).wait_recv()
            self.add(i, [(self.into, j - 1) for j in came])
            self.hop(i).start()

    def settle(self, result):
        came = [1 << b for b in range(self.bits)]
        for j in came:
            self.hop(j).wait_recv()

        def rows(at):
            span = pl.ds(pl.multiple_of(at, 16), 16)
            total = self.home[0, span, :].astype(F32)
            for j in came:
                total = total + self.into[j - 1, span, :].astype(F32)
            result[span, :] = total

        over_rows(0, self.rows, 16, rows, 2)
        for i in range(self.chips):
            self.pair_copy(i).wait_send()
        for i in range(1, self.chips):
            self.hop(i).wait_send()


def back_kernel(
    ex, half, gg_h, gu_h, wg_h, wu_h, full_h, mid_own, cot_h, cot_own, scale, gain, source,
    block_o, own_o, gain_o, sum_o,
    gg, gu, w_gate, w_up, full, cot, gsem, wsem, fsem, *refs,
):
    held = len(half.scratch())
    half.bind(refs[:held], source)
    ex.bind(refs[held:])
    n, width = ex.n, ex.width
    order = sorted(range(n), key=lambda m: -m.bit_count())

    def rows_load(c):
        span = pl.ds(c * ex.size, ex.size)
        return [
            pltpu.make_async_copy(gg_h.at[span], gg.at[span], gsem.at[0, c]),
            pltpu.make_async_copy(gu_h.at[span], gu.at[span], gsem.at[1, c]),
        ]

    def weight_load(mask):
        at = pl.ds(pl.multiple_of((ex.me ^ mask) * width, 128), width)
        return [
            pltpu.make_async_copy(wg_h.at[at], w_gate.at[at], wsem.at[0, mask]),
            pltpu.make_async_copy(wu_h.at[at], w_up.at[at], wsem.at[1, mask]),
        ]

    def final_load(c):
        span = ex.span(c)
        return [
            pltpu.make_async_copy(full_h.at[:, :, span], full, fsem.at[0]),
            pltpu.make_async_copy(cot_h.at[span], cot, fsem.at[1]),
        ]

    for copy in rows_load(0):
        copy.start()
    for mask in order:
        for copy in weight_load(mask):
            copy.start()
    for c in range(1, ex.chunks):
        for copy in rows_load(c):
            copy.start()
    for copy in final_load(0):
        copy.start()
    greet(ex.neighbours() + half.targets())
    half.launch()
    gain_o[...] = jnp.zeros_like(gain_o)

    def first(c):
        span = ex.span(c)
        for copy in rows_load(c):
            copy.wait()
        left, right = gg[span, :], gu[span, :]

        def block(mask):
            @pl.when(c == 0)
            def _():
                for copy in weight_load(mask):
                    copy.wait()

            at = pl.ds(pl.multiple_of((ex.me ^ mask) * width, 128), width)
            return nt_dot(left, w_gate[at, :]) + nt_dot(right, w_up[at, :])

        ex.produce(c, block)

    def own(c):
        span = ex.span(c)
        s = scale[span, :]
        grad = jnp.concatenate(ex.own_sum(c), axis=1)
        value = cot_own[span, :].astype(F32) + grad * own_part(gain, ex) * s
        own_o[span, :] = value
        ex.gather_start(c, [value[:, : ex.half], value[:, ex.half :]])
        ex.close_reduce(c)
        product = grad * mid_own[span, :] * s
        gain_o[...] += jnp.sum(product.reshape(-1, 8, width), axis=0)

    def final(c):
        ex.gather_close(c)
        for copy in final_load(c):
            copy.wait()

        def rows(at):
            here = pl.ds(pl.multiple_of(at, 16), 16)
            span = pl.ds(pl.multiple_of(c * ex.size + at, 16), 16)
            s = scale[span, :]
            pieces = [(d, part) for d in range(n) for part in range(2)]
            values = [ex.full[d, part, span, :].astype(F32) for d, part in pieces]
            mids = [full[d, part, here, :].astype(F32) for d, part in pieces]
            total = jnp.zeros((16, 1), F32)
            for i, (value, middle) in enumerate(zip(values, mids, strict=True)):
                columns = slice(i * ex.half, (i + 1) * ex.half)
                delta = value - cot[here, columns].astype(F32)
                total = total + jnp.sum(delta * middle, axis=1, keepdims=True)
            factor = s * s * total * (1.0 / (n * width))
            own_o[span, :] = own_o[span, :] - factor * mid_own[span, :]
            for i, (value, middle) in enumerate(zip(values, mids, strict=True)):
                columns = slice(i * ex.half, (i + 1) * ex.half)
                block_o[span, columns] = (value - factor * middle).astype(BF16)

        over_rows(0, ex.size, 16, rows)

        @pl.when(c + 1 < ex.chunks)
        def _():
            for copy in final_load(c + 1):
                copy.start()

    stages = [first]
    stages += [functools.partial(ex.pass_on, s) for s in range(1, ex.bits)]
    stages += [own]
    stages += [functools.partial(ex.gather_pass, s) for s in range(1, ex.bits)]
    stages += [final]
    turns = ex.chunks + len(stages) - 1
    acts = [half.join] + [functools.partial(half.step, s) for s in range(1, half.bits)]

    def after(t):
        for i, act in enumerate(acts):

            @pl.when(t == min(i * turns // len(acts) + i, turns - 1))
            def _():
                act()

    ex.run(stages, after=after)
    half.settle(sum_o)


def back_exchange(
    grad_gate, grad_up, w_gate, w_up, full, mid_own, cot, cot_own, scale, gain_own, source, ident,
    chunks=4,
):
    n, count = lax.axis_size("ch"), lax.axis_size("tok")
    rows, width = mid_own.shape
    ex = Exchange(n, rows, width, chunks, True)
    half = Halving(count, *source.shape)
    sem = pltpu.SemaphoreType.DMA
    anywhere = pl.BlockSpec(memory_space=pl.ANY)
    vmem = pl.BlockSpec(memory_space=pltpu.VMEM)
    return pl.pallas_call(
        functools.partial(back_kernel, ex, half),
        out_shape=[
            jax.ShapeDtypeStruct((rows, n * width), BF16),
            jax.ShapeDtypeStruct((rows, width), F32),
            jax.ShapeDtypeStruct((8, width), F32),
            jax.ShapeDtypeStruct((half.rows, half.columns), F32),
        ],
        in_specs=[anywhere] * 5 + [vmem, anywhere, vmem, vmem, vmem, anywhere],
        out_specs=[vmem] * 4,
        scratch_shapes=[
            pltpu.VMEM(grad_gate.shape, BF16),
            pltpu.VMEM(grad_up.shape, BF16),
            pltpu.VMEM(w_gate.shape, BF16),
            pltpu.VMEM(w_up.shape, BF16),
            pltpu.VMEM((n, 2, ex.size, ex.half), BF16),
            pltpu.VMEM((ex.size, n * width), BF16),
            sem((2, chunks)), sem((2, n)), sem((2,)),
        ]
        + half.scratch()
        + ex.scratch(),
        compiler_params=pltpu.CompilerParams(
            collective_id=ident, has_side_effects=True, vmem_limit_bytes=63 << 20
        ),
    )(grad_gate, grad_up, w_gate, w_up, full, mid_own, cot, cot_own, scale, gain_own, source)


class Line:
    def __init__(self, count, shape):
        self.count, self.shape, self.chips = count, shape, count // 2

    def scratch(self):
        blocks = (self.chips, *self.shape)
        hops = (max(self.chips - 1, 1), *self.shape)
        sems = [pltpu.SemaphoreType.DMA((self.chips,))] * 6
        return [pltpu.VMEM(blocks, BF16)] * 3 + [pltpu.VMEM(hops, BF16)] * 4 + sems

    def bind(self, refs):
        (self.pair_out, self.pair_in, self.home, self.up_out, self.up_in, self.dn_out, self.dn_in,
         self.ps, self.pr, self.us, self.ur, self.ds, self.dr) = refs
        self.tok, self.ch = lax.axis_index("tok"), lax.axis_index("ch")
        self.place, self.core = self.tok // 2, self.tok % 2

    def pair_copy(self, z):
        return pltpu.make_async_remote_copy(
            self.pair_out.at[z], self.pair_in.at[z], self.ps.at[z], self.pr.at[z],
            (self.tok + 1 - 2 * self.core, self.ch), MESH,
        )

    def away(self, z):
        return 2 * z + 1 - self.core

    def kept(self, z):
        return 2 * z + self.core

    def put_away(self, z, value):
        self.pair_out[z] = value.astype(BF16)
        self.pair_copy(z).start()

    def put_home(self, z, value):
        self.home[z] = value.astype(BF16)

    def over_rows(self, body):
        size = 32

        def one(i, _):
            body(pl.ds(i * size, size))
            return 0

        lax.fori_loop(0, self.shape[0] // size, one, 0, unroll=2)

    def join(self):
        for z in range(self.chips):
            self.pair_copy(z).wait_recv()

            def add(span, z=z):
                total = self.home[z, span, :].astype(F32) + self.pair_in[z, span, :].astype(F32)
                self.home[z, span, :] = total.astype(BF16)

            self.over_rows(add)

    def ways(self):
        last = self.chips - 1
        rising = (self.up_out, self.up_in, self.us, self.ur, self.place, 1)
        falling = (self.dn_out, self.dn_in, self.ds, self.dr, last - self.place, -1)
        return rising, falling

    def hop(self, way, far):
        out, into, ss, rs, _, sign = way
        count = self.count
        return pltpu.make_async_remote_copy(
            out.at[far - 1], into.at[far - 1], ss.at[far - 1], rs.at[far - 1],
            ((self.tok + 2 * sign + count) % count, self.ch), MESH,
        )

    def step(self, far):
        for way in self.ways():
            out, into, _, _, rank, sign = way

            @pl.when(rank + far <= self.chips - 1)
            def _():
                if far < self.chips - 1:

                    @pl.when(rank >= 1)
                    def _():
                        self.hop(way, far + 1).wait_recv()

                def add(span):
                    value = self.home[self.place + sign * far, span, :].astype(F32)
                    if far < self.chips - 1:
                        came = into[far, span, :].astype(F32)
                        value = value + jnp.where(rank >= 1, came, 0.0)
                    out[far - 1, span, :] = value.astype(BF16)

                self.over_rows(add)
                self.hop(way, far).start()

    def settle(self, result):
        if self.chips > 1:
            for way in self.ways():

                @pl.when(way[4] >= 1)
                def _():
                    self.hop(way, 1).wait_recv()

        def add(span):
            value = self.home[self.place, span, :].astype(F32)
            for way in self.ways() if self.chips > 1 else ():
                value = value + jnp.where(way[4] >= 1, way[1][0, span, :].astype(F32), 0.0)
            result[span, :] = value

        self.over_rows(add)

    def close(self):
        for z in range(self.chips):
            self.pair_copy(z).wait_send()
        for far in range(1, self.chips):
            for way in self.ways():

                @pl.when(way[4] + far <= self.chips - 1)
                def _():
                    self.hop(way, far).wait_send()


def end_kernel(
    ex, lines,
    g_rec, g_pre, wb_h, wg_h, stat, small, normed_h, branch, block_h, gate_blocks, x_own,
    scale, gain, mid_own,
    input_h, small_o, gain_o, mlp_o, taps_o, wb_o, wg_o, wo_o, gate_o,
    input_v, wide, w_branch, w_gelu, isem, lsem, stats, stat_sum, smalls, gains, gain_acc, st_s, st_r, sm_s, sm_r, gn_s, gn_r, *refs,
):
    held = len(lines[0].scratch())
    for i, line in enumerate(lines):
        line.bind(refs[i * held : (i + 1) * held])
    ex.bind(refs[len(lines) * held :])
    n, width = ex.n, ex.width
    count = lax.axis_size("tok")
    across = [(ex.tok, ex.me ^ m) for m in range(1, n)]
    block_load = pltpu.make_async_copy(block_h, wide, lsem.at[0])
    normed_load = pltpu.make_async_copy(normed_h, wide, lsem.at[1])
    loads = [
        pltpu.make_async_copy(wb_h, w_branch, lsem.at[2]),
        pltpu.make_async_copy(wg_h, w_gelu, lsem.at[3]),
    ]
    for load in [block_load, *loads]:
        load.start()
    greet(across + tok_targets())
    stats[ex.me] = stat[...]
    copies = []
    for m in range(1, n):
        copy = pltpu.make_async_remote_copy(
            stats.at[ex.me], stats.at[ex.me], st_s.at[m - 1], st_r.at[m - 1], across[m - 1], MESH
        )
        copy.start()
        copies.append(copy)

    def spread(buffer, send, recv):
        for o, target in enumerate(tok_targets()):
            copy = pltpu.make_async_remote_copy(
                buffer.at[ex.tok], buffer.at[ex.tok], send.at[o], recv.at[o], target, MESH
            )
            copy.start()
            copies.append(copy)

    def collect(buffer, send, recv):
        for o in range(count - 1):
            block = buffer.at[lax.rem(ex.tok + count - 1 - o, count)]
            pltpu.make_async_remote_copy(
                block, block, send.at[o], recv.at[o], tok_targets()[o], MESH
            ).wait_recv()

    smalls[ex.tok] = small[...]
    spread(smalls, sm_s, sm_r)
    wo_line, wb_line, wg_line, gate_line = lines

    def columns(source, block, line):
        size = source.shape[1] // count
        return source[:, pl.ds(pl.multiple_of(block * size, 128), size)]

    def fill(line, product):
        def far_side(z, _):
            line.put_away(z, product(line.away(z)))
            return 0

        def near_side(z, _):
            line.put_home(z, product(line.kept(z)))
            return 0

        lax.fori_loop(0, line.chips, far_side, 0)
        lax.fori_loop(0, line.chips, near_side, 0)

    def start(line):
        line.join()
        if line.chips > 1:
            line.step(line.chips - 1)

    fill(gate_line, lambda d: gate_blocks[d].astype(F32))
    block_load.wait()
    fill(wo_line, lambda d: tn_dot(branch[...], columns(wide, d, wo_line)))
    normed_load.start()
    start(wo_line)
    normed_load.wait()
    fill(wb_line, lambda d: tn_dot(columns(wide, d, wb_line), g_rec[...]))
    start(gate_line)
    start(wb_line)
    fill(wg_line, lambda d: tn_dot(columns(wide, d, wg_line), g_pre[...]))
    start(wg_line)
    for load in loads:
        load.wait()
    for m in range(1, n):
        block = stats.at[ex.me ^ m]
        pltpu.make_async_remote_copy(
            block, block, st_s.at[m - 1], st_r.at[m - 1], across[m - 1], MESH
        ).wait_recv()
    stat_sum[...] = jnp.sum(stats[...], axis=0)
    steps = ex.size // SEGS

    def input_store(c, part):
        source = input_v.at[pl.ds(c * steps, steps), part]
        target = input_h.at[pl.ds(part * (ex.rows // SEGS) + c * steps, steps)]
        return pltpu.make_async_copy(source, target, isem.at[part, c])

    gain_acc[...] = jnp.zeros_like(gain_acc)

    def first(c):
        span = ex.span(c)
        left, right = g_rec[span, :], g_pre[span, :]

        def block(mask):
            at = pl.ds(pl.multiple_of((ex.me ^ mask) * width, 128), width)
            return nt_dot(left, w_branch[at, :]) + nt_dot(right, w_gelu[at, :])

        ex.produce(c, block)

    def own(c):
        span = ex.span(c)
        grad = jnp.concatenate(ex.own_sum(c), axis=1)
        along = stat_sum[pl.ds(c, 1), :]
        square = (ex.size, ex.size)
        same = lax.broadcasted_iota(jnp.int32, square, 0) == lax.broadcasted_iota(
            jnp.int32, square, 1
        )
        term = jnp.sum(jnp.where(same, along, 0.0), axis=1, keepdims=True)
        s = scale[span, :]
        mine = x_own[span, :].astype(F32)
        value = (
            mid_own[span, :]
            + s * own_part(gain, ex) * grad
            - s * s * mine * (term * (1.0 / (n * width)))
        )
        input_v[pl.ds(c * steps, steps)] = eight(value)
        for part in range(SEGS):
            input_store(c, part).start()
        gain_acc[...] += jnp.sum((grad * mine * s).reshape(-1, 8, width), axis=0)
        ex.close_reduce(c)

    stages = [first]
    stages += [functools.partial(ex.pass_on, s) for s in range(1, ex.bits)]
    stages += [own]
    turns = ex.chunks + len(stages) - 1
    acts = [
        functools.partial(line.step, far)
        for far in range(wo_line.chips - 2, 0, -1)
        for line in (wo_line, gate_line, wb_line, wg_line)
    ]

    def extra(t):
        for i, act in enumerate(acts):
            when = 2 + i * (turns - 2) // max(len(acts), 1)

            @pl.when(t == when)
            def _():
                act()

    ex.run(stages, extra)
    gains[ex.tok] = jnp.broadcast_to(jnp.sum(gain_acc[...], axis=0, keepdims=True), (8, width))
    spread(gains, gn_s, gn_r)
    collect(smalls, sm_s, sm_r)
    all_small = jnp.sum(smalls[...], axis=0)
    chans = g_rec.shape[1]
    small_o[...] = all_small[:8]
    taps_o[...] = all_small[4:8, :chans]
    mlp_o[...] = all_small[8:9, :width]
    wo_line.settle(wo_o)
    gate_line.settle(gate_o)
    wb_line.settle(wb_o)
    wg_line.settle(wg_o)
    collect(gains, gn_s, gn_r)
    gain_o[...] = jnp.sum(gains[...], axis=0)[0:1]
    for c in range(ex.chunks):
        for part in range(SEGS):
            input_store(c, part).wait()
    for copy in copies:
        copy.wait_send()
    for line in lines:
        line.close()


def end_exchange(
    g_rec, g_pre, w_branch, w_gelu, stat, small, normed, branch, g_block, gate_blocks, x_own,
    scale, gain, mid_own, ident,
):
    n, count = lax.axis_size("ch"), lax.axis_size("tok")
    rows, width = x_own.shape
    chans, total = g_rec.shape[1], normed.shape[1]
    chunks = stat.shape[0]
    ex = Exchange(n, rows, width, chunks, False)
    lines = [
        Line(count, (chans, total // count)),
        Line(count, (total // count, chans)),
        Line(count, (total // count, chans)),
        Line(count, gate_blocks.shape[1:]),
    ]
    anywhere = pl.BlockSpec(memory_space=pl.ANY)
    vmem = pl.BlockSpec(memory_space=pltpu.VMEM)
    sem = pltpu.SemaphoreType.DMA
    return pl.pallas_call(
        functools.partial(end_kernel, ex, lines),
        out_shape=[
            jax.ShapeDtypeStruct((rows, width), F32),
            jax.ShapeDtypeStruct((8, small.shape[1]), F32),
            jax.ShapeDtypeStruct((1, width), F32),
            jax.ShapeDtypeStruct((1, width), F32),
            jax.ShapeDtypeStruct((4, chans), F32),
            jax.ShapeDtypeStruct(lines[1].shape, F32),
            jax.ShapeDtypeStruct(lines[2].shape, F32),
            jax.ShapeDtypeStruct(lines[0].shape, F32),
            jax.ShapeDtypeStruct(lines[3].shape, F32),
        ],
        in_specs=[anywhere if i in (2, 3, 6, 8) else vmem for i in range(14)],
        out_specs=[anywhere] + whole_vmem(8),
        scratch_shapes=[
            pltpu.VMEM((rows // SEGS, SEGS, width), F32),
            pltpu.VMEM((rows, total), BF16),
            pltpu.VMEM(w_branch.shape, BF16),
            pltpu.VMEM(w_gelu.shape, BF16),
            sem((SEGS, chunks)),
            sem((4,)),
            pltpu.VMEM((n, *stat.shape), F32),
            pltpu.VMEM(stat.shape, F32),
            pltpu.VMEM((count, *small.shape), F32),
            pltpu.VMEM((count, 8, width), F32),
            pltpu.VMEM((8, width), F32),
            sem((n - 1,)), sem((n - 1,)),
            sem((count - 1,)), sem((count - 1,)),
            sem((count - 1,)), sem((count - 1,)),
        ]
        + [shape for line in lines for shape in line.scratch()]
        + ex.scratch(),
        compiler_params=pltpu.CompilerParams(
            collective_id=ident, has_side_effects=True, vmem_limit_bytes=63 << 20
        ),
    )(g_rec, g_pre, w_branch, w_gelu, stat, small, normed, branch, g_block, gate_blocks, x_own,
      scale, gain, mid_own)


def to_major(rows):
    count, width = rows.shape
    return rows.reshape(SEGS, count // SEGS, width).swapaxes(0, 1).reshape(count, width)


def from_major(rows):
    count, width = rows.shape
    return rows.reshape(count // SEGS, SEGS, width).swapaxes(0, 1).reshape(count, width)


def rows_kernel(a, b, out):
    out[...] = jnp.dot(a[...], b[...], preferred_element_type=F32).astype(BF16)


def rows_product(a, b):
    rows, inner = a.shape
    right = b.shape[1]
    size = min(256, rows)
    return pl.pallas_call(
        rows_kernel,
        grid=(rows // size,),
        out_shape=jax.ShapeDtypeStruct((rows, right), BF16),
        in_specs=[
            pl.BlockSpec((size, inner), lambda i: (i, 0)),
            pl.BlockSpec((inner, right), lambda i: (0, 0)),
        ],
        out_specs=pl.BlockSpec((size, right), lambda i: (i, 0)),
        compiler_params=pltpu.CompilerParams(vmem_limit_bytes=62 << 20),
    )(a, b)


def weight_kernel(spans, a, *refs):
    out, at = refs[-1], 0
    for b, (first, last) in zip(refs, spans, strict=False):
        width = last - first
        out[:, at : at + width] = tn_dot(a[...], b[:, first:last]).astype(BF16)
        at += width


def weight_product(a, *parts):
    rows, left = a.shape
    spans = [span for _, span in parts]
    right = sum(last - first for first, last in spans)
    size = next(t for t in (256, 128, left) if left % t == 0)
    return pl.pallas_call(
        functools.partial(weight_kernel, spans),
        grid=(left // size,),
        out_shape=jax.ShapeDtypeStruct((left, right), BF16),
        in_specs=[pl.BlockSpec((rows, size), lambda i: (0, i))]
        + [pl.BlockSpec(b.shape, lambda i: (0, 0)) for b, _ in parts],
        out_specs=pl.BlockSpec((size, right), lambda i: (i, 0)),
        compiler_params=pltpu.CompilerParams(vmem_limit_bytes=62 << 20),
    )(a, *[b for b, _ in parts])


def tok_scatter(full, dim):
    return lax.psum_scatter(full, "tok", scatter_dimension=dim, tiled=True)


def close_kernel(
    input_in, wb_in, wg_in, wo_in, small, mlp, gain, taps, gate, wide, left, down,
    input_o, wb_o, wg_o, wo_o, gain_o, mlp_o, taps_o, convb_o, br_o, bi_o, decay_o, wr_o, wi_o,
    wgate_o, wup_o, wdown_o, sem,
):
    pairs = ((input_in, input_o), (wb_in, wb_o), (wg_in, wg_o), (wo_in, wo_o))
    copies = [pltpu.make_async_copy(a, b, sem.at[i]) for i, (a, b) in enumerate(pairs)]
    for copy in copies:
        copy.start()
    units = wgate_o.shape[1]
    cut = left.shape[1]

    def rows(at):
        span = pl.ds(at, 16)
        wgate_o[span, :] = wide[span, :units].astype(F32)
        wup_o[span, :cut] = left[span, :]
        wup_o[span, cut:] = wide[span, units:].astype(F32)

    over_rows(0, wgate_o.shape[0], 16, rows, 2)

    def tall_rows(at):
        span = pl.ds(at, 16)
        wdown_o[span, :] = down[span, :].astype(F32)

    over_rows(0, wdown_o.shape[0], 16, tall_rows, 4)
    for i, out in enumerate((decay_o, br_o, bi_o, convb_o)):
        out[...] = small[i, : out.shape[0]]
    gain_o[...] = gain[0, :]
    mlp_o[...] = mlp[0, :]
    taps_o[...] = taps[...]
    each, count = wr_o.shape[0], wr_o.shape[1]
    for half, out in enumerate((wr_o, wi_o)):
        for i in range(count):
            first = (half * count + i) * each
            out[:, i, :] = gate[first : first + each, :]
    for copy in copies:
        copy.wait()


def close(input_in, wb, wg, wo, small, mlp, gain, taps, gate, wide, left, down, chans, units, gates):
    width, block = gain.shape[1], gate.shape[1]
    each = gate.shape[0] // (2 * gates)
    anywhere = pl.BlockSpec(memory_space=pl.ANY)
    vmem = pl.BlockSpec(memory_space=pltpu.VMEM)

    def like(*shape):
        return jax.ShapeDtypeStruct(shape, F32)

    return pl.pallas_call(
        close_kernel,
        out_shape=[
            like(*input_in.shape), like(*wb.shape), like(*wg.shape), like(*wo.shape), like(width),
            like(width), like(*taps.shape), like(chans), like(chans), like(chans), like(chans),
            like(each, gates, block), like(each, gates, block), like(wide.shape[0], units),
            like(wide.shape[0], units), like(*down.shape),
        ],
        in_specs=[vmem] * 12,
        out_specs=[anywhere] * 4 + [vmem] * 12,
        scratch_shapes=[pltpu.SemaphoreType.DMA((4,))],
        compiler_params=pltpu.CompilerParams(vmem_limit_bytes=60 << 20),
    )(input_in, wb, wg, wo, small, mlp, gain, taps, gate, wide, left, down)


def local(
    layer_in,
    positions,
    norm_gain,
    w_branch,
    w_gelu,
    conv_w,
    conv_b,
    w_rgate,
    b_rgate,
    w_igate,
    b_igate,
    decay_param,
    w_out,
    mlp_gain,
    w_gate,
    w_up,
    w_down,
    cotangent,
):
    rows, width = layer_in.shape
    ch_index = lax.axis_index("ch")
    column = ch_index * width
    chans = decay_param.shape[0]
    gates, gate_width = w_rgate.shape[0], w_rgate.shape[1]
    layer_in, cotangent = to_major(layer_in), to_major(cotangent)
    pos = positions.reshape(SEGS, rows // SEGS)
    (
        normed, scale_in, gate_pre, ext, conv, rate, igate, lru, branch, cot, vectors, dense_r,
        dense_i, pos_tall,
    ) = front(
        layer_in, norm_gain[None], pos, w_branch, w_gelu, conv_w, conv_b, b_rgate, b_igate,
        decay_param, w_rgate.reshape(-1, gate_width), w_igate.reshape(-1, gate_width),
        cotangent, 0,
    )
    normed_mid, mid_full, mid_own, scale_mid, hidden, grad_gate, grad_up = mid_exchange(
        branch, w_out, layer_in, mlp_gain[None], w_gate, w_up, w_down, cot, 2
    )
    count = lax.axis_size("tok")
    total, units = cot.shape[1], hidden.shape[1]
    cut = units // 3
    wdown_full = weight_product(hidden, (cot, (0, total)))
    grad_up, wdown_full = lax.optimization_barrier((grad_up, wdown_full))
    grad_wdown = tok_scatter(wdown_full, 1)
    wup_one = weight_product(normed_mid, (grad_up, (0, cut)))
    grad_gate, wup_one = lax.optimization_barrier((grad_gate, wup_one))
    wide_full = weight_product(normed_mid, (grad_gate, (0, units)), (grad_up, (cut, units)))
    wide_sum = tok_scatter(wide_full, 0)
    hidden, wide_full = lax.optimization_barrier((hidden, wide_full))
    down = rows_product(hidden, w_down)
    grad_gate, down = lax.optimization_barrier((grad_gate, down))
    grad_block, grad_mid_own, gain_sum, wup_left = back_exchange(
        grad_gate, grad_up, w_gate, w_up, mid_full, mid_own, cot, cotangent, scale_mid,
        mlp_gain[None], wup_one, 3,
    )
    grad_rec, grad_gate_pre, gate_parts, sums, row_term, mlp_out = recur_bwd(
        grad_block, w_out, gate_pre, ext, conv, rate, igate, lru, pos_tall, conv_w, dense_r,
        dense_i, vectors, down, gate_width, 4,
    )
    layer_out = from_major((mid_own + mlp_out).astype(BF16))
    grad_rec, layer_out = lax.optimization_barrier((grad_rec, layer_out))
    stat = row_term.reshape(8, rows // 8)
    small_width = max(chans, width)
    small = jnp.concatenate(
        [
            jnp.pad(sums, ((0, 0), (0, small_width - chans))),
            jnp.pad(
                jnp.sum(gain_sum, axis=0, keepdims=True), ((0, 7), (0, small_width - width))
            ),
        ],
        axis=0,
    )
    (
        input_grad, small_sum, norm_gain_sum, mlp_gain_sum, taps_sum, grad_wbranch, grad_wgelu,
        grad_wout, gate_sum,
    ) = end_exchange(
        grad_rec, grad_gate_pre, w_branch, w_gelu, stat, small, normed, branch, grad_block,
        gate_parts, layer_in, scale_in, norm_gain[None], grad_mid_own, 5,
    )
    (
        input_grad, grad_wbranch, grad_wgelu, grad_wout, own_norm_gain, own_mlp_gain, grad_taps,
        grad_convb, grad_brate, grad_binput, grad_decay, grad_wrate, grad_winput, grad_wgate,
        grad_wup, grad_wdown,
    ) = close(
        input_grad, grad_wbranch, grad_wgelu, grad_wout, small_sum, mlp_gain_sum, norm_gain_sum,
        taps_sum, gate_sum, wide_sum, wup_left, grad_wdown, chans, units, gates,
    )
    return (
        layer_out,
        input_grad,
        own_norm_gain,
        grad_wbranch,
        grad_wgelu,
        grad_taps,
        grad_convb,
        grad_wrate.swapaxes(0, 1),
        grad_brate,
        grad_winput.swapaxes(0, 1),
        grad_binput,
        grad_decay,
        grad_wout,
        own_mlp_gain,
        grad_wgate,
        grad_wup,
        grad_wdown,
    )


def solution(mesh):
    placed = (
        P("tok", "ch"),
        P("tok"),
        P(),
        P(None, "ch"),
        P(None, "ch"),
        P(None, "ch"),
        P("ch"),
        P("ch", None, None),
        P("ch"),
        P("ch", None, None),
        P("ch"),
        P("ch"),
        P("ch", None),
        P(),
        P(None, "ch"),
        P(None, "ch"),
        P("ch", None),
        P("tok", "ch"),
    )
    return jax.shard_map(
        local,
        mesh=mesh,
        in_specs=placed,
        out_specs=(
            P("tok", "ch"),
            P("tok", "ch"),
            P("ch"),
            P("tok", "ch"),
            P("tok", "ch"),
            P(None, "ch"),
            P("ch"),
            P("ch", "tok", None),
            P("ch"),
            P("ch", "tok", None),
            P("ch"),
            P("ch"),
            P("ch", "tok"),
            P("ch"),
            P("tok", "ch"),
            P("tok", "ch"),
            P("ch", "tok"),
        ),
        check_vma=False,
    )
```

```python
import functools

import jax
import jax.numpy as jnp
from jax import lax
from jax.experimental import pallas as pl
from jax.experimental.pallas import tpu as pltpu
from jax.sharding import PartitionSpec as P

MESH = pl.DeviceIdType.MESH
F32 = jnp.float32
BF16 = jnp.bfloat16
SEGS = 8
GELU_A = 0.7978845608028654
GELU_B = 0.044715


def low_bit(mask):
    return (mask & -mask).bit_length() - 1


def high_bit(mask):
    return mask.bit_length() - 1


def gelu_parts(x):
    inner = jnp.tanh(GELU_A * (x + GELU_B * x * x * x))
    act = 0.5 * x * (1.0 + inner)
    slope = 0.5 * (1.0 + inner) + 0.5 * x * (1.0 - inner * inner) * GELU_A * (
        1.0 + 3.0 * GELU_B * x * x
    )
    return act, slope


def gelu_value(x):
    return 0.5 * x * (1.0 + jnp.tanh(GELU_A * (x + GELU_B * x * x * x)))


def minus_expm1(y, exp_y):
    series = 1.0 + y * (1.0 / 7.0)
    for k in (6, 5, 4, 3, 2):
        series = 1.0 + y * (1.0 / k) * series
    return jnp.where(y > -0.35, -y * series, 1.0 - exp_y)


def nt_dot(a, b):
    return lax.dot_general(a, b, (((1,), (1,)), ((), ())), preferred_element_type=F32)


def tn_dot(a, b):
    return lax.dot_general(a, b, (((0,), (0,)), ((), ())), preferred_element_type=F32)


def block_of(shape, axis, size):
    index = lax.broadcasted_iota(jnp.int32, shape, axis).astype(F32)
    return jnp.floor((index + 0.5) * (1.0 / size))


def tiled_ones(size, count):
    shape = (size, count * size)
    row = lax.broadcasted_iota(jnp.int32, shape, 0).astype(F32)
    column = lax.broadcasted_iota(jnp.int32, shape, 1).astype(F32)
    return (column - block_of(shape, 1, size) * size == row).astype(BF16)


def same_block(count, size):
    shape = (count * size, count * size)
    return block_of(shape, 0, size) == block_of(shape, 1, size)


def whole_vmem(count):
    return [pl.BlockSpec(memory_space=pltpu.VMEM)] * count


def greet(targets):
    barrier = pltpu.get_barrier_semaphore()
    for target in targets:
        pl.semaphore_signal(barrier, inc=1, device_id=target, device_id_type=MESH)
    pl.semaphore_wait(barrier, len(targets))


class Routes:
    def __init__(self, n, rows, width):
        self.n, self.rows, self.width = n, rows, width
        self.bits = n.bit_length() - 1
        self.half = width // 2
        self.keeps = [(part, m) for part in range(2) for m in range(n) if self.incoming(part, m)]

    def peer(self, b):
        return (self.tok, self.me ^ (1 << b))

    def neighbours(self):
        return [self.peer(b) for b in range(self.bits)]

    def bit_of(self, part, mask):
        return low_bit(mask) if part == 0 else high_bit(mask)

    def incoming(self, part, mask):
        if mask == 0:
            return list(range(self.bits)) if part == 0 else list(reversed(range(self.bits)))
        if part == 0:
            return list(range(low_bit(mask)))
        return list(reversed(range(high_bit(mask) + 1, self.bits)))

    def stage_of(self, part, mask):
        return low_bit(mask) if part == 0 else self.bits - 1 - high_bit(mask)


class Spread(Routes):
    def scratch(self):
        shape = (2, self.n, self.rows, self.half)
        keeps = (len(self.keeps), self.rows, self.half)
        return [
            pltpu.VMEM(shape, BF16),
            pltpu.VMEM(keeps, BF16),
            pltpu.SemaphoreType.DMA((2, self.n)),
            pltpu.SemaphoreType.DMA((2, self.n)),
            pltpu.SemaphoreType.DMA((len(self.keeps),)),
        ]

    def bind(self, refs, source):
        self.into, self.own, self.ss, self.rs, self.ls = refs
        self.source = source
        self.tok, self.me = lax.axis_index("tok"), lax.axis_index("ch")

    def view(self, part, mask):
        at = (self.me ^ mask) * self.width + part * self.half
        return self.source.at[:, pl.ds(pl.multiple_of(at, 128), self.half)]

    def copy(self, part, mask):
        held = (part, mask) in self.keeps
        block = self.own.at[self.keeps.index((part, mask))] if held else self.view(part, mask)
        return pltpu.make_async_remote_copy(
            block,
            self.into.at[part, mask],
            self.ss.at[part, mask],
            self.rs.at[part, mask],
            self.peer(self.bit_of(part, mask)),
            MESH,
        )

    def fetch(self, at):
        return pltpu.make_async_copy(self.view(*self.keeps[at]), self.own.at[at], self.ls.at[at])

    def launch(self):
        for part in range(2):
            for mask in range(1, self.n):
                if (part, mask) not in self.keeps:
                    self.copy(part, mask).start()
        for at in range(len(self.keeps)):
            self.fetch(at).start()

    def gather_in(self, part, mask, write):
        at = self.keeps.index((part, mask))
        self.fetch(at).wait()
        came = [mask | (1 << b) for b in self.incoming(part, mask)]
        for m in came:
            self.copy(part, m).wait_recv()

        def add(i, _):
            span = pl.ds(i * 32, 32)
            value = self.own[at, span, :].astype(F32)
            for m in came:
                value = value + self.into[part, m, span, :].astype(F32)
            write(at, span, value)
            return 0

        lax.fori_loop(0, self.rows // 32, add, 0, unroll=2)

    def relay(self, stage):
        def write(at, span, value):
            self.own[at, span, :] = value.astype(BF16)

        for part in range(2):
            for mask in range(1, self.n):
                if self.stage_of(part, mask) == stage:
                    self.gather_in(part, mask, write)
                    self.copy(part, mask).start()

    def settle(self, result):
        for part in range(2):

            def write(at, span, value, part=part):
                result[span, part * self.half : (part + 1) * self.half] = value

            self.gather_in(part, 0, write)
        for part in range(2):
            for mask in range(1, self.n):
                self.copy(part, mask).wait_send()


def tok_targets():
    count = lax.axis_size("tok")
    tok, ch = lax.axis_index("tok"), lax.axis_index("ch")
    return [(lax.rem(tok + o, count), ch) for o in range(1, count)]


def share_start(buffer, send, recv):
    tok = lax.axis_index("tok")
    copies = []
    for o, target in enumerate(tok_targets()):
        copy = pltpu.make_async_remote_copy(
            buffer.at[tok], buffer.at[tok], send.at[o], recv.at[o], target, MESH
        )
        copy.start()
        copies.append(copy)
    return copies


def share_wait(buffer, send, recv):
    tok = lax.axis_index("tok")
    count = lax.axis_size("tok")
    for o in range(count - 1):
        source = lax.rem(tok + count - 1 - o, count)
        pltpu.make_async_remote_copy(
            buffer.at[source], buffer.at[source], send.at[o], recv.at[o], tok_targets()[o], MESH
        ).wait_recv()


class Gather(Routes):
    def __init__(self, n, rows, width, chunks):
        super().__init__(n, rows, width)
        self.chunks, self.size = chunks, rows // chunks

    def scratch(self):
        sem = pltpu.SemaphoreType.DMA
        near, far = (self.bits, self.chunks), (2, self.n, self.chunks)
        return [sem(near), sem(near), sem(far), sem(far), sem]

    def bind(self, refs, x, full):
        self.gs, self.gr, self.fs, self.fr, self.here = refs
        self.x, self.full = x, full
        self.tok, self.me = lax.axis_index("tok"), lax.axis_index("ch")

    def place(self, owner, part, c):
        span = pl.ds(c * self.size, self.size)
        if part is None:
            return self.full.at[span, pl.ds(pl.multiple_of(owner * self.width, 128), self.width)]
        at = owner * self.width + part * self.half
        return self.full.at[span, pl.ds(pl.multiple_of(at, 128), self.half)]

    def near_copy(self, b, c, owner):
        return pltpu.make_async_remote_copy(
            self.x.at[pl.ds(c * self.size, self.size)],
            self.place(owner, None, c),
            self.gs.at[b, c],
            self.gr.at[b, c],
            self.peer(b),
            MESH,
        )

    def far_copy(self, part, mask, b, c):
        block, got = self.place(self.me ^ mask, part, c), mask | (1 << b)
        return pltpu.make_async_remote_copy(
            block, block, self.fs.at[part, got, c], self.fr.at[part, got, c], self.peer(b), MESH
        )

    def own_copy(self):
        at = pl.ds(pl.multiple_of(self.me * self.width, 128), self.width)
        return pltpu.make_async_copy(self.x, self.full.at[:, at], self.here)

    def launch(self, order):
        for c in order:
            for b in range(self.bits):
                self.near_copy(b, c, self.me).start()
        self.own_copy().start()

    def nexts(self, part, mask):
        return range(high_bit(mask) + 1, self.bits) if part == 0 else range(low_bit(mask))

    def far_arrived(self, part, mask, c):
        block = self.place(self.me ^ mask, part, c)
        pltpu.make_async_remote_copy(
            block, block, self.fs.at[part, mask, c], self.fr.at[part, mask, c], self.peer(0), MESH
        ).wait_recv()

    def forward(self, c):
        for count in range(1, self.bits):
            for mask in [m for m in range(1, self.n) if m.bit_count() == count]:
                if count == 1:
                    self.near_copy(low_bit(mask), c, self.me ^ mask).wait_recv()
                for part in range(2):
                    if count > 1:
                        self.far_arrived(part, mask, c)
                    for b in self.nexts(part, mask):
                        self.far_copy(part, mask, b, c).start()

    def finish(self, c):
        for part in range(2):
            self.far_arrived(part, self.n - 1, c)

    def close(self):
        for c in range(self.chunks):
            for b in range(self.bits):
                self.near_copy(b, c, self.me).wait_send()
            for mask in range(1, self.n):
                for part in range(2):
                    for b in self.nexts(part, mask):
                        self.far_copy(part, mask, b, c).wait_send()


def over_rows(start, rows, step, body, unroll=1):
    def one(i, _):
        body(pl.multiple_of(start + i * step, 8))
        return 0

    lax.fori_loop(0, rows // step, one, 0, unroll=unroll)


def eight(value):
    return value.reshape(-1, SEGS, value.shape[-1])


def with_segments(value, seg):
    return (eight(value) * seg[None]).reshape(value.shape)


def front_kernel(
    ga, late, x, gain, pos_in, wb_h, wg_h, cw, cb_in, br_in, bi_in, dp_in, gate_r, gate_i, cot_in,
    normed_h, scale, gpre_h, ext_h, conv_h, rate_h, igate_h, lru, branch, cot_full, vectors, wr, wi,
    pos, cot,
    full, normed, wb, wg, gpre, ext, conv, rate, igate, low, a_s, h_s, act_s, cot_f, carry, halo,
    ends,
    wsem, osem, halo_send, halo_recv, send, recv, *refs,
):
    held = len(ga.scratch())
    ga.bind(refs[:held], x, full)
    late.bind(refs[held:], cot, cot_full)
    cb, br, bi, sp = (vectors.at[i : i + 1] for i in range(4))
    for i, vector in enumerate((cb_in, br_in, bi_in)):
        vectors[i : i + 1, :] = vector[...].reshape(1, -1)
    minus = -dp_in[...].reshape(1, -1)
    vectors[3:4, :] = jnp.maximum(minus, 0.0) + jnp.log1p(jnp.exp(-jnp.abs(minus)))
    vectors[4:5, :] = jax.nn.sigmoid(minus)
    rows, chans = gpre.shape
    taps = cw.shape[0]
    pad = 8 * (taps - 1)
    tok, ch = lax.axis_index("tok"), lax.axis_index("ch")
    count = lax.axis_size("tok")
    total_width = full.shape[1]
    greet(tok_targets() + ga.neighbours())
    order = [ga.chunks - 1] + list(range(ga.chunks - 1))
    ga.launch(order)
    loads = [
        pltpu.make_async_copy(a, b, wsem.at[i])
        for i, (a, b) in enumerate(((wb_h, wb), (wg_h, wg)))
    ]
    for load in loads:
        load.start()
    blocks, block = gate_r.shape[0] // gate_r.shape[1], gate_r.shape[1]
    for source, target in ((gate_r, wr), (gate_i, wi)):
        copies = jnp.dot(source[...], tiled_ones(block, blocks), preferred_element_type=F32)
        target[...] = jnp.where(same_block(blocks, block), copies, 0.0).astype(BF16)
    length = rows // SEGS
    for s in range(SEGS):

        def lift(at, s=s):
            value = cot_in[pl.ds(s * length + at, 16), :].astype(F32)
            cot_f[pl.ds(at, 16), s, :] = value

        over_rows(0, length, 16, lift)

    def lower(at):
        value = cot_f[pl.ds(at, 2)].reshape(16, cot_f.shape[2])
        cot[pl.ds(pl.multiple_of(at * SEGS, 16), 16), :] = value.astype(BF16)

    def lower_two(i, _):
        lower(2 * i)
        return 0

    lax.fori_loop(0, length // 2, lower_two, 0, unroll=2)
    for t in range(rows // SEGS):
        pos[t * SEGS : (t + 1) * SEGS, :] = pos_in[:, t : t + 1]
    pos[rows:, :] = jnp.zeros((pos.shape[0] - rows, 1), jnp.int32)
    step = 16
    size = ga.size
    stores = []

    def store(source, target):
        copy = pltpu.make_async_copy(source, target, osem.at[len(stores)])
        copy.start()
        stores.append(copy)

    halo_copy = pltpu.make_async_remote_copy(
        ext.at[pl.ds(rows, pad)], halo, halo_send, halo_recv,
        (lax.rem(tok + 1, count), ch), MESH,
    )

    def norm_rows(at):
        span = pl.ds(at, step)
        value = full[span, :].astype(F32)
        s = lax.rsqrt(
            jnp.sum(value * value, axis=1, keepdims=True) * (1.0 / total_width) + 1e-06
        )
        scale[span, :] = s
        normed[span, :] = (value * s * gain[...]).astype(BF16)

    def enter(c):
        over_rows(c * size, size, step, norm_rows)
        span = pl.ds(c * size, size)
        ext[pl.ds(pad + c * size, size), :] = jnp.dot(
            normed[span, :], wb[...], preferred_element_type=F32
        )
        gpre[span, :] = jnp.dot(normed[span, :], wg[...], preferred_element_type=F32)

    def conv_rows(at):
        span = pl.ds(at, step)
        window = ext[pl.ds(at, step + pad), :]
        where = pos[span, :]
        value = cb[...] + cw[0:1, :] * window[pad : pad + step]
        for k in range(1, taps):
            shifted = window[pad - 8 * k : pad - 8 * k + step]
            value = value + jnp.where(where >= k, cw[k : k + 1, :] * shifted, 0.0)
        conv[span, :] = value
        low[span, :] = value.astype(BF16)

    def gate_rows(at):
        span = pl.ds(at, step)
        where = pos[span, :]
        r = jax.nn.sigmoid(rate[span, :])
        g = jax.nn.sigmoid(igate[span, :])
        rate[span, :] = r
        igate[span, :] = g
        log_decay = -8.0 * r * sp[...]
        decay = jnp.exp(log_decay)
        mult = jnp.sqrt(minus_expm1(2.0 * log_decay, decay * decay))
        mult = jnp.where(where > 0, mult, 1.0)
        a_s[span, :] = jnp.where(where > 0, decay, 0.0)
        h_s[span, :] = g * conv[span, :] * mult

    def scan_rows(c):
        def one(t, state):
            h, p = state
            span = pl.ds(pl.multiple_of(c * size + t * SEGS, SEGS), SEGS)
            a = a_s[span, :]
            h = a * h + h_s[span, :]
            p = a * p
            h_s[span, :] = h
            a_s[span, :] = p
            return h, p

        h, p = lax.fori_loop(0, size // SEGS, one, (carry[0], carry[1]), unroll=4)
        carry[0] = h
        carry[1] = p

    def recur(c):
        over_rows(c * size, size, step, conv_rows, 2)
        span = pl.ds(c * size, size)
        rate[span, :] = jnp.dot(low[span, :], wr[...], preferred_element_type=F32) + br[...]
        igate[span, :] = jnp.dot(low[span, :], wi[...], preferred_element_type=F32) + bi[...]
        over_rows(c * size, size, step, gate_rows, 2)
        scan_rows(c)

    carry[0] = jnp.zeros((SEGS, chans), F32)
    carry[1] = jnp.ones((SEGS, chans), F32)
    for i, c in enumerate(order):
        if i == 0:
            ga.forward(c)
        if i + 1 < len(order):
            ga.forward(order[i + 1])
        if i + 2 == len(order):
            late.launch(range(late.chunks))
        ga.finish(c)
        if i == 0:
            ga.own_copy().wait()
            for load in loads:
                load.wait()
        enter(c)
        if i == 0:
            halo_copy.start()
        if i == 1:
            halo_copy.wait()
            last_row = lax.broadcasted_iota(jnp.int32, (SEGS, chans), 0) == SEGS - 1
            for j in range(taps - 1):
                here = ext[pl.ds(rows + 8 * j, 8), :]
                joined = jnp.where(last_row, halo[8 * j : 8 * j + 8, :], here)
                ext[8 * j : 8 * j + 8, :] = pltpu.roll(joined, 1, 0)
        if i + 1 == len(order):
            late.forward(0)
        if i >= 1:
            recur(c)
    late.forward(1)
    store(normed, normed_h)
    store(gpre, gpre_h)
    store(ext, ext_h)
    recur(ga.chunks - 1)
    late.forward(2)
    store(conv, conv_h)
    store(rate, rate_h)
    store(igate, igate_h)
    h_end, p_end = carry[0], carry[1]
    total_h, total_p = jnp.zeros((1, chans), F32), jnp.ones((1, chans), F32)
    for s in range(SEGS):
        total_h = p_end[s : s + 1] * total_h + h_end[s : s + 1]
        total_p = p_end[s : s + 1] * total_p
    ends[tok, 0:1, :] = total_h
    ends[tok, 1:2, :] = total_p
    sends = share_start(ends, send, recv)

    def act_rows(at):
        span = pl.ds(at, step)
        act_s[span, :] = gelu_value(gpre[span, :])

    over_rows(0, rows, step, act_rows, 2)
    share_wait(ends, send, recv)
    state = jnp.zeros((1, chans), F32)
    for source in range(count - 1):
        after = ends[source, 1:2, :] * state + ends[source, 0:1, :]
        state = jnp.where(source < tok, after, state)
    for s in range(SEGS):
        lru[s : s + 1, :] = state
        state = p_end[s : s + 1] * state + h_end[s : s + 1]
    seg = lru[0:8, :]
    late.forward(3)

    def finish_rows(at):
        span = pl.ds(at, step)
        value = h_s[span, :] + with_segments(a_s[span, :], seg)
        lru[pl.ds(8 + at, step), :] = value
        branch[span, :] = (value * act_s[span, :]).astype(BF16)

    over_rows(0, rows, step, finish_rows, 2)
    for copy in sends:
        copy.wait_send()
    ga.close()
    for c in range(late.chunks):
        late.finish(c)
    late.close()
    late.own_copy().wait()
    for copy in stores:
        copy.wait()


def front(x, gain, pos, w_branch, w_gelu, cw, cb, br, bi, dp, gate_r, gate_i, cot, ident, chunks=4):
    n, count = lax.axis_size("ch"), lax.axis_size("tok")
    rows, width = x.shape
    total, chans = w_branch.shape
    taps = cw.shape[0]
    pad = 8 * (taps - 1)
    ga, late = Gather(n, rows, width, chunks), Gather(n, rows, width, 4)
    sem = pltpu.SemaphoreType.DMA
    grid = (rows, chans)
    anywhere = pl.BlockSpec(memory_space=pl.ANY)
    vmem = pl.BlockSpec(memory_space=pltpu.VMEM)
    return pl.pallas_call(
        functools.partial(front_kernel, ga, late),
        out_shape=[
            jax.ShapeDtypeStruct((rows, total), BF16),
            jax.ShapeDtypeStruct((rows, 1), F32),
            jax.ShapeDtypeStruct(grid, F32),
            jax.ShapeDtypeStruct((rows + pad, chans), F32),
            jax.ShapeDtypeStruct(grid, F32),
            jax.ShapeDtypeStruct(grid, F32),
            jax.ShapeDtypeStruct(grid, F32),
            jax.ShapeDtypeStruct((rows + 8, chans), F32),
            jax.ShapeDtypeStruct(grid, BF16),
            jax.ShapeDtypeStruct((rows, total), BF16),
            jax.ShapeDtypeStruct((8, chans), F32),
            jax.ShapeDtypeStruct((chans, chans), BF16),
            jax.ShapeDtypeStruct((chans, chans), BF16),
            jax.ShapeDtypeStruct((rows + pad, 1), jnp.int32),
            jax.ShapeDtypeStruct(x.shape, BF16),
        ],
        in_specs=[anywhere, vmem, vmem, anywhere, anywhere] + [vmem] * 8,
        out_specs=[
            anywhere, vmem, anywhere, anywhere, anywhere, anywhere, anywhere, vmem, vmem,
            anywhere, vmem, vmem, vmem, vmem, vmem,
        ],
        scratch_shapes=[
            pltpu.VMEM((rows, total), BF16),
            pltpu.VMEM((rows, total), BF16),
            pltpu.VMEM(w_branch.shape, BF16),
            pltpu.VMEM(w_gelu.shape, BF16),
            pltpu.VMEM(grid, F32),
            pltpu.VMEM((rows + pad, chans), F32),
            pltpu.VMEM(grid, F32),
            pltpu.VMEM(grid, F32),
            pltpu.VMEM(grid, F32),
            pltpu.VMEM(grid, BF16),
            pltpu.VMEM(grid, F32),
            pltpu.VMEM(grid, F32),
            pltpu.VMEM(grid, F32),
            pltpu.VMEM((rows // SEGS, SEGS, width), F32),
            pltpu.VMEM((2, SEGS, chans), F32),
            pltpu.VMEM((pad, chans), F32),
            pltpu.VMEM((count, 8, chans), F32),
            sem((2,)), sem((6,)), sem, sem, sem((count - 1,)), sem((count - 1,)),
        ]
        + ga.scratch()
        + late.scratch(),
        compiler_params=pltpu.CompilerParams(
            collective_id=ident, has_side_effects=True, vmem_limit_bytes=60 << 20
        ),
    )(x, gain, pos, w_branch, w_gelu, cw, cb, br, bi, dp, gate_r, gate_i, cot)


def recur_bwd_kernel(
    ex, line, g_block_h, w_out_h, gpre_h, ext_h, conv_h, rate_h, igate_h, lru_h, pos, cw, wr_h, wi_h, vectors,
    down, branch_h,
    grec, ggp_h, gate_o, sums, row_term, down_sum, carry_o,
    g_block, w_out, gpre, ext, conv, rate, igate, lru, wr, wi, branch,
    ggp, grate, ginput, low,
    g_s, a_s, gc, ends, edge, landed, acc, lsem, osem, edge_send, edge_recv, send, recv, *refs,
):
    held = len(line.scratch())
    line.bind(refs[:held])
    ex.bind(refs[held:], down)
    sp, sg = vectors.at[3:4], vectors.at[4:5]
    rows, chans = conv.shape
    taps = cw.shape[0]
    pad = 8 * (taps - 1)
    tok, ch = lax.axis_index("tok"), lax.axis_index("ch")
    count = lax.axis_size("tok")
    pairs = (
        (g_block_h, g_block), (w_out_h, w_out), (gpre_h, gpre), (lru_h, lru), (rate_h, rate),
        (branch_h, branch), (igate_h, igate), (conv_h, conv), (wr_h, wr), (wi_h, wi), (ext_h, ext),
    )
    loads = [pltpu.make_async_copy(a, b, lsem.at[i]) for i, (a, b) in enumerate(pairs)]
    for load in loads:
        load.start()
    greet(tok_targets() + ex.neighbours())
    ex.launch()
    step = 16
    big = min(256, rows)
    for load in loads[:5]:
        load.wait()

    def begin_rows(at):
        span = pl.ds(at, step)
        act, slope = gelu_parts(gpre[span, :])
        grad = g_s[span, :]
        g_s[span, :] = grad * act
        ggp[span, :] = (grad * lru[pl.ds(8 + at, step), :] * slope).astype(BF16)
        a_s[span, :] = jnp.where(pos[span, :] > 0, jnp.exp(-8.0 * rate[span, :] * sp[...]), 0.0)

    def begin(i, state):
        at = pl.multiple_of(rows - (i + 1) * big, 8)
        g_s[pl.ds(at, big), :] = nt_dot(g_block[pl.ds(at, big), :], w_out[...])
        over_rows(at, big, step, begin_rows, 2)

        def one(t, state):
            v, q = state
            span = pl.ds(pl.multiple_of(at + big - (t + 1) * SEGS, SEGS), SEGS)
            a = a_s[span, :]
            c = g_s[span, :] + v
            g_s[span, :] = c
            a_s[span, :] = q
            return a * c, a * q

        return lax.fori_loop(0, big // SEGS, one, state, unroll=4)

    v_end, q_end = lax.fori_loop(
        0, rows // big, begin, (jnp.zeros((SEGS, chans), F32), jnp.ones((SEGS, chans), F32))
    )
    total_v, total_q = jnp.zeros((1, chans), F32), jnp.ones((1, chans), F32)
    for s in reversed(range(SEGS)):
        total_v = q_end[s : s + 1] * total_v + v_end[s : s + 1]
        total_q = q_end[s : s + 1] * total_q
    ends[tok, 0:1, :] = total_v
    ends[tok, 1:2, :] = total_q
    ggp_store = pltpu.make_async_copy(ggp, ggp_h, osem)
    ggp_store.start()
    sends = share_start(ends, send, recv)
    loads[5].wait()
    fill(line, lambda d: tn_dot(branch[...], block_columns(g_block, d, count)))
    share_wait(ends, send, recv)
    line.join()
    if line.chips > 2:
        line.step(line.chips - 1)
    state = jnp.zeros((1, chans), F32)
    for source in reversed(range(1, count)):
        after = ends[source, 1:2, :] * state + ends[source, 0:1, :]
        state = jnp.where(source > tok, after, state)
    entering = [None] * SEGS
    for s in reversed(range(SEGS)):
        entering[s] = state
        state = q_end[s : s + 1] * state + v_end[s : s + 1]
    for s in range(SEGS):
        edge[s : s + 1, :] = entering[s]
    seg = edge[0:8, :]
    acc[...] = jnp.zeros_like(acc)
    for load in loads[6:]:
        load.wait()

    def folded(x):
        return jnp.sum(eight(x), axis=0)

    def middle_rows(at):
        span = pl.ds(at, step)
        carried = g_s[span, :] + with_segments(a_s[span, :], seg)
        before = lru[span, :]
        keep = pos[span, :] > 0
        r, g, out = rate[span, :], igate[span, :], conv[span, :]
        log_decay = -8.0 * r * sp[...]
        decay = jnp.exp(log_decay)
        square = decay * decay
        mult = jnp.where(keep, jnp.sqrt(minus_expm1(2.0 * log_decay, square)), 1.0)
        scaled = carried * g
        grad_log = jnp.where(keep, decay * carried * before - scaled * out * square / mult, 0.0)
        slope = 8.0 * r * grad_log
        grad_rate = (-slope * sp[...] * (1.0 - r)).astype(BF16)
        grad_input = (scaled * out * mult * (1.0 - g)).astype(BF16)
        grate[span, :] = grad_rate
        ginput[span, :] = grad_input
        low[span, :] = out.astype(BF16)
        gc[span, :] = scaled * mult
        acc[0] += folded(slope * sg[...])
        acc[1] += folded(grad_rate.astype(F32))
        acc[2] += folded(grad_input.astype(F32))

    def middle(i, _):
        at = pl.multiple_of(i * big, 8)
        over_rows(at, big, step, middle_rows)
        span = pl.ds(at, big)
        gc[span, :] += nt_dot(grate[span, :], wr[...]) + nt_dot(ginput[span, :], wi[...])
        return 0

    lax.fori_loop(0, rows // big, middle, 0)
    gc[pl.ds(rows, pad), :] = jnp.zeros((pad, chans), F32)
    for j in range(1, taps):
        value = jnp.zeros((8, chans), F32)
        for k in range(j, taps):
            e = 8 * (k - j)
            masked = jnp.where(pos[e : e + 8, :] >= k, gc[e : e + 8, :], 0.0)
            value = value + cw[k : k + 1, :] * masked
        edge[pad - 8 * j : pad - 8 * j + 8, :] = value
    edge_copy = pltpu.make_async_remote_copy(
        edge, landed, edge_send, edge_recv, (lax.rem(tok + count - 1, count), ch), MESH
    )
    edge_copy.start()
    for stage in range(1, ex.bits):
        ex.relay(stage)
    for far in range(line.chips - 2, 1, -1):
        line.step(far)

    block = gate_o.shape[2]
    blocks = chans // block
    each = block // count
    shape = (chans, chans)
    row = lax.broadcasted_iota(jnp.int32, shape, 0).astype(F32)
    part = block_of(shape, 0, blocks * each)
    which = block_of(shape, 0, each) - part * blocks
    within = row - block_of(shape, 0, each) * each
    wanted = which * block + part * each + within
    column = lax.broadcasted_iota(jnp.int32, shape, 1).astype(F32)
    order = (column == wanted).astype(BF16)
    same = same_block(blocks, block)
    for i, grads in enumerate((grate, ginput)):
        kept = jnp.where(same, tn_dot(low[...], grads[...]), 0.0).astype(BF16)
        folded_in = nt_dot(kept, tiled_ones(block, blocks)).astype(BF16)
        value = jnp.dot(order, folded_in, preferred_element_type=F32)
        height = blocks * each
        for d in range(count):
            gate_o[d, i * height : (i + 1) * height, :] = value[d * height : (d + 1) * height]

    def last_rows(at):
        step = 32
        span = pl.ds(at, step)
        window = gc[pl.ds(at, step + pad), :]
        where = pos[pl.ds(at, step + pad), :]
        source = ext[pl.ds(at, step + pad), :]
        here = window[:step]
        total = cw[0:1, :] * here
        acc[3] += folded(here)
        acc[4] += folded(here * source[pad : pad + step])
        for k in range(1, taps):
            masked = jnp.where(where >= k, window, 0.0)
            total = total + cw[k : k + 1, :] * masked[8 * k : 8 * k + step]
            acc[4 + k] += folded(masked[:step] * source[pad - 8 * k : pad - 8 * k + step])
        gc[span, :] = total
        grec[span, :] = total.astype(BF16)
        both = total.astype(BF16).astype(F32) * source[pad : pad + step]
        both = both + ggp[span, :].astype(F32) * gpre[span, :]
        row_term[span, :] = jnp.sum(both, axis=1, keepdims=True)

    over_rows(0, rows, 32, last_rows)
    edge_copy.wait()
    first_row = lax.broadcasted_iota(jnp.int32, (SEGS, chans), 0) == 0
    for j in range(0, pad, 8):
        joined = jnp.where(first_row, landed[j : j + 8, :], edge[j : j + 8, :])
        at = pl.ds(rows - pad + j, 8)
        gc[at, :] = gc[at, :] + pltpu.roll(joined, SEGS - 1, 0)
    tail = -(-pad // 16) * 16
    span = pl.ds(rows - tail, tail)
    total = gc[span, :].astype(BF16)
    grec[span, :] = total
    both = total.astype(F32) * ext[pl.ds(pad + rows - tail, tail), :]
    both = both + ggp[span, :].astype(F32) * gpre[span, :]
    row_term[span, :] = jnp.sum(both, axis=1, keepdims=True)
    for k in range(8):
        sums[k : k + 1, :] = jnp.sum(acc[k], axis=0, keepdims=True)
    ex.settle(down_sum)
    line.step(1, carry_o)
    carry_o[2] = line.home[line.place]
    line.close(2)
    ggp_store.wait()
    for copy in sends:
        copy.wait_send()


def recur_bwd(
    g_block, w_out, gpre, ext, conv, rate, igate, lru, pos, cw, wr, wi, vectors, down, branch, block,
    ident,
):
    rows, chans = conv.shape
    n, count = lax.axis_size("ch"), lax.axis_size("tok")
    width = down.shape[1] // n
    pad = 8 * (cw.shape[0] - 1)
    ex = Spread(n, rows, width)
    half = jax.ShapeDtypeStruct((rows, chans), BF16)
    sem = pltpu.SemaphoreType.DMA
    anywhere = pl.BlockSpec(memory_space=pl.ANY)
    vmem = pl.BlockSpec(memory_space=pltpu.VMEM)
    loaded = (g_block, w_out, gpre, ext, conv, rate, igate, lru, wr, wi, branch)
    line = Line(count, (chans, g_block.shape[1] // count))
    return pl.pallas_call(
        functools.partial(recur_bwd_kernel, ex, line),
        out_shape=[
            half, half,
            jax.ShapeDtypeStruct((count, 2 * chans // count, block), F32),
            jax.ShapeDtypeStruct((8, chans), F32),
            jax.ShapeDtypeStruct((rows, 1), F32),
            jax.ShapeDtypeStruct((rows, width), F32),
            jax.ShapeDtypeStruct((3, *line.shape), BF16),
        ],
        in_specs=[anywhere] * 8 + [vmem] * 2 + [anywhere] * 2 + [vmem, anywhere, anywhere],
        out_specs=[vmem, anywhere] + [vmem] * 5,
        scratch_shapes=[pltpu.VMEM(array.shape, array.dtype) for array in loaded]
        + [pltpu.VMEM((rows, chans), BF16)] * 4
        + [
            pltpu.VMEM((rows, chans), F32),
            pltpu.VMEM((rows, chans), F32),
            pltpu.VMEM((rows + pad, chans), F32),
            pltpu.VMEM((count, 8, chans), F32),
            pltpu.VMEM((pad, chans), F32),
            pltpu.VMEM((pad, chans), F32),
            pltpu.VMEM((8, 8, chans), F32),
            sem((len(loaded),)), sem, sem, sem, sem((count - 1,)), sem((count - 1,)),
        ]
        + line.scratch()
        + ex.scratch(),
        compiler_params=pltpu.CompilerParams(
            collective_id=ident, has_side_effects=True, vmem_limit_bytes=62 << 20
        ),
    )(g_block, w_out, gpre, ext, conv, rate, igate, lru, pos, cw, wr, wi, vectors, down,
      branch)


class Exchange(Routes):
    def __init__(self, n, rows, width, chunks, gather):
        super().__init__(n, rows, width)
        self.chunks, self.gather = chunks, gather
        self.size = rows // chunks
        self.ring = min(chunks, self.bits + 2)

    def scratch(self):
        n, rows, half, chunks = self.n, self.rows, self.half, self.chunks
        shapes = [
            pltpu.VMEM((2, n - 1, rows, half), BF16),
            pltpu.VMEM((2, n - 1, rows, half), BF16),
            pltpu.VMEM((len(self.keeps), self.ring * self.size, half), F32),
            pltpu.SemaphoreType.DMA((2, n, chunks)),
            pltpu.SemaphoreType.DMA((2, n, chunks)),
        ]
        if self.gather:
            shapes += [
                pltpu.VMEM((n, 2, rows, half), BF16),
                pltpu.SemaphoreType.DMA((self.bits, 2, chunks)),
                pltpu.SemaphoreType.DMA((self.bits, 2, chunks)),
                pltpu.SemaphoreType.DMA((2, n, chunks)),
                pltpu.SemaphoreType.DMA((2, n, chunks)),
            ]
        return shapes

    def bind(self, refs):
        if self.gather:
            (self.out, self.into, self.acc, self.ss, self.rs,
             self.full, self.gs, self.gr, self.fs, self.fr) = refs
        else:
            self.out, self.into, self.acc, self.ss, self.rs = refs
        self.tok, self.me = lax.axis_index("tok"), lax.axis_index("ch")

    def span(self, c):
        return pl.ds(pl.multiple_of(c * self.size, self.size), self.size)

    def acc_span(self, c):
        at = lax.rem(c, self.ring) * self.size
        return pl.ds(pl.multiple_of(at, self.size), self.size)

    def reduce_copy(self, part, mask, c):
        return pltpu.make_async_remote_copy(
            self.out.at[part, mask - 1, self.span(c)],
            self.into.at[part, mask - 1, self.span(c)],
            self.ss.at[part, mask, c],
            self.rs.at[part, mask, c],
            self.peer(self.bit_of(part, mask)),
            MESH,
        )

    def produce(self, c, block):
        span = self.span(c)
        for mask in sorted(range(self.n), key=lambda m: -m.bit_count()):
            value = block(mask)
            for part in range(2):
                piece = value[:, part * self.half : (part + 1) * self.half]
                if (part, mask) in self.keeps:
                    self.acc[self.keeps.index((part, mask)), self.acc_span(c), :] = piece
                else:
                    self.out[part, mask - 1, span, :] = piece.astype(BF16)
                    self.reduce_copy(part, mask, c).start()

    def summed(self, part, mask, c):
        span = self.span(c)
        value = self.acc[self.keeps.index((part, mask)), self.acc_span(c), :]
        for b in self.incoming(part, mask):
            came = mask | (1 << b)
            self.reduce_copy(part, came, c).wait_recv()
            value = value + self.into[part, came - 1, span, :].astype(F32)
        return value

    def pass_on(self, stage, c):
        for part in range(2):
            for mask in range(1, self.n):
                if self.stage_of(part, mask) == stage:
                    value = self.summed(part, mask, c)
                    self.out[part, mask - 1, self.span(c), :] = value.astype(BF16)
                    self.reduce_copy(part, mask, c).start()

    def close_reduce(self, c):
        for part in range(2):
            for mask in range(1, self.n):
                self.reduce_copy(part, mask, c).wait_send()

    def gather_copy(self, part, mask, b, c):
        block = self.full.at[self.me ^ mask, part, self.span(c)]
        if mask == 0:
            return pltpu.make_async_remote_copy(
                block, block, self.gs.at[b, part, c], self.gr.at[b, part, c], self.peer(b), MESH
            )
        got = mask | (1 << b)
        return pltpu.make_async_remote_copy(
            block, block, self.fs.at[part, got, c], self.fr.at[part, got, c], self.peer(b), MESH
        )

    def arrived(self, part, mask, c):
        block = self.full.at[self.me ^ mask, part, self.span(c)]
        if mask.bit_count() == 1:
            b = low_bit(mask)
            sems = (self.gs.at[b, part, c], self.gr.at[b, part, c])
        else:
            sems = (self.fs.at[part, mask, c], self.fr.at[part, mask, c])
        pltpu.make_async_remote_copy(block, block, *sems, self.peer(0), MESH).wait_recv()

    def gather_start(self, c, halves):
        for part in range(2):
            self.full[self.me, part, self.span(c), :] = halves[part].astype(BF16)
            for b in range(self.bits):
                self.gather_copy(part, 0, b, c).start()

    def nexts(self, part, mask):
        return range(high_bit(mask) + 1, self.bits) if part == 0 else range(low_bit(mask))

    def gather_pass(self, stage, c):
        for mask in [m for m in range(1, self.n) if m.bit_count() == stage]:
            for part in range(2):
                self.arrived(part, mask, c)
                for b in self.nexts(part, mask):
                    self.gather_copy(part, mask, b, c).start()

    def gather_close(self, c):
        for part in range(2):
            self.arrived(part, self.n - 1, c)
        for part in range(2):
            for b in range(self.bits):
                self.gather_copy(part, 0, b, c).wait_send()
            for mask in range(1, self.n):
                for b in self.nexts(part, mask):
                    self.gather_copy(part, mask, b, c).wait_send()

    def piece(self, owner, c):
        span = self.span(c)
        return jnp.concatenate([self.full[owner, 0, span, :], self.full[owner, 1, span, :]], axis=1)

    def own_sum(self, c):
        return [self.summed(part, 0, c) for part in range(2)]

    def run(self, stages, extra=None, after=None):
        depth = len(stages)

        def turn(t, _):
            if extra is not None:
                extra(t)
            for s in reversed(range(depth)):
                c = t - s

                @pl.when(jnp.logical_and(c >= 0, c < self.chunks))
                def _():
                    stages[s](c)

            if after is not None:
                after(t)
            return 0

        lax.fori_loop(0, self.chunks + depth - 1, turn, 0)


def own_part(gain, ex):
    return gain[:, pl.ds(pl.multiple_of(ex.me * ex.width, 128), ex.width)]


def tile_of(size):
    return next(t for t in (512, 384, 256, 128, size) if size % t == 0)


def mid_kernel(
    ex, branch, w_out, x_own, gain, wg_h, wu_h, wd_h, cot_h,
    normed_h, full_h, own_o, scale_o, hidden_h, gg_h, gu_h,
    wg, wu, wd, cot, normed, hidden, gg, gu, wsem, csem, osem, fsem, *refs,
):
    ex.bind(refs)
    n, width = ex.n, ex.width
    units = wg.shape[1]
    tile = tile_of(units)
    greet(ex.neighbours())
    loads = [
        pltpu.make_async_copy(a, b, wsem.at[i])
        for i, (a, b) in enumerate(((wg_h, wg), (wu_h, wu), (wd_h, wd)))
    ]
    for load in loads:
        load.start()

    def cot_load(c):
        return pltpu.make_async_copy(cot_h.at[ex.span(c)], cot, csem)

    outs = ((normed, normed_h), (hidden, hidden_h), (gg, gg_h), (gu, gu_h))

    def store(i, c):
        source, target = outs[i]
        return pltpu.make_async_copy(source, target.at[ex.span(c)], osem.at[i])

    def full_store(c):
        span = ex.span(c)
        return pltpu.make_async_copy(
            ex.full.at[:, :, span], full_h.at[:, :, span], fsem.at[c]
        )

    cot_load(0).start()

    def first(c):
        rows = branch[ex.span(c), :]

        def block(mask):
            at = pl.multiple_of((ex.me ^ mask) * width, 128)
            return jnp.dot(rows, w_out[:, pl.ds(at, width)], preferred_element_type=F32)

        ex.produce(c, block)

    def own(c):
        span = ex.span(c)
        value = jnp.concatenate(ex.own_sum(c), axis=1) + x_own[span, :].astype(F32)
        own_o[span, :] = value
        ex.gather_start(c, [value[:, : ex.half], value[:, ex.half :]])
        ex.close_reduce(c)

    def final(c):
        ex.gather_close(c)
        full_store(c).start()

        @pl.when(c > 0)
        def _():
            store(0, c - 1).wait()

        def norm_rows(at):
            span = pl.ds(pl.multiple_of(c * ex.size + at, 16), 16)
            pieces = [
                ex.full[d, part, span, :].astype(F32) for d in range(n) for part in range(2)
            ]
            total = sum(jnp.sum(p * p, axis=1, keepdims=True) for p in pieces)
            scale = lax.rsqrt(total * (1.0 / (n * width)) + 1e-06)
            scale_o[span, :] = scale
            for i, p in enumerate(pieces):
                columns = slice(i * ex.half, (i + 1) * ex.half)
                normed[pl.ds(at, 16), columns] = (p * scale * gain[:, columns]).astype(BF16)

        over_rows(0, ex.size, 16, norm_rows)
        store(0, c).start()

    def feed(c):
        @pl.when(c == 0)
        def _():
            for load in loads:
                load.wait()

        cot_load(c).wait()

        @pl.when(c > 0)
        def _():
            for i in range(1, 4):
                store(i, c - 1).wait()

        for j in range(units // tile):
            columns = slice(j * tile, (j + 1) * tile)
            act, slope = gelu_parts(
                jnp.dot(normed[...], wg[:, columns], preferred_element_type=F32)
            )
            up = jnp.dot(normed[...], wu[:, columns], preferred_element_type=F32)
            grad = nt_dot(cot[...], wd[columns, :])
            hidden[:, columns] = (act * up).astype(BF16)
            gg[:, columns] = (grad * up * slope).astype(BF16)
            gu[:, columns] = (grad * act).astype(BF16)

        @pl.when(c + 1 < ex.chunks)
        def _():
            cot_load(c + 1).start()

        for i in range(1, 4):
            store(i, c).start()

    stages = [first]
    stages += [functools.partial(ex.pass_on, s) for s in range(1, ex.bits)]
    stages += [own]
    stages += [functools.partial(ex.gather_pass, s) for s in range(1, ex.bits)]
    stages += [final]
    depth = len(stages)

    def after(t):
        c = t - (depth - 1)

        @pl.when(c >= 0)
        def _():
            feed(c)

    ex.run(stages, after=after)
    for i in range(4):
        store(i, ex.chunks - 1).wait()
    for c in range(ex.chunks):
        full_store(c).wait()


def mid_exchange(branch, w_out, x_own, gain, w_gate, w_up, w_down, cot, ident, chunks=4):
    n = lax.axis_size("ch")
    rows, width = x_own.shape
    units = w_gate.shape[1]
    ex = Exchange(n, rows, width, chunks, True)
    whole = jax.ShapeDtypeStruct((rows, n * width), BF16)
    inner = jax.ShapeDtypeStruct((rows, units), BF16)
    wide, narrow = pltpu.VMEM((ex.size, n * width), BF16), pltpu.VMEM((ex.size, units), BF16)
    sem = pltpu.SemaphoreType.DMA
    anywhere = pl.BlockSpec(memory_space=pl.ANY)
    vmem = pl.BlockSpec(memory_space=pltpu.VMEM)
    return pl.pallas_call(
        functools.partial(mid_kernel, ex),
        out_shape=[
            whole,
            jax.ShapeDtypeStruct((n, 2, rows, ex.half), BF16),
            jax.ShapeDtypeStruct((rows, width), F32),
            jax.ShapeDtypeStruct((rows, 1), F32),
            inner, inner, inner,
        ],
        in_specs=[vmem] * 4 + [anywhere] * 4,
        out_specs=[anywhere, anywhere, vmem, vmem] + [anywhere] * 3,
        scratch_shapes=[
            pltpu.VMEM(w_gate.shape, BF16),
            pltpu.VMEM(w_up.shape, BF16),
            pltpu.VMEM(w_down.shape, BF16),
            wide, wide, narrow, narrow, narrow,
            sem((3,)), sem, sem((4,)), sem((chunks,)),
        ]
        + ex.scratch(),
        compiler_params=pltpu.CompilerParams(
            collective_id=ident, has_side_effects=True, vmem_limit_bytes=62 << 20
        ),
    )(branch, w_out, x_own, gain, w_gate, w_up, w_down, cot)


class Halving:
    def __init__(self, count, rows, columns):
        self.count, self.chips = count, count // 2
        self.bits = self.chips.bit_length() - 1
        self.rows, self.columns = rows // count, columns

    def scratch(self):
        block = (self.rows, self.columns)
        sem = pltpu.SemaphoreType.DMA
        steps = max(self.bits, 1)
        return [
            pltpu.VMEM((self.chips, *block), BF16),
            pltpu.VMEM((self.chips, *block), BF16),
            pltpu.VMEM((max(self.chips - 1, 1), *block), BF16),
            sem((self.chips,)), sem((self.chips,)), sem((self.chips,)),
            sem((max(self.chips - 1, 1),)), sem((max(self.chips - 1, 1),)),
        ]

    def bind(self, refs, source):
        (self.home, self.pair, self.into, self.ls, self.ps, self.pr, self.ss, self.rs) = refs
        self.source = source
        self.tok, self.ch = lax.axis_index("tok"), lax.axis_index("ch")
        self.place, self.core = self.tok // 2, self.tok % 2

    def targets(self):
        found = [(self.tok + 1 - 2 * self.core, self.ch)]
        for step in range(self.bits):
            bit = (self.place // (1 << step)) % 2
            found.append((self.tok + (2 << step) * (1 - 2 * bit), self.ch))
        return found

    def rows_of(self, block):
        return self.source.at[pl.ds(pl.multiple_of(block * self.rows, self.rows), self.rows)]

    def chip_at(self, i):
        return self.place + sum(
            (1 << b) * (1 - 2 * ((self.place // (1 << b)) % 2)) for b in range(self.bits) if i >> b & 1
        )

    def load(self, i):
        return pltpu.make_async_copy(
            self.rows_of(2 * self.chip_at(i) + self.core), self.home.at[i], self.ls.at[i]
        )

    def pair_copy(self, i):
        away = self.rows_of(2 * self.chip_at(i) + 1 - self.core)
        return pltpu.make_async_remote_copy(
            away, self.pair.at[i], self.ps.at[i], self.pr.at[i], self.targets()[0], MESH
        )

    def sent_at(self, step):
        return [i for i in range(1, self.chips) if low_bit(i) == step]

    def hop(self, i):
        return pltpu.make_async_remote_copy(
            self.home.at[i], self.into.at[i - 1], self.ss.at[i - 1], self.rs.at[i - 1],
            self.targets()[1 + low_bit(i)], MESH,
        )

    def launch(self):
        for i in reversed(range(self.chips)):
            self.pair_copy(i).start()
        for i in reversed(range(self.chips)):
            self.load(i).start()

    def add(self, i, came):
        def rows(at):
            span = pl.ds(pl.multiple_of(at, 16), 16)
            total = self.home[i, span, :].astype(F32)
            for ref, j in came:
                total = total + ref[j, span, :].astype(F32)
            self.home[i, span, :] = total.astype(BF16)

        over_rows(0, self.rows, 16, rows, 2)

    def join(self):
        for i in sorted(range(self.chips), key=lambda i: i % 2 == 0):
            self.load(i).wait()
            self.pair_copy(i).wait_recv()
            self.add(i, [(self.pair, i)])
            if i in self.sent_at(0):
                self.hop(i).start()

    def step(self, step):
        for i in self.sent_at(step):
            came = [i | (1 << b) for b in range(step)]
            for j in came:
                self.hop(j).wait_recv()
            self.add(i, [(self.into, j - 1) for j in came])
            self.hop(i).start()

    def settle(self, result):
        came = [1 << b for b in range(self.bits)]
        for j in came:
            self.hop(j).wait_recv()

        def rows(at):
            span = pl.ds(pl.multiple_of(at, 16), 16)
            total = self.home[0, span, :].astype(F32)
            for j in came:
                total = total + self.into[j - 1, span, :].astype(F32)
            result[span, :] = total

        over_rows(0, self.rows, 16, rows, 2)
        for i in range(self.chips):
            self.pair_copy(i).wait_send()
        for i in range(1, self.chips):
            self.hop(i).wait_send()


def back_kernel(
    ex, half, gg_h, gu_h, wg_h, wu_h, full_h, mid_own, cot_h, cot_own, scale, gain, source,
    block_o, own_o, gain_o, sum_o,
    gg, gu, w_gate, w_up, full, cot, gsem, wsem, fsem, *refs,
):
    held = len(half.scratch())
    half.bind(refs[:held], source)
    ex.bind(refs[held:])
    n, width = ex.n, ex.width
    order = sorted(range(n), key=lambda m: -m.bit_count())

    def rows_load(c):
        span = pl.ds(c * ex.size, ex.size)
        return [
            pltpu.make_async_copy(gg_h.at[span], gg.at[span], gsem.at[0, c]),
            pltpu.make_async_copy(gu_h.at[span], gu.at[span], gsem.at[1, c]),
        ]

    def weight_load(mask):
        at = pl.ds(pl.multiple_of((ex.me ^ mask) * width, 128), width)
        return [
            pltpu.make_async_copy(wg_h.at[at], w_gate.at[at], wsem.at[0, mask]),
            pltpu.make_async_copy(wu_h.at[at], w_up.at[at], wsem.at[1, mask]),
        ]

    def final_load(c):
        span = ex.span(c)
        return [
            pltpu.make_async_copy(full_h.at[:, :, span], full, fsem.at[0]),
            pltpu.make_async_copy(cot_h.at[span], cot, fsem.at[1]),
        ]

    for copy in rows_load(0):
        copy.start()
    for mask in order:
        for copy in weight_load(mask):
            copy.start()
    for c in range(1, ex.chunks):
        for copy in rows_load(c):
            copy.start()
    for copy in final_load(0):
        copy.start()
    greet(ex.neighbours() + half.targets())
    half.launch()
    gain_o[...] = jnp.zeros_like(gain_o)

    def first(c):
        span = ex.span(c)
        for copy in rows_load(c):
            copy.wait()
        left, right = gg[span, :], gu[span, :]

        def block(mask):
            @pl.when(c == 0)
            def _():
                for copy in weight_load(mask):
                    copy.wait()

            at = pl.ds(pl.multiple_of((ex.me ^ mask) * width, 128), width)
            return nt_dot(left, w_gate[at, :]) + nt_dot(right, w_up[at, :])

        ex.produce(c, block)

    def own(c):
        span = ex.span(c)
        s = scale[span, :]
        grad = jnp.concatenate(ex.own_sum(c), axis=1)
        value = cot_own[span, :].astype(F32) + grad * own_part(gain, ex) * s
        own_o[span, :] = value
        ex.gather_start(c, [value[:, : ex.half], value[:, ex.half :]])
        ex.close_reduce(c)
        product = grad * mid_own[span, :] * s
        gain_o[...] += jnp.sum(product.reshape(-1, 8, width), axis=0)

    def final(c):
        ex.gather_close(c)
        for copy in final_load(c):
            copy.wait()

        def rows(at):
            here = pl.ds(pl.multiple_of(at, 16), 16)
            span = pl.ds(pl.multiple_of(c * ex.size + at, 16), 16)
            s = scale[span, :]
            pieces = [(d, part) for d in range(n) for part in range(2)]
            values = [ex.full[d, part, span, :].astype(F32) for d, part in pieces]
            mids = [full[d, part, here, :].astype(F32) for d, part in pieces]
            total = jnp.zeros((16, 1), F32)
            for i, (value, middle) in enumerate(zip(values, mids, strict=True)):
                columns = slice(i * ex.half, (i + 1) * ex.half)
                delta = value - cot[here, columns].astype(F32)
                total = total + jnp.sum(delta * middle, axis=1, keepdims=True)
            factor = s * s * total * (1.0 / (n * width))
            own_o[span, :] = own_o[span, :] - factor * mid_own[span, :]
            for i, (value, middle) in enumerate(zip(values, mids, strict=True)):
                columns = slice(i * ex.half, (i + 1) * ex.half)
                block_o[span, columns] = (value - factor * middle).astype(BF16)

        over_rows(0, ex.size, 16, rows)

        @pl.when(c + 1 < ex.chunks)
        def _():
            for copy in final_load(c + 1):
                copy.start()

    stages = [first]
    stages += [functools.partial(ex.pass_on, s) for s in range(1, ex.bits)]
    stages += [own]
    stages += [functools.partial(ex.gather_pass, s) for s in range(1, ex.bits)]
    stages += [final]
    turns = ex.chunks + len(stages) - 1
    acts = [half.join] + [functools.partial(half.step, s) for s in range(1, half.bits)]

    def after(t):
        for i, act in enumerate(acts):

            @pl.when(t == min(i * turns // len(acts) + i, turns - 1))
            def _():
                act()

    ex.run(stages, after=after)
    half.settle(sum_o)


def back_exchange(
    grad_gate, grad_up, w_gate, w_up, full, mid_own, cot, cot_own, scale, gain_own, source, ident,
    chunks=4,
):
    n, count = lax.axis_size("ch"), lax.axis_size("tok")
    rows, width = mid_own.shape
    ex = Exchange(n, rows, width, chunks, True)
    half = Halving(count, *source.shape)
    sem = pltpu.SemaphoreType.DMA
    anywhere = pl.BlockSpec(memory_space=pl.ANY)
    vmem = pl.BlockSpec(memory_space=pltpu.VMEM)
    return pl.pallas_call(
        functools.partial(back_kernel, ex, half),
        out_shape=[
            jax.ShapeDtypeStruct((rows, n * width), BF16),
            jax.ShapeDtypeStruct((rows, width), F32),
            jax.ShapeDtypeStruct((8, width), F32),
            jax.ShapeDtypeStruct((half.rows, half.columns), F32),
        ],
        in_specs=[anywhere] * 5 + [vmem, anywhere, vmem, vmem, vmem, anywhere],
        out_specs=[vmem] * 4,
        scratch_shapes=[
            pltpu.VMEM(grad_gate.shape, BF16),
            pltpu.VMEM(grad_up.shape, BF16),
            pltpu.VMEM(w_gate.shape, BF16),
            pltpu.VMEM(w_up.shape, BF16),
            pltpu.VMEM((n, 2, ex.size, ex.half), BF16),
            pltpu.VMEM((ex.size, n * width), BF16),
            sem((2, chunks)), sem((2, n)), sem((2,)),
        ]
        + half.scratch()
        + ex.scratch(),
        compiler_params=pltpu.CompilerParams(
            collective_id=ident, has_side_effects=True, vmem_limit_bytes=63 << 20
        ),
    )(grad_gate, grad_up, w_gate, w_up, full, mid_own, cot, cot_own, scale, gain_own, source)


class Line:
    def __init__(self, count, shape):
        self.count, self.shape, self.chips = count, shape, count // 2

    def scratch(self):
        blocks = (self.chips, *self.shape)
        hops = (max(self.chips - 1, 1), *self.shape)
        sems = [pltpu.SemaphoreType.DMA((self.chips,))] * 6
        return [pltpu.VMEM(blocks, BF16)] * 3 + [pltpu.VMEM(hops, BF16)] * 4 + sems

    def bind(self, refs):
        (self.pair_out, self.pair_in, self.home, self.up_out, self.up_in, self.dn_out, self.dn_in,
         self.ps, self.pr, self.us, self.ur, self.ds, self.dr) = refs
        self.tok, self.ch = lax.axis_index("tok"), lax.axis_index("ch")
        self.place, self.core = self.tok // 2, self.tok % 2

    def pair_copy(self, z):
        return pltpu.make_async_remote_copy(
            self.pair_out.at[z], self.pair_in.at[z], self.ps.at[z], self.pr.at[z],
            (self.tok + 1 - 2 * self.core, self.ch), MESH,
        )

    def away(self, z):
        return 2 * z + 1 - self.core

    def kept(self, z):
        return 2 * z + self.core

    def put_away(self, z, value):
        self.pair_out[z] = value.astype(BF16)
        self.pair_copy(z).start()

    def put_home(self, z, value):
        self.home[z] = value.astype(BF16)

    def over_rows(self, body):
        size = 32

        def one(i, _):
            body(pl.ds(i * size, size))
            return 0

        lax.fori_loop(0, self.shape[0] // size, one, 0, unroll=2)

    def join(self):
        for z in range(self.chips):
            self.pair_copy(z).wait_recv()

            def add(span, z=z):
                total = self.home[z, span, :].astype(F32) + self.pair_in[z, span, :].astype(F32)
                self.home[z, span, :] = total.astype(BF16)

            self.over_rows(add)

    def ways(self):
        last = self.chips - 1
        rising = (self.up_out, self.up_in, self.us, self.ur, self.place, 1)
        falling = (self.dn_out, self.dn_in, self.ds, self.dr, last - self.place, -1)
        return rising, falling

    def hop(self, way, far):
        out, into, ss, rs, _, sign = way
        count = self.count
        return pltpu.make_async_remote_copy(
            out.at[far - 1], into.at[far - 1], ss.at[far - 1], rs.at[far - 1],
            ((self.tok + 2 * sign + count) % count, self.ch), MESH,
        )

    def step(self, far, kept=None):
        for way in self.ways():
            out, into, _, _, rank, sign = way

            @pl.when(rank + far <= self.chips - 1)
            def _():
                if far < self.chips - 1:

                    @pl.when(rank >= 1)
                    def _():
                        self.hop(way, far + 1).wait_recv()

                def add(span):
                    value = self.home[self.place + sign * far, span, :].astype(F32)
                    if far < self.chips - 1:
                        came = into[far, span, :].astype(F32)
                        value = value + jnp.where(rank >= 1, came, 0.0)
                    out[far - 1, span, :] = value.astype(BF16)

                self.over_rows(add)
                if kept is None:
                    self.hop(way, far).start()
                else:
                    kept[(1 - sign) // 2] = out[far - 1]

    def settle(self, result):
        if self.chips > 1:
            for way in self.ways():

                @pl.when(way[4] >= 1)
                def _():
                    self.hop(way, 1).wait_recv()

        def add(span):
            value = self.home[self.place, span, :].astype(F32)
            for way in self.ways() if self.chips > 1 else ():
                value = value + jnp.where(way[4] >= 1, way[1][0, span, :].astype(F32), 0.0)
            result[span, :] = value

        self.over_rows(add)

    def close(self, least=1):
        for z in range(self.chips):
            self.pair_copy(z).wait_send()
        for far in range(least, self.chips):
            for way in self.ways():

                @pl.when(way[4] + far <= self.chips - 1)
                def _():
                    self.hop(way, far).wait_send()


class LastHop:
    def __init__(self, count, shape):
        self.count, self.chips, self.shape = count, count // 2, shape

    def scratch(self):
        sem = pltpu.SemaphoreType.DMA((2,))
        return [pltpu.VMEM((2, *self.shape), BF16), sem, sem]

    def bind(self, refs, carry):
        self.into, self.ss, self.rs = refs
        self.carry = carry
        self.tok, self.ch = lax.axis_index("tok"), lax.axis_index("ch")
        place = self.tok // 2
        self.ranks = (place, self.chips - 1 - place)

    def hop(self, way):
        target = (self.tok + 2 - 4 * way + self.count) % self.count
        return pltpu.make_async_remote_copy(
            self.carry.at[way], self.into.at[way], self.ss.at[way], self.rs.at[way],
            (target, self.ch), MESH,
        )

    def launch(self):
        for way in range(2):

            @pl.when(self.ranks[1 - way] >= 1)
            def _():
                self.hop(way).start()

    def settle(self, result):
        for way in range(2):

            @pl.when(self.ranks[way] >= 1)
            def _():
                self.hop(way).wait_recv()

        def rows(at):
            span = pl.ds(pl.multiple_of(at, 16), 16)
            total = self.carry[2, span, :].astype(F32)
            for way in range(2):
                came = self.into[way, span, :].astype(F32)
                total = total + jnp.where(self.ranks[way] >= 1, came, 0.0)
            result[span, :] = total

        over_rows(0, self.shape[0], 16, rows, 2)
        for way in range(2):

            @pl.when(self.ranks[1 - way] >= 1)
            def _():
                self.hop(way).wait_send()


def block_columns(source, block, count):
    size = source.shape[1] // count
    return source[:, pl.ds(pl.multiple_of(block * size, 128), size)]


def fill(line, product):
    def far_side(z, _):
        line.put_away(z, product(line.away(z)))
        return 0

    def near_side(z, _):
        line.put_home(z, product(line.kept(z)))
        return 0

    lax.fori_loop(0, line.chips, far_side, 0)
    lax.fori_loop(0, line.chips, near_side, 0)


def end_kernel(
    ex, last, lines,
    g_rec, g_pre, wb_h, wg_h, stat, small, normed_h, carry, gate_blocks, x_own,
    scale, gain, mid_own,
    input_h, small_o, gain_o, mlp_o, taps_o, wb_o, wg_o, wo_o, gate_o,
    input_v, wide, w_branch, w_gelu, isem, lsem, stats, stat_sum, smalls, gains, gain_acc, st_s, st_r, sm_s, sm_r, gn_s, gn_r, *refs,
):
    held = len(lines[0].scratch())
    for i, line in enumerate(lines):
        line.bind(refs[i * held : (i + 1) * held])
    ahead = len(lines) * held
    last.bind(refs[ahead : ahead + 3], carry)
    ex.bind(refs[ahead + 3 :])
    n, width = ex.n, ex.width
    count = lax.axis_size("tok")
    across = [(ex.tok, ex.me ^ m) for m in range(1, n)]
    normed_load = pltpu.make_async_copy(normed_h, wide, lsem.at[0])
    loads = [
        pltpu.make_async_copy(wb_h, w_branch, lsem.at[1]),
        pltpu.make_async_copy(wg_h, w_gelu, lsem.at[2]),
    ]
    for load in [normed_load, *loads]:
        load.start()
    greet(across + tok_targets())
    last.launch()
    stats[ex.me] = stat[...]
    copies = []
    for m in range(1, n):
        copy = pltpu.make_async_remote_copy(
            stats.at[ex.me], stats.at[ex.me], st_s.at[m - 1], st_r.at[m - 1], across[m - 1], MESH
        )
        copy.start()
        copies.append(copy)

    def spread(buffer, send, recv):
        for o, target in enumerate(tok_targets()):
            copy = pltpu.make_async_remote_copy(
                buffer.at[ex.tok], buffer.at[ex.tok], send.at[o], recv.at[o], target, MESH
            )
            copy.start()
            copies.append(copy)

    def collect(buffer, send, recv):
        for o in range(count - 1):
            block = buffer.at[lax.rem(ex.tok + count - 1 - o, count)]
            pltpu.make_async_remote_copy(
                block, block, send.at[o], recv.at[o], tok_targets()[o], MESH
            ).wait_recv()

    smalls[ex.tok] = small[...]
    spread(smalls, sm_s, sm_r)
    wb_line, wg_line, gate_line = lines

    def start(line):
        line.join()
        if line.chips > 1:
            line.step(line.chips - 1)

    fill(gate_line, lambda d: gate_blocks[d].astype(F32))
    normed_load.wait()
    fill(wb_line, lambda d: tn_dot(block_columns(wide, d, count), g_rec[...]))
    start(gate_line)
    start(wb_line)
    fill(wg_line, lambda d: tn_dot(block_columns(wide, d, count), g_pre[...]))
    start(wg_line)
    for load in loads:
        load.wait()
    for m in range(1, n):
        block = stats.at[ex.me ^ m]
        pltpu.make_async_remote_copy(
            block, block, st_s.at[m - 1], st_r.at[m - 1], across[m - 1], MESH
        ).wait_recv()
    stat_sum[...] = jnp.sum(stats[...], axis=0)
    steps = ex.size // SEGS

    def input_store(c, part):
        source = input_v.at[pl.ds(c * steps, steps), part]
        target = input_h.at[pl.ds(part * (ex.rows // SEGS) + c * steps, steps)]
        return pltpu.make_async_copy(source, target, isem.at[part, c])

    gain_acc[...] = jnp.zeros_like(gain_acc)

    def first(c):
        span = ex.span(c)
        left, right = g_rec[span, :], g_pre[span, :]

        def block(mask):
            at = pl.ds(pl.multiple_of((ex.me ^ mask) * width, 128), width)
            return nt_dot(left, w_branch[at, :]) + nt_dot(right, w_gelu[at, :])

        ex.produce(c, block)

    def own(c):
        span = ex.span(c)
        grad = jnp.concatenate(ex.own_sum(c), axis=1)
        along = stat_sum[pl.ds(c, 1), :]
        square = (ex.size, ex.size)
        same = lax.broadcasted_iota(jnp.int32, square, 0) == lax.broadcasted_iota(
            jnp.int32, square, 1
        )
        term = jnp.sum(jnp.where(same, along, 0.0), axis=1, keepdims=True)
        s = scale[span, :]
        mine = x_own[span, :].astype(F32)
        value = (
            mid_own[span, :]
            + s * own_part(gain, ex) * grad
            - s * s * mine * (term * (1.0 / (n * width)))
        )
        input_v[pl.ds(c * steps, steps)] = eight(value)
        for part in range(SEGS):
            input_store(c, part).start()
        gain_acc[...] += jnp.sum((grad * mine * s).reshape(-1, 8, width), axis=0)
        ex.close_reduce(c)

    stages = [first]
    stages += [functools.partial(ex.pass_on, s) for s in range(1, ex.bits)]
    stages += [own]
    turns = ex.chunks + len(stages) - 1
    acts = [
        functools.partial(line.step, far)
        for far in range(wb_line.chips - 2, 0, -1)
        for line in (gate_line, wb_line, wg_line)
    ]

    def extra(t):
        for i, act in enumerate(acts):
            when = 2 + i * (turns - 2) // max(len(acts), 1)

            @pl.when(t == when)
            def _():
                act()

    ex.run(stages, extra)
    gains[ex.tok] = jnp.broadcast_to(jnp.sum(gain_acc[...], axis=0, keepdims=True), (8, width))
    spread(gains, gn_s, gn_r)
    collect(smalls, sm_s, sm_r)
    all_small = jnp.sum(smalls[...], axis=0)
    chans = g_rec.shape[1]
    small_o[...] = all_small[:8]
    taps_o[...] = all_small[4:8, :chans]
    mlp_o[...] = all_small[8:9, :width]
    last.settle(wo_o)
    gate_line.settle(gate_o)
    wb_line.settle(wb_o)
    wg_line.settle(wg_o)
    collect(gains, gn_s, gn_r)
    gain_o[...] = jnp.sum(gains[...], axis=0)[0:1]
    for c in range(ex.chunks):
        for part in range(SEGS):
            input_store(c, part).wait()
    for copy in copies:
        copy.wait_send()
    for line in lines:
        line.close()


def end_exchange(
    g_rec, g_pre, w_branch, w_gelu, stat, small, normed, carry, gate_blocks, x_own, scale, gain,
    mid_own, ident,
):
    n, count = lax.axis_size("ch"), lax.axis_size("tok")
    rows, width = x_own.shape
    chans, total = g_rec.shape[1], normed.shape[1]
    chunks = stat.shape[0]
    ex = Exchange(n, rows, width, chunks, False)
    lines = [
        Line(count, (total // count, chans)),
        Line(count, (total // count, chans)),
        Line(count, gate_blocks.shape[1:]),
    ]
    last = LastHop(count, carry.shape[1:])
    anywhere = pl.BlockSpec(memory_space=pl.ANY)
    vmem = pl.BlockSpec(memory_space=pltpu.VMEM)
    sem = pltpu.SemaphoreType.DMA
    return pl.pallas_call(
        functools.partial(end_kernel, ex, last, lines),
        out_shape=[
            jax.ShapeDtypeStruct((rows, width), F32),
            jax.ShapeDtypeStruct((8, small.shape[1]), F32),
            jax.ShapeDtypeStruct((1, width), F32),
            jax.ShapeDtypeStruct((1, width), F32),
            jax.ShapeDtypeStruct((4, chans), F32),
            jax.ShapeDtypeStruct(lines[0].shape, F32),
            jax.ShapeDtypeStruct(lines[1].shape, F32),
            jax.ShapeDtypeStruct(last.shape, F32),
            jax.ShapeDtypeStruct(lines[2].shape, F32),
        ],
        in_specs=[anywhere if i in (2, 3, 6) else vmem for i in range(13)],
        out_specs=[anywhere] + whole_vmem(8),
        scratch_shapes=[
            pltpu.VMEM((rows // SEGS, SEGS, width), F32),
            pltpu.VMEM((rows, total), BF16),
            pltpu.VMEM(w_branch.shape, BF16),
            pltpu.VMEM(w_gelu.shape, BF16),
            sem((SEGS, chunks)),
            sem((3,)),
            pltpu.VMEM((n, *stat.shape), F32),
            pltpu.VMEM(stat.shape, F32),
            pltpu.VMEM((count, *small.shape), F32),
            pltpu.VMEM((count, 8, width), F32),
            pltpu.VMEM((8, width), F32),
            sem((n - 1,)), sem((n - 1,)),
            sem((count - 1,)), sem((count - 1,)),
            sem((count - 1,)), sem((count - 1,)),
        ]
        + [shape for line in lines for shape in line.scratch()]
        + last.scratch()
        + ex.scratch(),
        compiler_params=pltpu.CompilerParams(
            collective_id=ident, has_side_effects=True, vmem_limit_bytes=63 << 20
        ),
    )(g_rec, g_pre, w_branch, w_gelu, stat, small, normed, carry, gate_blocks, x_own, scale, gain,
      mid_own)


def to_major(rows):
    count, width = rows.shape
    return rows.reshape(SEGS, count // SEGS, width).swapaxes(0, 1).reshape(count, width)


def from_major(rows):
    count, width = rows.shape
    return rows.reshape(count // SEGS, SEGS, width).swapaxes(0, 1).reshape(count, width)


def rows_kernel(a, b, out):
    out[...] = jnp.dot(a[...], b[...], preferred_element_type=F32).astype(BF16)


def rows_product(a, b):
    rows, inner = a.shape
    right = b.shape[1]
    size = min(256, rows)
    return pl.pallas_call(
        rows_kernel,
        grid=(rows // size,),
        out_shape=jax.ShapeDtypeStruct((rows, right), BF16),
        in_specs=[
            pl.BlockSpec((size, inner), lambda i: (i, 0)),
            pl.BlockSpec((inner, right), lambda i: (0, 0)),
        ],
        out_specs=pl.BlockSpec((size, right), lambda i: (i, 0)),
        compiler_params=pltpu.CompilerParams(vmem_limit_bytes=62 << 20),
    )(a, b)


def weight_kernel(plan, a, *refs):
    for out, parts in zip(refs[-len(plan) :], plan, strict=True):
        at = 0
        for i, first, last in parts:
            width = last - first
            out[:, at : at + width] = tn_dot(a[...], refs[i][:, first:last]).astype(BF16)
            at += width


def weight_products(a, sources, plan):
    rows, left = a.shape
    widths = [sum(last - first for _, first, last in parts) for parts in plan]
    size = next(t for t in (256, 128, left) if left % t == 0)
    return pl.pallas_call(
        functools.partial(weight_kernel, plan),
        grid=(left // size,),
        out_shape=[jax.ShapeDtypeStruct((left, width), BF16) for width in widths],
        in_specs=[pl.BlockSpec((rows, size), lambda i: (0, i))]
        + [pl.BlockSpec(b.shape, lambda i: (0, 0)) for b in sources],
        out_specs=[pl.BlockSpec((size, width), lambda i: (i, 0)) for width in widths],
        compiler_params=pltpu.CompilerParams(vmem_limit_bytes=62 << 20),
    )(a, *sources)


def tok_scatter(full, dim):
    return lax.psum_scatter(full, "tok", scatter_dimension=dim, tiled=True)


def close_kernel(
    input_in, wb_in, wg_in, wo_in, small, mlp, gain, taps, gate, wide, left, down,
    input_o, wb_o, wg_o, wo_o, gain_o, mlp_o, taps_o, convb_o, br_o, bi_o, decay_o, wr_o, wi_o,
    wgate_o, wup_o, wdown_o, sem,
):
    pairs = ((input_in, input_o), (wb_in, wb_o), (wg_in, wg_o), (wo_in, wo_o))
    copies = [pltpu.make_async_copy(a, b, sem.at[i]) for i, (a, b) in enumerate(pairs)]
    for copy in copies:
        copy.start()
    units = wgate_o.shape[1]
    cut = left.shape[1]

    def rows(at):
        span = pl.ds(at, 16)
        wgate_o[span, :] = wide[span, :units].astype(F32)
        wup_o[span, :cut] = left[span, :]
        wup_o[span, cut:] = wide[span, units:].astype(F32)

    over_rows(0, wgate_o.shape[0], 16, rows, 2)

    def tall_rows(at):
        span = pl.ds(at, 16)
        wdown_o[span, :] = down[span, :].astype(F32)

    over_rows(0, wdown_o.shape[0], 16, tall_rows, 4)
    for i, out in enumerate((decay_o, br_o, bi_o, convb_o)):
        out[...] = small[i, : out.shape[0]]
    gain_o[...] = gain[0, :]
    mlp_o[...] = mlp[0, :]
    taps_o[...] = taps[...]
    each, count = wr_o.shape[0], wr_o.shape[1]
    for half, out in enumerate((wr_o, wi_o)):
        for i in range(count):
            first = (half * count + i) * each
            out[:, i, :] = gate[first : first + each, :]
    for copy in copies:
        copy.wait()


def close(input_in, wb, wg, wo, small, mlp, gain, taps, gate, wide, left, down, chans, units, gates):
    width, block = gain.shape[1], gate.shape[1]
    each = gate.shape[0] // (2 * gates)
    anywhere = pl.BlockSpec(memory_space=pl.ANY)
    vmem = pl.BlockSpec(memory_space=pltpu.VMEM)

    def like(*shape):
        return jax.ShapeDtypeStruct(shape, F32)

    return pl.pallas_call(
        close_kernel,
        out_shape=[
            like(*input_in.shape), like(*wb.shape), like(*wg.shape), like(*wo.shape), like(width),
            like(width), like(*taps.shape), like(chans), like(chans), like(chans), like(chans),
            like(each, gates, block), like(each, gates, block), like(wide.shape[0], units),
            like(wide.shape[0], units), like(*down.shape),
        ],
        in_specs=[vmem] * 12,
        out_specs=[anywhere] * 4 + [vmem] * 12,
        scratch_shapes=[pltpu.SemaphoreType.DMA((4,))],
        compiler_params=pltpu.CompilerParams(vmem_limit_bytes=60 << 20),
    )(input_in, wb, wg, wo, small, mlp, gain, taps, gate, wide, left, down)


def local(
    layer_in,
    positions,
    norm_gain,
    w_branch,
    w_gelu,
    conv_w,
    conv_b,
    w_rgate,
    b_rgate,
    w_igate,
    b_igate,
    decay_param,
    w_out,
    mlp_gain,
    w_gate,
    w_up,
    w_down,
    cotangent,
):
    rows, width = layer_in.shape
    ch_index = lax.axis_index("ch")
    column = ch_index * width
    chans = decay_param.shape[0]
    gates, gate_width = w_rgate.shape[0], w_rgate.shape[1]
    layer_in = to_major(layer_in)
    pos = positions.reshape(SEGS, rows // SEGS)
    (
        normed, scale_in, gate_pre, ext, conv, rate, igate, lru, branch, cot, vectors, dense_r,
        dense_i, pos_tall, cotangent,
    ) = front(
        layer_in, norm_gain[None], pos, w_branch, w_gelu, conv_w, conv_b, b_rgate, b_igate,
        decay_param, w_rgate.reshape(-1, gate_width), w_igate.reshape(-1, gate_width),
        cotangent, 0,
    )
    normed_mid, mid_full, mid_own, scale_mid, hidden, grad_gate, grad_up = mid_exchange(
        branch, w_out, layer_in, mlp_gain[None], w_gate, w_up, w_down, cot, 2
    )
    count = lax.axis_size("tok")
    total, units = cot.shape[1], hidden.shape[1]
    cut = units // 2
    (wdown_full,) = weight_products(hidden, (cot,), (((0, 0, total),),))
    grad_up, wdown_full = lax.optimization_barrier((grad_up, wdown_full))
    grad_wdown = tok_scatter(wdown_full, 1)
    wide_full, wup_one = weight_products(
        normed_mid, (grad_gate, grad_up), (((0, 0, units), (1, cut, units)), ((1, 0, cut),))
    )
    wide_sum = tok_scatter(wide_full, 0)
    hidden, wide_full = lax.optimization_barrier((hidden, wide_full))
    down = rows_product(hidden, w_down)
    grad_gate, down = lax.optimization_barrier((grad_gate, down))
    grad_block, grad_mid_own, gain_sum, wup_left = back_exchange(
        grad_gate, grad_up, w_gate, w_up, mid_full, mid_own, cot, cotangent, scale_mid,
        mlp_gain[None], wup_one, 3,
    )
    grad_rec, grad_gate_pre, gate_parts, sums, row_term, mlp_out, wout_carry = recur_bwd(
        grad_block, w_out, gate_pre, ext, conv, rate, igate, lru, pos_tall, conv_w, dense_r,
        dense_i, vectors, down, branch, gate_width, 4,
    )
    layer_out = from_major((mid_own + mlp_out).astype(BF16))
    grad_rec, layer_out = lax.optimization_barrier((grad_rec, layer_out))
    stat = row_term.reshape(8, rows // 8)
    small_width = max(chans, width)
    small = jnp.concatenate(
        [
            jnp.pad(sums, ((0, 0), (0, small_width - chans))),
            jnp.pad(
                jnp.sum(gain_sum, axis=0, keepdims=True), ((0, 7), (0, small_width - width))
            ),
        ],
        axis=0,
    )
    (
        input_grad, small_sum, norm_gain_sum, mlp_gain_sum, taps_sum, grad_wbranch, grad_wgelu,
        grad_wout, gate_sum,
    ) = end_exchange(
        grad_rec, grad_gate_pre, w_branch, w_gelu, stat, small, normed, wout_carry, gate_parts,
        layer_in, scale_in, norm_gain[None], grad_mid_own, 5,
    )
    (
        input_grad, grad_wbranch, grad_wgelu, grad_wout, own_norm_gain, own_mlp_gain, grad_taps,
        grad_convb, grad_brate, grad_binput, grad_decay, grad_wrate, grad_winput, grad_wgate,
        grad_wup, grad_wdown,
    ) = close(
        input_grad, grad_wbranch, grad_wgelu, grad_wout, small_sum, mlp_gain_sum, norm_gain_sum,
        taps_sum, gate_sum, wide_sum, wup_left, grad_wdown, chans, units, gates,
    )
    return (
        layer_out,
        input_grad,
        own_norm_gain,
        grad_wbranch,
        grad_wgelu,
        grad_taps,
        grad_convb,
        grad_wrate.swapaxes(0, 1),
        grad_brate,
        grad_winput.swapaxes(0, 1),
        grad_binput,
        grad_decay,
        grad_wout,
        own_mlp_gain,
        grad_wgate,
        grad_wup,
        grad_wdown,
    )


def solution(mesh):
    placed = (
        P("tok", "ch"),
        P("tok"),
        P(),
        P(None, "ch"),
        P(None, "ch"),
        P(None, "ch"),
        P("ch"),
        P("ch", None, None),
        P("ch"),
        P("ch", None, None),
        P("ch"),
        P("ch"),
        P("ch", None),
        P(),
        P(None, "ch"),
        P(None, "ch"),
        P("ch", None),
        P("tok", "ch"),
    )
    return jax.shard_map(
        local,
        mesh=mesh,
        in_specs=placed,
        out_specs=(
            P("tok", "ch"),
            P("tok", "ch"),
            P("ch"),
            P("tok", "ch"),
            P("tok", "ch"),
            P(None, "ch"),
            P("ch"),
            P("ch", "tok", None),
            P("ch"),
            P("ch", "tok", None),
            P("ch"),
            P("ch"),
            P("ch", "tok"),
            P("ch"),
            P("tok", "ch"),
            P("tok", "ch"),
            P("ch", "tok"),
        ),
        check_vma=False,
    )
```

```python
import functools

import jax
import jax.numpy as jnp
from jax import lax
from jax.experimental import pallas as pl
from jax.experimental.pallas import tpu as pltpu
from jax.sharding import PartitionSpec as P

MESH = pl.DeviceIdType.MESH
F32 = jnp.float32
BF16 = jnp.bfloat16
SEGS = 8
GELU_A = 0.7978845608028654
GELU_B = 0.044715


def low_bit(mask):
    return (mask & -mask).bit_length() - 1


def high_bit(mask):
    return mask.bit_length() - 1


def gelu_parts(x):
    inner = jnp.tanh(GELU_A * (x + GELU_B * x * x * x))
    act = 0.5 * x * (1.0 + inner)
    slope = 0.5 * (1.0 + inner) + 0.5 * x * (1.0 - inner * inner) * GELU_A * (
        1.0 + 3.0 * GELU_B * x * x
    )
    return act, slope


def gelu_value(x):
    return 0.5 * x * (1.0 + jnp.tanh(GELU_A * (x + GELU_B * x * x * x)))


def minus_expm1(y, exp_y):
    series = 1.0 + y * (1.0 / 7.0)
    for k in (6, 5, 4, 3, 2):
        series = 1.0 + y * (1.0 / k) * series
    return jnp.where(y > -0.35, -y * series, 1.0 - exp_y)


def nt_dot(a, b):
    return lax.dot_general(a, b, (((1,), (1,)), ((), ())), preferred_element_type=F32)


def tn_dot(a, b):
    return lax.dot_general(a, b, (((0,), (0,)), ((), ())), preferred_element_type=F32)


def block_of(shape, axis, size):
    index = lax.broadcasted_iota(jnp.int32, shape, axis).astype(F32)
    return jnp.floor((index + 0.5) * (1.0 / size))


def tiled_ones(size, count):
    shape = (size, count * size)
    row = lax.broadcasted_iota(jnp.int32, shape, 0).astype(F32)
    column = lax.broadcasted_iota(jnp.int32, shape, 1).astype(F32)
    return (column - block_of(shape, 1, size) * size == row).astype(BF16)


def same_block(count, size):
    shape = (count * size, count * size)
    return block_of(shape, 0, size) == block_of(shape, 1, size)


def whole_vmem(count):
    return [pl.BlockSpec(memory_space=pltpu.VMEM)] * count


def greet(targets):
    barrier = pltpu.get_barrier_semaphore()
    for target in targets:
        pl.semaphore_signal(barrier, inc=1, device_id=target, device_id_type=MESH)
    pl.semaphore_wait(barrier, len(targets))


class Routes:
    def __init__(self, n, rows, width):
        self.n, self.rows, self.width = n, rows, width
        self.bits = n.bit_length() - 1
        self.half = width // 2
        self.keeps = [(part, m) for part in range(2) for m in range(n) if self.incoming(part, m)]

    def peer(self, b):
        return (self.tok, self.me ^ (1 << b))

    def neighbours(self):
        return [self.peer(b) for b in range(self.bits)]

    def bit_of(self, part, mask):
        return low_bit(mask) if part == 0 else high_bit(mask)

    def incoming(self, part, mask):
        if mask == 0:
            return list(range(self.bits)) if part == 0 else list(reversed(range(self.bits)))
        if part == 0:
            return list(range(low_bit(mask)))
        return list(reversed(range(high_bit(mask) + 1, self.bits)))

    def stage_of(self, part, mask):
        return low_bit(mask) if part == 0 else self.bits - 1 - high_bit(mask)


class Spread(Routes):
    def scratch(self):
        shape = (2, self.n, self.rows, self.half)
        keeps = (len(self.keeps), self.rows, self.half)
        return [
            pltpu.VMEM(shape, BF16),
            pltpu.VMEM(keeps, BF16),
            pltpu.SemaphoreType.DMA((2, self.n)),
            pltpu.SemaphoreType.DMA((2, self.n)),
            pltpu.SemaphoreType.DMA((len(self.keeps),)),
        ]

    def bind(self, refs, source):
        self.into, self.own, self.ss, self.rs, self.ls = refs
        self.source = source
        self.tok, self.me = lax.axis_index("tok"), lax.axis_index("ch")

    def view(self, part, mask):
        at = (self.me ^ mask) * self.width + part * self.half
        return self.source.at[:, pl.ds(pl.multiple_of(at, 128), self.half)]

    def copy(self, part, mask):
        held = (part, mask) in self.keeps
        block = self.own.at[self.keeps.index((part, mask))] if held else self.view(part, mask)
        return pltpu.make_async_remote_copy(
            block,
            self.into.at[part, mask],
            self.ss.at[part, mask],
            self.rs.at[part, mask],
            self.peer(self.bit_of(part, mask)),
            MESH,
        )

    def fetch(self, at):
        return pltpu.make_async_copy(self.view(*self.keeps[at]), self.own.at[at], self.ls.at[at])

    def launch(self):
        for part in range(2):
            for mask in range(1, self.n):
                if (part, mask) not in self.keeps:
                    self.copy(part, mask).start()
        for at in range(len(self.keeps)):
            self.fetch(at).start()

    def gather_in(self, part, mask, write):
        at = self.keeps.index((part, mask))
        self.fetch(at).wait()
        came = [mask | (1 << b) for b in self.incoming(part, mask)]
        for m in came:
            self.copy(part, m).wait_recv()

        def add(i, _):
            span = pl.ds(i * 32, 32)
            value = self.own[at, span, :].astype(F32)
            for m in came:
                value = value + self.into[part, m, span, :].astype(F32)
            write(at, span, value)
            return 0

        lax.fori_loop(0, self.rows // 32, add, 0, unroll=2)

    def relay(self, stage):
        def write(at, span, value):
            self.own[at, span, :] = value.astype(BF16)

        for part in range(2):
            for mask in range(1, self.n):
                if self.stage_of(part, mask) == stage:
                    self.gather_in(part, mask, write)
                    self.copy(part, mask).start()

    def settle(self, result):
        for part in range(2):

            def write(at, span, value, part=part):
                result[span, part * self.half : (part + 1) * self.half] = value

            self.gather_in(part, 0, write)
        for part in range(2):
            for mask in range(1, self.n):
                self.copy(part, mask).wait_send()


def tok_targets():
    count = lax.axis_size("tok")
    tok, ch = lax.axis_index("tok"), lax.axis_index("ch")
    return [(lax.rem(tok + o, count), ch) for o in range(1, count)]


def share_start(buffer, send, recv):
    tok = lax.axis_index("tok")
    copies = []
    for o, target in enumerate(tok_targets()):
        copy = pltpu.make_async_remote_copy(
            buffer.at[tok], buffer.at[tok], send.at[o], recv.at[o], target, MESH
        )
        copy.start()
        copies.append(copy)
    return copies


def share_wait(buffer, send, recv):
    tok = lax.axis_index("tok")
    count = lax.axis_size("tok")
    for o in range(count - 1):
        source = lax.rem(tok + count - 1 - o, count)
        pltpu.make_async_remote_copy(
            buffer.at[source], buffer.at[source], send.at[o], recv.at[o], tok_targets()[o], MESH
        ).wait_recv()


class Gather(Routes):
    def __init__(self, n, rows, width, chunks):
        super().__init__(n, rows, width)
        self.chunks, self.size = chunks, rows // chunks

    def scratch(self):
        sem = pltpu.SemaphoreType.DMA
        near, far = (self.bits, self.chunks), (2, self.n, self.chunks)
        return [sem(near), sem(near), sem(far), sem(far), sem]

    def bind(self, refs, x, full):
        self.gs, self.gr, self.fs, self.fr, self.here = refs
        self.x, self.full = x, full
        self.tok, self.me = lax.axis_index("tok"), lax.axis_index("ch")

    def place(self, owner, part, c):
        span = pl.ds(c * self.size, self.size)
        if part is None:
            return self.full.at[span, pl.ds(pl.multiple_of(owner * self.width, 128), self.width)]
        at = owner * self.width + part * self.half
        return self.full.at[span, pl.ds(pl.multiple_of(at, 128), self.half)]

    def near_copy(self, b, c, owner):
        return pltpu.make_async_remote_copy(
            self.x.at[pl.ds(c * self.size, self.size)],
            self.place(owner, None, c),
            self.gs.at[b, c],
            self.gr.at[b, c],
            self.peer(b),
            MESH,
        )

    def far_copy(self, part, mask, b, c):
        block, got = self.place(self.me ^ mask, part, c), mask | (1 << b)
        return pltpu.make_async_remote_copy(
            block, block, self.fs.at[part, got, c], self.fr.at[part, got, c], self.peer(b), MESH
        )

    def own_copy(self):
        at = pl.ds(pl.multiple_of(self.me * self.width, 128), self.width)
        return pltpu.make_async_copy(self.x, self.full.at[:, at], self.here)

    def launch(self, order):
        for c in order:
            for b in range(self.bits):
                self.near_copy(b, c, self.me).start()
        self.own_copy().start()

    def nexts(self, part, mask):
        return range(high_bit(mask) + 1, self.bits) if part == 0 else range(low_bit(mask))

    def far_arrived(self, part, mask, c):
        block = self.place(self.me ^ mask, part, c)
        pltpu.make_async_remote_copy(
            block, block, self.fs.at[part, mask, c], self.fr.at[part, mask, c], self.peer(0), MESH
        ).wait_recv()

    def forward(self, c):
        for count in range(1, self.bits):
            for mask in [m for m in range(1, self.n) if m.bit_count() == count]:
                if count == 1:
                    self.near_copy(low_bit(mask), c, self.me ^ mask).wait_recv()
                for part in range(2):
                    if count > 1:
                        self.far_arrived(part, mask, c)
                    for b in self.nexts(part, mask):
                        self.far_copy(part, mask, b, c).start()

    def finish(self, c):
        for part in range(2):
            self.far_arrived(part, self.n - 1, c)

    def close(self):
        for c in range(self.chunks):
            for b in range(self.bits):
                self.near_copy(b, c, self.me).wait_send()
            for mask in range(1, self.n):
                for part in range(2):
                    for b in self.nexts(part, mask):
                        self.far_copy(part, mask, b, c).wait_send()


def over_rows(start, rows, step, body, unroll=1):
    def one(i, _):
        body(pl.multiple_of(start + i * step, 8))
        return 0

    lax.fori_loop(0, rows // step, one, 0, unroll=unroll)


def eight(value):
    return value.reshape(-1, SEGS, value.shape[-1])


def with_segments(value, seg):
    return (eight(value) * seg[None]).reshape(value.shape)


def front_kernel(
    ga, late, x, gain, pos_in, wb_h, wg_h, cw, cb_in, br_in, bi_in, dp_in, gate_r, gate_i, cot_in,
    normed_h, scale, gpre_h, ext_h, conv_h, rate_h, igate_h, lru, branch, cot_full, vectors, wr, wi,
    pos, cot,
    full, normed, wb, wg, gpre, ext, conv, rate, igate, low, a_s, h_s, act_s, cot_f, carry, halo,
    ends,
    wsem, osem, halo_send, halo_recv, send, recv, *refs,
):
    held = len(ga.scratch())
    ga.bind(refs[:held], x, full)
    late.bind(refs[held:], cot, cot_full)
    cb, br, bi, sp = (vectors.at[i : i + 1] for i in range(4))
    for i, vector in enumerate((cb_in, br_in, bi_in)):
        vectors[i : i + 1, :] = vector[...].reshape(1, -1)
    minus = -dp_in[...].reshape(1, -1)
    vectors[3:4, :] = jnp.maximum(minus, 0.0) + jnp.log1p(jnp.exp(-jnp.abs(minus)))
    vectors[4:5, :] = jax.nn.sigmoid(minus)
    rows, chans = gpre.shape
    taps = cw.shape[0]
    pad = 8 * (taps - 1)
    tok, ch = lax.axis_index("tok"), lax.axis_index("ch")
    count = lax.axis_size("tok")
    total_width = full.shape[1]
    greet(tok_targets() + ga.neighbours())
    order = [ga.chunks - 1] + list(range(ga.chunks - 1))
    ga.launch(order)
    loads = [
        pltpu.make_async_copy(a, b, wsem.at[i])
        for i, (a, b) in enumerate(((wb_h, wb), (wg_h, wg)))
    ]
    for load in loads:
        load.start()
    blocks, block = gate_r.shape[0] // gate_r.shape[1], gate_r.shape[1]
    for source, target in ((gate_r, wr), (gate_i, wi)):
        copies = jnp.dot(source[...], tiled_ones(block, blocks), preferred_element_type=F32)
        target[...] = jnp.where(same_block(blocks, block), copies, 0.0).astype(BF16)
    length = rows // SEGS
    for s in range(SEGS):

        def lift(at, s=s):
            value = cot_in[pl.ds(s * length + at, 16), :].astype(F32)
            cot_f[pl.ds(at, 16), s, :] = value

        over_rows(0, length, 16, lift)

    def lower(at):
        value = cot_f[pl.ds(at, 2)].reshape(16, cot_f.shape[2])
        cot[pl.ds(pl.multiple_of(at * SEGS, 16), 16), :] = value.astype(BF16)

    def lower_two(i, _):
        lower(2 * i)
        return 0

    lax.fori_loop(0, length // 2, lower_two, 0, unroll=2)
    for t in range(rows // SEGS):
        pos[t * SEGS : (t + 1) * SEGS, :] = pos_in[:, t : t + 1]
    pos[rows:, :] = jnp.zeros((pos.shape[0] - rows, 1), jnp.int32)
    step = 16
    size = ga.size
    stores = []

    def store(source, target):
        copy = pltpu.make_async_copy(source, target, osem.at[len(stores)])
        copy.start()
        stores.append(copy)

    halo_copy = pltpu.make_async_remote_copy(
        ext.at[pl.ds(rows, pad)], halo, halo_send, halo_recv,
        (lax.rem(tok + 1, count), ch), MESH,
    )

    def norm_rows(at):
        span = pl.ds(at, step)
        value = full[span, :].astype(F32)
        s = lax.rsqrt(
            jnp.sum(value * value, axis=1, keepdims=True) * (1.0 / total_width) + 1e-06
        )
        scale[span, :] = s
        normed[span, :] = (value * s * gain[...]).astype(BF16)

    def enter(c):
        over_rows(c * size, size, step, norm_rows)
        span = pl.ds(c * size, size)
        ext[pl.ds(pad + c * size, size), :] = jnp.dot(
            normed[span, :], wb[...], preferred_element_type=F32
        )
        gpre[span, :] = jnp.dot(normed[span, :], wg[...], preferred_element_type=F32)

    def conv_rows(at):
        span = pl.ds(at, step)
        window = ext[pl.ds(at, step + pad), :]
        where = pos[span, :]
        value = cb[...] + cw[0:1, :] * window[pad : pad + step]
        for k in range(1, taps):
            shifted = window[pad - 8 * k : pad - 8 * k + step]
            value = value + jnp.where(where >= k, cw[k : k + 1, :] * shifted, 0.0)
        conv[span, :] = value
        low[span, :] = value.astype(BF16)

    def gate_rows(at):
        span = pl.ds(at, step)
        where = pos[span, :]
        r = jax.nn.sigmoid(rate[span, :])
        g = jax.nn.sigmoid(igate[span, :])
        rate[span, :] = r
        igate[span, :] = g
        log_decay = -8.0 * r * sp[...]
        decay = jnp.exp(log_decay)
        mult = jnp.sqrt(minus_expm1(2.0 * log_decay, decay * decay))
        mult = jnp.where(where > 0, mult, 1.0)
        a_s[span, :] = jnp.where(where > 0, decay, 0.0)
        h_s[span, :] = g * conv[span, :] * mult

    def scan_rows(c):
        def one(t, state):
            h, p = state
            span = pl.ds(pl.multiple_of(c * size + t * SEGS, SEGS), SEGS)
            a = a_s[span, :]
            h = a * h + h_s[span, :]
            p = a * p
            h_s[span, :] = h
            a_s[span, :] = p
            return h, p

        h, p = lax.fori_loop(0, size // SEGS, one, (carry[0], carry[1]), unroll=4)
        carry[0] = h
        carry[1] = p

    def recur(c):
        over_rows(c * size, size, step, conv_rows, 2)
        span = pl.ds(c * size, size)
        rate[span, :] = jnp.dot(low[span, :], wr[...], preferred_element_type=F32) + br[...]
        igate[span, :] = jnp.dot(low[span, :], wi[...], preferred_element_type=F32) + bi[...]
        over_rows(c * size, size, step, gate_rows, 2)
        scan_rows(c)

    carry[0] = jnp.zeros((SEGS, chans), F32)
    carry[1] = jnp.ones((SEGS, chans), F32)
    for i, c in enumerate(order):
        if i == 0:
            ga.forward(c)
        if i + 1 < len(order):
            ga.forward(order[i + 1])
        if i + 2 == len(order):
            late.launch(range(late.chunks))
        ga.finish(c)
        if i == 0:
            ga.own_copy().wait()
            for load in loads:
                load.wait()
        enter(c)
        if i == 0:
            halo_copy.start()
        if i == 1:
            halo_copy.wait()
            last_row = lax.broadcasted_iota(jnp.int32, (SEGS, chans), 0) == SEGS - 1
            for j in range(taps - 1):
                here = ext[pl.ds(rows + 8 * j, 8), :]
                joined = jnp.where(last_row, halo[8 * j : 8 * j + 8, :], here)
                ext[8 * j : 8 * j + 8, :] = pltpu.roll(joined, 1, 0)
        if i + 1 == len(order):
            late.forward(0)
        if i >= 1:
            recur(c)
    late.forward(1)
    store(normed, normed_h)
    store(gpre, gpre_h)
    store(ext, ext_h)
    recur(ga.chunks - 1)
    late.forward(2)
    store(conv, conv_h)
    store(rate, rate_h)
    store(igate, igate_h)
    h_end, p_end = carry[0], carry[1]
    total_h, total_p = jnp.zeros((1, chans), F32), jnp.ones((1, chans), F32)
    for s in range(SEGS):
        total_h = p_end[s : s + 1] * total_h + h_end[s : s + 1]
        total_p = p_end[s : s + 1] * total_p
    ends[tok, 0:1, :] = total_h
    ends[tok, 1:2, :] = total_p
    sends = share_start(ends, send, recv)

    def act_rows(at):
        span = pl.ds(at, step)
        act_s[span, :] = gelu_value(gpre[span, :])

    over_rows(0, rows, step, act_rows, 2)
    share_wait(ends, send, recv)
    state = jnp.zeros((1, chans), F32)
    for source in range(count - 1):
        after = ends[source, 1:2, :] * state + ends[source, 0:1, :]
        state = jnp.where(source < tok, after, state)
    for s in range(SEGS):
        lru[s : s + 1, :] = state
        state = p_end[s : s + 1] * state + h_end[s : s + 1]
    seg = lru[0:8, :]
    late.forward(3)

    def finish_rows(at):
        span = pl.ds(at, step)
        value = h_s[span, :] + with_segments(a_s[span, :], seg)
        lru[pl.ds(8 + at, step), :] = value
        branch[span, :] = (value * act_s[span, :]).astype(BF16)

    over_rows(0, rows, step, finish_rows, 2)
    for copy in sends:
        copy.wait_send()
    ga.close()
    for c in range(late.chunks):
        late.finish(c)
    late.close()
    late.own_copy().wait()
    for copy in stores:
        copy.wait()


def front(x, gain, pos, w_branch, w_gelu, cw, cb, br, bi, dp, gate_r, gate_i, cot, ident, chunks=4):
    n, count = lax.axis_size("ch"), lax.axis_size("tok")
    rows, width = x.shape
    total, chans = w_branch.shape
    taps = cw.shape[0]
    pad = 8 * (taps - 1)
    ga, late = Gather(n, rows, width, chunks), Gather(n, rows, width, 4)
    sem = pltpu.SemaphoreType.DMA
    grid = (rows, chans)
    anywhere = pl.BlockSpec(memory_space=pl.ANY)
    vmem = pl.BlockSpec(memory_space=pltpu.VMEM)
    return pl.pallas_call(
        functools.partial(front_kernel, ga, late),
        out_shape=[
            jax.ShapeDtypeStruct((rows, total), BF16),
            jax.ShapeDtypeStruct((rows, 1), F32),
            jax.ShapeDtypeStruct(grid, F32),
            jax.ShapeDtypeStruct((rows + pad, chans), F32),
            jax.ShapeDtypeStruct(grid, F32),
            jax.ShapeDtypeStruct(grid, F32),
            jax.ShapeDtypeStruct(grid, F32),
            jax.ShapeDtypeStruct((rows + 8, chans), F32),
            jax.ShapeDtypeStruct(grid, BF16),
            jax.ShapeDtypeStruct((rows, total), BF16),
            jax.ShapeDtypeStruct((8, chans), F32),
            jax.ShapeDtypeStruct((chans, chans), BF16),
            jax.ShapeDtypeStruct((chans, chans), BF16),
            jax.ShapeDtypeStruct((rows + pad, 1), jnp.int32),
            jax.ShapeDtypeStruct(x.shape, BF16),
        ],
        in_specs=[anywhere, vmem, vmem, anywhere, anywhere] + [vmem] * 8,
        out_specs=[
            anywhere, vmem, anywhere, anywhere, anywhere, anywhere, anywhere, vmem, vmem,
            anywhere, vmem, vmem, vmem, vmem, vmem,
        ],
        scratch_shapes=[
            pltpu.VMEM((rows, total), BF16),
            pltpu.VMEM((rows, total), BF16),
            pltpu.VMEM(w_branch.shape, BF16),
            pltpu.VMEM(w_gelu.shape, BF16),
            pltpu.VMEM(grid, F32),
            pltpu.VMEM((rows + pad, chans), F32),
            pltpu.VMEM(grid, F32),
            pltpu.VMEM(grid, F32),
            pltpu.VMEM(grid, F32),
            pltpu.VMEM(grid, BF16),
            pltpu.VMEM(grid, F32),
            pltpu.VMEM(grid, F32),
            pltpu.VMEM(grid, F32),
            pltpu.VMEM((rows // SEGS, SEGS, width), F32),
            pltpu.VMEM((2, SEGS, chans), F32),
            pltpu.VMEM((pad, chans), F32),
            pltpu.VMEM((count, 8, chans), F32),
            sem((2,)), sem((6,)), sem, sem, sem((count - 1,)), sem((count - 1,)),
        ]
        + ga.scratch()
        + late.scratch(),
        compiler_params=pltpu.CompilerParams(
            collective_id=ident, has_side_effects=True, vmem_limit_bytes=60 << 20
        ),
    )(x, gain, pos, w_branch, w_gelu, cw, cb, br, bi, dp, gate_r, gate_i, cot)


def recur_bwd_kernel(
    ex, line, g_block_h, w_out_h, gpre_h, ext_h, conv_h, rate_h, igate_h, lru_h, pos, cw, wr_h, wi_h, vectors,
    down, branch_h,
    grec, ggp_h, gate_o, sums, row_term, down_sum, carry_o,
    g_block, w_out, gpre, ext, conv, rate, igate, lru, wr, wi, branch,
    ggp, grate, ginput, low,
    g_s, a_s, gc, ends, edge, landed, acc, lsem, osem, edge_send, edge_recv, send, recv, *refs,
):
    held = len(line.scratch())
    line.bind(refs[:held])
    ex.bind(refs[held:], down)
    sp, sg = vectors.at[3:4], vectors.at[4:5]
    rows, chans = conv.shape
    taps = cw.shape[0]
    pad = 8 * (taps - 1)
    tok, ch = lax.axis_index("tok"), lax.axis_index("ch")
    count = lax.axis_size("tok")
    pairs = (
        (g_block_h, g_block), (w_out_h, w_out), (gpre_h, gpre), (lru_h, lru), (rate_h, rate),
        (branch_h, branch), (igate_h, igate), (conv_h, conv), (wr_h, wr), (wi_h, wi), (ext_h, ext),
    )
    loads = [pltpu.make_async_copy(a, b, lsem.at[i]) for i, (a, b) in enumerate(pairs)]
    for load in loads:
        load.start()
    greet(tok_targets() + ex.neighbours())
    ex.launch()
    step = 16
    big = min(256, rows)
    for load in loads[:5]:
        load.wait()

    def begin_rows(at):
        span = pl.ds(at, step)
        act, slope = gelu_parts(gpre[span, :])
        grad = g_s[span, :]
        g_s[span, :] = grad * act
        ggp[span, :] = (grad * lru[pl.ds(8 + at, step), :] * slope).astype(BF16)
        a_s[span, :] = jnp.where(pos[span, :] > 0, jnp.exp(-8.0 * rate[span, :] * sp[...]), 0.0)

    def begin(i, state):
        at = pl.multiple_of(rows - (i + 1) * big, 8)
        g_s[pl.ds(at, big), :] = nt_dot(g_block[pl.ds(at, big), :], w_out[...])
        over_rows(at, big, step, begin_rows, 2)

        def one(t, state):
            v, q = state
            span = pl.ds(pl.multiple_of(at + big - (t + 1) * SEGS, SEGS), SEGS)
            a = a_s[span, :]
            c = g_s[span, :] + v
            g_s[span, :] = c
            a_s[span, :] = q
            return a * c, a * q

        return lax.fori_loop(0, big // SEGS, one, state, unroll=4)

    v_end, q_end = lax.fori_loop(
        0, rows // big, begin, (jnp.zeros((SEGS, chans), F32), jnp.ones((SEGS, chans), F32))
    )
    total_v, total_q = jnp.zeros((1, chans), F32), jnp.ones((1, chans), F32)
    for s in reversed(range(SEGS)):
        total_v = q_end[s : s + 1] * total_v + v_end[s : s + 1]
        total_q = q_end[s : s + 1] * total_q
    ends[tok, 0:1, :] = total_v
    ends[tok, 1:2, :] = total_q
    ggp_store = pltpu.make_async_copy(ggp, ggp_h, osem)
    ggp_store.start()
    sends = share_start(ends, send, recv)
    loads[5].wait()
    fill(line, lambda d: tn_dot(branch[...], block_columns(g_block, d, count)))
    share_wait(ends, send, recv)
    line.join()
    if line.chips > 2:
        line.step(line.chips - 1)
    state = jnp.zeros((1, chans), F32)
    for source in reversed(range(1, count)):
        after = ends[source, 1:2, :] * state + ends[source, 0:1, :]
        state = jnp.where(source > tok, after, state)
    entering = [None] * SEGS
    for s in reversed(range(SEGS)):
        entering[s] = state
        state = q_end[s : s + 1] * state + v_end[s : s + 1]
    for s in range(SEGS):
        edge[s : s + 1, :] = entering[s]
    seg = edge[0:8, :]
    acc[...] = jnp.zeros_like(acc)
    for load in loads[6:]:
        load.wait()

    def folded(x):
        return jnp.sum(eight(x), axis=0)

    def middle_rows(at):
        span = pl.ds(at, step)
        carried = g_s[span, :] + with_segments(a_s[span, :], seg)
        before = lru[span, :]
        keep = pos[span, :] > 0
        r, g, out = rate[span, :], igate[span, :], conv[span, :]
        log_decay = -8.0 * r * sp[...]
        decay = jnp.exp(log_decay)
        square = decay * decay
        mult = jnp.where(keep, jnp.sqrt(minus_expm1(2.0 * log_decay, square)), 1.0)
        scaled = carried * g
        grad_log = jnp.where(keep, decay * carried * before - scaled * out * square / mult, 0.0)
        slope = 8.0 * r * grad_log
        grad_rate = (-slope * sp[...] * (1.0 - r)).astype(BF16)
        grad_input = (scaled * out * mult * (1.0 - g)).astype(BF16)
        grate[span, :] = grad_rate
        ginput[span, :] = grad_input
        low[span, :] = out.astype(BF16)
        gc[span, :] = scaled * mult
        acc[0] += folded(slope * sg[...])
        acc[1] += folded(grad_rate.astype(F32))
        acc[2] += folded(grad_input.astype(F32))

    def middle(i, _):
        at = pl.multiple_of(i * big, 8)
        over_rows(at, big, step, middle_rows)
        span = pl.ds(at, big)
        gc[span, :] += nt_dot(grate[span, :], wr[...]) + nt_dot(ginput[span, :], wi[...])
        return 0

    lax.fori_loop(0, rows // big, middle, 0)
    gc[pl.ds(rows, pad), :] = jnp.zeros((pad, chans), F32)
    for j in range(1, taps):
        value = jnp.zeros((8, chans), F32)
        for k in range(j, taps):
            e = 8 * (k - j)
            masked = jnp.where(pos[e : e + 8, :] >= k, gc[e : e + 8, :], 0.0)
            value = value + cw[k : k + 1, :] * masked
        edge[pad - 8 * j : pad - 8 * j + 8, :] = value
    edge_copy = pltpu.make_async_remote_copy(
        edge, landed, edge_send, edge_recv, (lax.rem(tok + count - 1, count), ch), MESH
    )
    edge_copy.start()
    for stage in range(1, ex.bits):
        ex.relay(stage)
    for far in range(line.chips - 2, 1, -1):
        line.step(far)

    block = gate_o.shape[2]
    blocks = chans // block
    each = block // count
    shape = (chans, chans)
    row = lax.broadcasted_iota(jnp.int32, shape, 0).astype(F32)
    part = block_of(shape, 0, blocks * each)
    which = block_of(shape, 0, each) - part * blocks
    within = row - block_of(shape, 0, each) * each
    wanted = which * block + part * each + within
    column = lax.broadcasted_iota(jnp.int32, shape, 1).astype(F32)
    order = (column == wanted).astype(BF16)
    same = same_block(blocks, block)
    for i, grads in enumerate((grate, ginput)):
        kept = jnp.where(same, tn_dot(low[...], grads[...]), 0.0).astype(BF16)
        folded_in = nt_dot(kept, tiled_ones(block, blocks)).astype(BF16)
        value = jnp.dot(order, folded_in, preferred_element_type=F32)
        height = blocks * each
        for d in range(count):
            gate_o[d, i * height : (i + 1) * height, :] = value[d * height : (d + 1) * height]

    def last_rows(at):
        step = 32
        span = pl.ds(at, step)
        window = gc[pl.ds(at, step + pad), :]
        where = pos[pl.ds(at, step + pad), :]
        source = ext[pl.ds(at, step + pad), :]
        here = window[:step]
        total = cw[0:1, :] * here
        acc[3] += folded(here)
        acc[4] += folded(here * source[pad : pad + step])
        for k in range(1, taps):
            masked = jnp.where(where >= k, window, 0.0)
            total = total + cw[k : k + 1, :] * masked[8 * k : 8 * k + step]
            acc[4 + k] += folded(masked[:step] * source[pad - 8 * k : pad - 8 * k + step])
        gc[span, :] = total
        grec[span, :] = total.astype(BF16)
        both = total.astype(BF16).astype(F32) * source[pad : pad + step]
        both = both + ggp[span, :].astype(F32) * gpre[span, :]
        row_term[span, :] = jnp.sum(both, axis=1, keepdims=True)

    over_rows(0, rows, 32, last_rows)
    edge_copy.wait()
    first_row = lax.broadcasted_iota(jnp.int32, (SEGS, chans), 0) == 0
    for j in range(0, pad, 8):
        joined = jnp.where(first_row, landed[j : j + 8, :], edge[j : j + 8, :])
        at = pl.ds(rows - pad + j, 8)
        gc[at, :] = gc[at, :] + pltpu.roll(joined, SEGS - 1, 0)
    tail = -(-pad // 16) * 16
    span = pl.ds(rows - tail, tail)
    total = gc[span, :].astype(BF16)
    grec[span, :] = total
    both = total.astype(F32) * ext[pl.ds(pad + rows - tail, tail), :]
    both = both + ggp[span, :].astype(F32) * gpre[span, :]
    row_term[span, :] = jnp.sum(both, axis=1, keepdims=True)
    for k in range(8):
        sums[k : k + 1, :] = jnp.sum(acc[k], axis=0, keepdims=True)
    ex.settle(down_sum)
    line.step(1, carry_o)
    carry_o[2] = line.home[line.place]
    line.close(2)
    ggp_store.wait()
    for copy in sends:
        copy.wait_send()


def recur_bwd(
    g_block, w_out, gpre, ext, conv, rate, igate, lru, pos, cw, wr, wi, vectors, down, branch, block,
    ident,
):
    rows, chans = conv.shape
    n, count = lax.axis_size("ch"), lax.axis_size("tok")
    width = down.shape[1] // n
    pad = 8 * (cw.shape[0] - 1)
    ex = Spread(n, rows, width)
    half = jax.ShapeDtypeStruct((rows, chans), BF16)
    sem = pltpu.SemaphoreType.DMA
    anywhere = pl.BlockSpec(memory_space=pl.ANY)
    vmem = pl.BlockSpec(memory_space=pltpu.VMEM)
    loaded = (g_block, w_out, gpre, ext, conv, rate, igate, lru, wr, wi, branch)
    line = Line(count, (chans, g_block.shape[1] // count))
    return pl.pallas_call(
        functools.partial(recur_bwd_kernel, ex, line),
        out_shape=[
            half, half,
            jax.ShapeDtypeStruct((count, 2 * chans // count, block), F32),
            jax.ShapeDtypeStruct((8, chans), F32),
            jax.ShapeDtypeStruct((rows, 1), F32),
            jax.ShapeDtypeStruct((rows, width), F32),
            jax.ShapeDtypeStruct((3, *line.shape), BF16),
        ],
        in_specs=[anywhere] * 8 + [vmem] * 2 + [anywhere] * 2 + [vmem, anywhere, anywhere],
        out_specs=[vmem, anywhere] + [vmem] * 5,
        scratch_shapes=[pltpu.VMEM(array.shape, array.dtype) for array in loaded]
        + [pltpu.VMEM((rows, chans), BF16)] * 4
        + [
            pltpu.VMEM((rows, chans), F32),
            pltpu.VMEM((rows, chans), F32),
            pltpu.VMEM((rows + pad, chans), F32),
            pltpu.VMEM((count, 8, chans), F32),
            pltpu.VMEM((pad, chans), F32),
            pltpu.VMEM((pad, chans), F32),
            pltpu.VMEM((8, 8, chans), F32),
            sem((len(loaded),)), sem, sem, sem, sem((count - 1,)), sem((count - 1,)),
        ]
        + line.scratch()
        + ex.scratch(),
        compiler_params=pltpu.CompilerParams(
            collective_id=ident, has_side_effects=True, vmem_limit_bytes=62 << 20
        ),
    )(g_block, w_out, gpre, ext, conv, rate, igate, lru, pos, cw, wr, wi, vectors, down,
      branch)


class Exchange(Routes):
    def __init__(self, n, rows, width, chunks, gather):
        super().__init__(n, rows, width)
        self.chunks, self.gather = chunks, gather
        self.size = rows // chunks
        self.ring = min(chunks, self.bits + 2)

    def scratch(self):
        n, rows, half, chunks = self.n, self.rows, self.half, self.chunks
        shapes = [
            pltpu.VMEM((2, n - 1, rows, half), BF16),
            pltpu.VMEM((2, n - 1, rows, half), BF16),
            pltpu.VMEM((len(self.keeps), self.ring * self.size, half), F32),
            pltpu.SemaphoreType.DMA((2, n, chunks)),
            pltpu.SemaphoreType.DMA((2, n, chunks)),
        ]
        if self.gather:
            shapes += [
                pltpu.VMEM((n, 2, rows, half), BF16),
                pltpu.SemaphoreType.DMA((self.bits, 2, chunks)),
                pltpu.SemaphoreType.DMA((self.bits, 2, chunks)),
                pltpu.SemaphoreType.DMA((2, n, chunks)),
                pltpu.SemaphoreType.DMA((2, n, chunks)),
            ]
        return shapes

    def bind(self, refs):
        if self.gather:
            (self.out, self.into, self.acc, self.ss, self.rs,
             self.full, self.gs, self.gr, self.fs, self.fr) = refs
        else:
            self.out, self.into, self.acc, self.ss, self.rs = refs
        self.tok, self.me = lax.axis_index("tok"), lax.axis_index("ch")

    def span(self, c):
        return pl.ds(pl.multiple_of(c * self.size, self.size), self.size)

    def acc_span(self, c):
        at = lax.rem(c, self.ring) * self.size
        return pl.ds(pl.multiple_of(at, self.size), self.size)

    def reduce_copy(self, part, mask, c):
        return pltpu.make_async_remote_copy(
            self.out.at[part, mask - 1, self.span(c)],
            self.into.at[part, mask - 1, self.span(c)],
            self.ss.at[part, mask, c],
            self.rs.at[part, mask, c],
            self.peer(self.bit_of(part, mask)),
            MESH,
        )

    def produce(self, c, block):
        span = self.span(c)
        for mask in sorted(range(self.n), key=lambda m: -m.bit_count()):
            value = block(mask)
            for part in range(2):
                piece = value[:, part * self.half : (part + 1) * self.half]
                if (part, mask) in self.keeps:
                    self.acc[self.keeps.index((part, mask)), self.acc_span(c), :] = piece
                else:
                    self.out[part, mask - 1, span, :] = piece.astype(BF16)
                    self.reduce_copy(part, mask, c).start()

    def summed(self, part, mask, c):
        span = self.span(c)
        value = self.acc[self.keeps.index((part, mask)), self.acc_span(c), :]
        for b in self.incoming(part, mask):
            came = mask | (1 << b)
            self.reduce_copy(part, came, c).wait_recv()
            value = value + self.into[part, came - 1, span, :].astype(F32)
        return value

    def pass_on(self, stage, c):
        for part in range(2):
            for mask in range(1, self.n):
                if self.stage_of(part, mask) == stage:
                    value = self.summed(part, mask, c)
                    self.out[part, mask - 1, self.span(c), :] = value.astype(BF16)
                    self.reduce_copy(part, mask, c).start()

    def close_reduce(self, c):
        for part in range(2):
            for mask in range(1, self.n):
                self.reduce_copy(part, mask, c).wait_send()

    def gather_copy(self, part, mask, b, c):
        block = self.full.at[self.me ^ mask, part, self.span(c)]
        if mask == 0:
            return pltpu.make_async_remote_copy(
                block, block, self.gs.at[b, part, c], self.gr.at[b, part, c], self.peer(b), MESH
            )
        got = mask | (1 << b)
        return pltpu.make_async_remote_copy(
            block, block, self.fs.at[part, got, c], self.fr.at[part, got, c], self.peer(b), MESH
        )

    def arrived(self, part, mask, c):
        block = self.full.at[self.me ^ mask, part, self.span(c)]
        if mask.bit_count() == 1:
            b = low_bit(mask)
            sems = (self.gs.at[b, part, c], self.gr.at[b, part, c])
        else:
            sems = (self.fs.at[part, mask, c], self.fr.at[part, mask, c])
        pltpu.make_async_remote_copy(block, block, *sems, self.peer(0), MESH).wait_recv()

    def gather_start(self, c, halves):
        for part in range(2):
            self.full[self.me, part, self.span(c), :] = halves[part].astype(BF16)
            for b in range(self.bits):
                self.gather_copy(part, 0, b, c).start()

    def nexts(self, part, mask):
        return range(high_bit(mask) + 1, self.bits) if part == 0 else range(low_bit(mask))

    def gather_pass(self, stage, c):
        for mask in [m for m in range(1, self.n) if m.bit_count() == stage]:
            for part in range(2):
                self.arrived(part, mask, c)
                for b in self.nexts(part, mask):
                    self.gather_copy(part, mask, b, c).start()

    def gather_close(self, c):
        for part in range(2):
            self.arrived(part, self.n - 1, c)
        for part in range(2):
            for b in range(self.bits):
                self.gather_copy(part, 0, b, c).wait_send()
            for mask in range(1, self.n):
                for b in self.nexts(part, mask):
                    self.gather_copy(part, mask, b, c).wait_send()

    def piece(self, owner, c):
        span = self.span(c)
        return jnp.concatenate([self.full[owner, 0, span, :], self.full[owner, 1, span, :]], axis=1)

    def own_sum(self, c):
        return [self.summed(part, 0, c) for part in range(2)]

    def run(self, stages, extra=None, after=None):
        depth = len(stages)

        def turn(t, _):
            if extra is not None:
                extra(t)
            for s in reversed(range(depth)):
                c = t - s

                @pl.when(jnp.logical_and(c >= 0, c < self.chunks))
                def _():
                    stages[s](c)

            if after is not None:
                after(t)
            return 0

        lax.fori_loop(0, self.chunks + depth - 1, turn, 0)


def own_part(gain, ex):
    return gain[:, pl.ds(pl.multiple_of(ex.me * ex.width, 128), ex.width)]


def tile_of(size):
    return next(t for t in (512, 384, 256, 128, size) if size % t == 0)


def mid_kernel(
    ex, branch, w_out, x_own, gain, wg_h, wu_h, wd_h, cot_h,
    normed_h, full_h, own_o, scale_o, hidden_h, gg_h, gu_h,
    wg, wu, wd, cot, normed, hidden, gg, gu, wsem, csem, osem, fsem, *refs,
):
    ex.bind(refs)
    n, width = ex.n, ex.width
    units = wg.shape[1]
    tile = tile_of(units)
    greet(ex.neighbours())
    loads = [
        pltpu.make_async_copy(a, b, wsem.at[i])
        for i, (a, b) in enumerate(((wg_h, wg), (wu_h, wu), (wd_h, wd)))
    ]
    for load in loads:
        load.start()

    def cot_load(c):
        return pltpu.make_async_copy(cot_h.at[ex.span(c)], cot, csem)

    outs = ((normed, normed_h), (hidden, hidden_h), (gg, gg_h), (gu, gu_h))

    def store(i, c):
        source, target = outs[i]
        return pltpu.make_async_copy(source, target.at[ex.span(c)], osem.at[i])

    def full_store(c):
        span = ex.span(c)
        return pltpu.make_async_copy(
            ex.full.at[:, :, span], full_h.at[:, :, span], fsem.at[c]
        )

    cot_load(0).start()

    def first(c):
        rows = branch[ex.span(c), :]

        def block(mask):
            at = pl.multiple_of((ex.me ^ mask) * width, 128)
            return jnp.dot(rows, w_out[:, pl.ds(at, width)], preferred_element_type=F32)

        ex.produce(c, block)

    def own(c):
        span = ex.span(c)
        value = jnp.concatenate(ex.own_sum(c), axis=1) + x_own[span, :].astype(F32)
        own_o[span, :] = value
        ex.gather_start(c, [value[:, : ex.half], value[:, ex.half :]])
        ex.close_reduce(c)

    def final(c):
        ex.gather_close(c)
        full_store(c).start()

        @pl.when(c > 0)
        def _():
            store(0, c - 1).wait()

        def norm_rows(at):
            span = pl.ds(pl.multiple_of(c * ex.size + at, 16), 16)
            pieces = [
                ex.full[d, part, span, :].astype(F32) for d in range(n) for part in range(2)
            ]
            total = sum(jnp.sum(p * p, axis=1, keepdims=True) for p in pieces)
            scale = lax.rsqrt(total * (1.0 / (n * width)) + 1e-06)
            scale_o[span, :] = scale
            for i, p in enumerate(pieces):
                columns = slice(i * ex.half, (i + 1) * ex.half)
                normed[pl.ds(at, 16), columns] = (p * scale * gain[:, columns]).astype(BF16)

        over_rows(0, ex.size, 16, norm_rows)
        store(0, c).start()

    def feed(c):
        @pl.when(c == 0)
        def _():
            for load in loads:
                load.wait()

        cot_load(c).wait()

        @pl.when(c > 0)
        def _():
            for i in range(1, 4):
                store(i, c - 1).wait()

        for j in range(units // tile):
            columns = slice(j * tile, (j + 1) * tile)
            act, slope = gelu_parts(
                jnp.dot(normed[...], wg[:, columns], preferred_element_type=F32)
            )
            up = jnp.dot(normed[...], wu[:, columns], preferred_element_type=F32)
            grad = nt_dot(cot[...], wd[columns, :])
            hidden[:, columns] = (act * up).astype(BF16)
            gg[:, columns] = (grad * up * slope).astype(BF16)
            gu[:, columns] = (grad * act).astype(BF16)

        @pl.when(c + 1 < ex.chunks)
        def _():
            cot_load(c + 1).start()

        for i in range(1, 4):
            store(i, c).start()

    stages = [first]
    stages += [functools.partial(ex.pass_on, s) for s in range(1, ex.bits)]
    stages += [own]
    stages += [functools.partial(ex.gather_pass, s) for s in range(1, ex.bits)]
    stages += [final]
    depth = len(stages)

    def after(t):
        c = t - (depth - 1)

        @pl.when(c >= 0)
        def _():
            feed(c)

    ex.run(stages, after=after)
    for i in range(4):
        store(i, ex.chunks - 1).wait()
    for c in range(ex.chunks):
        full_store(c).wait()


def mid_exchange(branch, w_out, x_own, gain, w_gate, w_up, w_down, cot, ident, chunks=4):
    n = lax.axis_size("ch")
    rows, width = x_own.shape
    units = w_gate.shape[1]
    ex = Exchange(n, rows, width, chunks, True)
    whole = jax.ShapeDtypeStruct((rows, n * width), BF16)
    inner = jax.ShapeDtypeStruct((rows, units), BF16)
    wide, narrow = pltpu.VMEM((ex.size, n * width), BF16), pltpu.VMEM((ex.size, units), BF16)
    sem = pltpu.SemaphoreType.DMA
    anywhere = pl.BlockSpec(memory_space=pl.ANY)
    vmem = pl.BlockSpec(memory_space=pltpu.VMEM)
    return pl.pallas_call(
        functools.partial(mid_kernel, ex),
        out_shape=[
            whole,
            jax.ShapeDtypeStruct((n, 2, rows, ex.half), BF16),
            jax.ShapeDtypeStruct((rows, width), F32),
            jax.ShapeDtypeStruct((rows, 1), F32),
            inner, inner, inner,
        ],
        in_specs=[vmem] * 4 + [anywhere] * 4,
        out_specs=[anywhere, anywhere, vmem, vmem] + [anywhere] * 3,
        scratch_shapes=[
            pltpu.VMEM(w_gate.shape, BF16),
            pltpu.VMEM(w_up.shape, BF16),
            pltpu.VMEM(w_down.shape, BF16),
            wide, wide, narrow, narrow, narrow,
            sem((3,)), sem, sem((4,)), sem((chunks,)),
        ]
        + ex.scratch(),
        compiler_params=pltpu.CompilerParams(
            collective_id=ident, has_side_effects=True, vmem_limit_bytes=62 << 20
        ),
    )(branch, w_out, x_own, gain, w_gate, w_up, w_down, cot)


class Halving:
    def __init__(self, count, rows, columns):
        self.count, self.chips = count, count // 2
        self.bits = self.chips.bit_length() - 1
        self.rows, self.columns = rows // count, columns

    def scratch(self):
        block = (self.rows, self.columns)
        sem = pltpu.SemaphoreType.DMA
        steps = max(self.bits, 1)
        return [
            pltpu.VMEM((self.chips, *block), BF16),
            pltpu.VMEM((self.chips, *block), BF16),
            pltpu.VMEM((max(self.chips - 1, 1), *block), BF16),
            sem((self.chips,)), sem((self.chips,)), sem((self.chips,)),
            sem((max(self.chips - 1, 1),)), sem((max(self.chips - 1, 1),)),
        ]

    def bind(self, refs, source):
        (self.home, self.pair, self.into, self.ls, self.ps, self.pr, self.ss, self.rs) = refs
        self.source = source
        self.tok, self.ch = lax.axis_index("tok"), lax.axis_index("ch")
        self.place, self.core = self.tok // 2, self.tok % 2

    def targets(self):
        found = [(self.tok + 1 - 2 * self.core, self.ch)]
        for step in range(self.bits):
            bit = (self.place // (1 << step)) % 2
            found.append((self.tok + (2 << step) * (1 - 2 * bit), self.ch))
        return found

    def rows_of(self, block):
        return self.source.at[pl.ds(pl.multiple_of(block * self.rows, self.rows), self.rows)]

    def chip_at(self, i):
        return self.place + sum(
            (1 << b) * (1 - 2 * ((self.place // (1 << b)) % 2)) for b in range(self.bits) if i >> b & 1
        )

    def load(self, i):
        return pltpu.make_async_copy(
            self.rows_of(2 * self.chip_at(i) + self.core), self.home.at[i], self.ls.at[i]
        )

    def pair_copy(self, i):
        away = self.rows_of(2 * self.chip_at(i) + 1 - self.core)
        return pltpu.make_async_remote_copy(
            away, self.pair.at[i], self.ps.at[i], self.pr.at[i], self.targets()[0], MESH
        )

    def sent_at(self, step):
        return [i for i in range(1, self.chips) if low_bit(i) == step]

    def hop(self, i):
        return pltpu.make_async_remote_copy(
            self.home.at[i], self.into.at[i - 1], self.ss.at[i - 1], self.rs.at[i - 1],
            self.targets()[1 + low_bit(i)], MESH,
        )

    def launch(self):
        for i in reversed(range(self.chips)):
            self.pair_copy(i).start()
        for i in reversed(range(self.chips)):
            self.load(i).start()

    def add(self, i, came):
        def rows(at):
            span = pl.ds(pl.multiple_of(at, 16), 16)
            total = self.home[i, span, :].astype(F32)
            for ref, j in came:
                total = total + ref[j, span, :].astype(F32)
            self.home[i, span, :] = total.astype(BF16)

        over_rows(0, self.rows, 16, rows, 2)

    def join(self):
        for i in sorted(range(self.chips), key=lambda i: i % 2 == 0):
            self.load(i).wait()
            self.pair_copy(i).wait_recv()
            self.add(i, [(self.pair, i)])
            if i in self.sent_at(0):
                self.hop(i).start()

    def step(self, step):
        for i in self.sent_at(step):
            came = [i | (1 << b) for b in range(step)]
            for j in came:
                self.hop(j).wait_recv()
            self.add(i, [(self.into, j - 1) for j in came])
            self.hop(i).start()

    def settle(self, result):
        came = [1 << b for b in range(self.bits)]
        for j in came:
            self.hop(j).wait_recv()

        def rows(at):
            span = pl.ds(pl.multiple_of(at, 16), 16)
            total = self.home[0, span, :].astype(F32)
            for j in came:
                total = total + self.into[j - 1, span, :].astype(F32)
            result[span, :] = total

        over_rows(0, self.rows, 16, rows, 2)
        for i in range(self.chips):
            self.pair_copy(i).wait_send()
        for i in range(1, self.chips):
            self.hop(i).wait_send()


def back_kernel(
    ex, halves, gg_h, gu_h, wg_h, wu_h, full_h, mid_own, cot_h, cot_own, scale, gain, source_a, source_b,
    block_o, own_o, gain_o, sum_a, sum_b,
    gg, gu, w_gate, w_up, full, cot, gsem, wsem, fsem, *refs,
):
    held = len(halves[0].scratch())
    for i, source in enumerate((source_a, source_b)):
        halves[i].bind(refs[i * held : (i + 1) * held], source)
    ex.bind(refs[2 * held :])
    n, width = ex.n, ex.width
    order = sorted(range(n), key=lambda m: -m.bit_count())

    def rows_load(c):
        span = pl.ds(c * ex.size, ex.size)
        return [
            pltpu.make_async_copy(gg_h.at[span], gg.at[span], gsem.at[0, c]),
            pltpu.make_async_copy(gu_h.at[span], gu.at[span], gsem.at[1, c]),
        ]

    def weight_load(mask):
        at = pl.ds(pl.multiple_of((ex.me ^ mask) * width, 128), width)
        return [
            pltpu.make_async_copy(wg_h.at[at], w_gate.at[at], wsem.at[0, mask]),
            pltpu.make_async_copy(wu_h.at[at], w_up.at[at], wsem.at[1, mask]),
        ]

    def final_load(c):
        span = ex.span(c)
        return [
            pltpu.make_async_copy(full_h.at[:, :, span], full, fsem.at[0]),
            pltpu.make_async_copy(cot_h.at[span], cot, fsem.at[1]),
        ]

    for copy in rows_load(0):
        copy.start()
    for mask in order:
        for copy in weight_load(mask):
            copy.start()
    for c in range(1, ex.chunks):
        for copy in rows_load(c):
            copy.start()
    for copy in final_load(0):
        copy.start()
    greet(ex.neighbours() + halves[0].targets())
    for half in halves:
        half.launch()
    gain_o[...] = jnp.zeros_like(gain_o)

    def first(c):
        span = ex.span(c)
        for copy in rows_load(c):
            copy.wait()
        left, right = gg[span, :], gu[span, :]

        def block(mask):
            @pl.when(c == 0)
            def _():
                for copy in weight_load(mask):
                    copy.wait()

            at = pl.ds(pl.multiple_of((ex.me ^ mask) * width, 128), width)
            return nt_dot(left, w_gate[at, :]) + nt_dot(right, w_up[at, :])

        ex.produce(c, block)

    def own(c):
        span = ex.span(c)
        s = scale[span, :]
        grad = jnp.concatenate(ex.own_sum(c), axis=1)
        value = cot_own[span, :].astype(F32) + grad * own_part(gain, ex) * s
        own_o[span, :] = value
        ex.gather_start(c, [value[:, : ex.half], value[:, ex.half :]])
        ex.close_reduce(c)
        product = grad * mid_own[span, :] * s
        gain_o[...] += jnp.sum(product.reshape(-1, 8, width), axis=0)

    def final(c):
        ex.gather_close(c)
        for copy in final_load(c):
            copy.wait()

        def rows(at):
            here = pl.ds(pl.multiple_of(at, 16), 16)
            span = pl.ds(pl.multiple_of(c * ex.size + at, 16), 16)
            s = scale[span, :]
            pieces = [(d, part) for d in range(n) for part in range(2)]
            values = [ex.full[d, part, span, :].astype(F32) for d, part in pieces]
            mids = [full[d, part, here, :].astype(F32) for d, part in pieces]
            total = jnp.zeros((16, 1), F32)
            for i, (value, middle) in enumerate(zip(values, mids, strict=True)):
                columns = slice(i * ex.half, (i + 1) * ex.half)
                delta = value - cot[here, columns].astype(F32)
                total = total + jnp.sum(delta * middle, axis=1, keepdims=True)
            factor = s * s * total * (1.0 / (n * width))
            own_o[span, :] = own_o[span, :] - factor * mid_own[span, :]
            for i, (value, middle) in enumerate(zip(values, mids, strict=True)):
                columns = slice(i * ex.half, (i + 1) * ex.half)
                block_o[span, columns] = (value - factor * middle).astype(BF16)

        over_rows(0, ex.size, 16, rows)

        @pl.when(c + 1 < ex.chunks)
        def _():
            for copy in final_load(c + 1):
                copy.start()

    stages = [first]
    stages += [functools.partial(ex.pass_on, s) for s in range(1, ex.bits)]
    stages += [own]
    stages += [functools.partial(ex.gather_pass, s) for s in range(1, ex.bits)]
    stages += [final]
    turns = ex.chunks + len(stages) - 1
    acts = [(0, half.join) for half in halves]
    for i, half in enumerate(halves):
        for step in range(1, half.bits):
            turn = min(2 * step + 1 + 2 * i, turns - 1)
            acts.append((turn, functools.partial(half.step, step)))

    def after(t):
        for turn, act in acts:

            @pl.when(t == turn)
            def _(act=act):
                act()

    ex.run(stages, after=after)
    halves[0].settle(sum_a)
    halves[1].settle(sum_b)


def back_exchange(
    grad_gate, grad_up, w_gate, w_up, full, mid_own, cot, cot_own, scale, gain_own, sources,
    ident, chunks=4,
):
    n, count = lax.axis_size("ch"), lax.axis_size("tok")
    rows, width = mid_own.shape
    ex = Exchange(n, rows, width, chunks, True)
    halves = [Halving(count, *source.shape) for source in sources]
    sem = pltpu.SemaphoreType.DMA
    anywhere = pl.BlockSpec(memory_space=pl.ANY)
    vmem = pl.BlockSpec(memory_space=pltpu.VMEM)
    return pl.pallas_call(
        functools.partial(back_kernel, ex, halves),
        out_shape=[
            jax.ShapeDtypeStruct((rows, n * width), BF16),
            jax.ShapeDtypeStruct((rows, width), F32),
            jax.ShapeDtypeStruct((8, width), F32),
        ]
        + [jax.ShapeDtypeStruct((half.rows, half.columns), F32) for half in halves],
        in_specs=[anywhere] * 5 + [vmem, anywhere, vmem, vmem, vmem, anywhere, anywhere],
        out_specs=[vmem] * 5,
        scratch_shapes=[
            pltpu.VMEM(grad_gate.shape, BF16),
            pltpu.VMEM(grad_up.shape, BF16),
            pltpu.VMEM(w_gate.shape, BF16),
            pltpu.VMEM(w_up.shape, BF16),
            pltpu.VMEM((n, 2, ex.size, ex.half), BF16),
            pltpu.VMEM((ex.size, n * width), BF16),
            sem((2, chunks)), sem((2, n)), sem((2,)),
        ]
        + [shape for half in halves for shape in half.scratch()]
        + ex.scratch(),
        compiler_params=pltpu.CompilerParams(
            collective_id=ident, has_side_effects=True, vmem_limit_bytes=63 << 20
        ),
    )(grad_gate, grad_up, w_gate, w_up, full, mid_own, cot, cot_own, scale, gain_own, *sources)


class Line:
    def __init__(self, count, shape):
        self.count, self.shape, self.chips = count, shape, count // 2

    def scratch(self):
        blocks = (self.chips, *self.shape)
        hops = (max(self.chips - 1, 1), *self.shape)
        sems = [pltpu.SemaphoreType.DMA((self.chips,))] * 6
        return [pltpu.VMEM(blocks, BF16)] * 3 + [pltpu.VMEM(hops, BF16)] * 4 + sems

    def bind(self, refs):
        (self.pair_out, self.pair_in, self.home, self.up_out, self.up_in, self.dn_out, self.dn_in,
         self.ps, self.pr, self.us, self.ur, self.ds, self.dr) = refs
        self.tok, self.ch = lax.axis_index("tok"), lax.axis_index("ch")
        self.place, self.core = self.tok // 2, self.tok % 2

    def pair_copy(self, z):
        return pltpu.make_async_remote_copy(
            self.pair_out.at[z], self.pair_in.at[z], self.ps.at[z], self.pr.at[z],
            (self.tok + 1 - 2 * self.core, self.ch), MESH,
        )

    def away(self, z):
        return 2 * z + 1 - self.core

    def kept(self, z):
        return 2 * z + self.core

    def put_away(self, z, value):
        self.pair_out[z] = value.astype(BF16)
        self.pair_copy(z).start()

    def put_home(self, z, value):
        self.home[z] = value.astype(BF16)

    def over_rows(self, body):
        size = 32

        def one(i, _):
            body(pl.ds(i * size, size))
            return 0

        lax.fori_loop(0, self.shape[0] // size, one, 0, unroll=2)

    def join(self):
        for z in range(self.chips):
            self.pair_copy(z).wait_recv()

            def add(span, z=z):
                total = self.home[z, span, :].astype(F32) + self.pair_in[z, span, :].astype(F32)
                self.home[z, span, :] = total.astype(BF16)

            self.over_rows(add)

    def ways(self):
        last = self.chips - 1
        rising = (self.up_out, self.up_in, self.us, self.ur, self.place, 1)
        falling = (self.dn_out, self.dn_in, self.ds, self.dr, last - self.place, -1)
        return rising, falling

    def hop(self, way, far):
        out, into, ss, rs, _, sign = way
        count = self.count
        return pltpu.make_async_remote_copy(
            out.at[far - 1], into.at[far - 1], ss.at[far - 1], rs.at[far - 1],
            ((self.tok + 2 * sign + count) % count, self.ch), MESH,
        )

    def step(self, far, kept=None):
        for way in self.ways():
            out, into, _, _, rank, sign = way

            @pl.when(rank + far <= self.chips - 1)
            def _():
                if far < self.chips - 1:

                    @pl.when(rank >= 1)
                    def _():
                        self.hop(way, far + 1).wait_recv()

                def add(span):
                    value = self.home[self.place + sign * far, span, :].astype(F32)
                    if far < self.chips - 1:
                        came = into[far, span, :].astype(F32)
                        value = value + jnp.where(rank >= 1, came, 0.0)
                    out[far - 1, span, :] = value.astype(BF16)

                self.over_rows(add)
                if kept is None:
                    self.hop(way, far).start()
                else:
                    kept[(1 - sign) // 2] = out[far - 1]

    def settle(self, result):
        if self.chips > 1:
            for way in self.ways():

                @pl.when(way[4] >= 1)
                def _():
                    self.hop(way, 1).wait_recv()

        def add(span):
            value = self.home[self.place, span, :].astype(F32)
            for way in self.ways() if self.chips > 1 else ():
                value = value + jnp.where(way[4] >= 1, way[1][0, span, :].astype(F32), 0.0)
            result[span, :] = value

        self.over_rows(add)

    def close(self, least=1):
        for z in range(self.chips):
            self.pair_copy(z).wait_send()
        for far in range(least, self.chips):
            for way in self.ways():

                @pl.when(way[4] + far <= self.chips - 1)
                def _():
                    self.hop(way, far).wait_send()


class LastHop:
    def __init__(self, count, shape):
        self.count, self.chips, self.shape = count, count // 2, shape

    def scratch(self):
        sem = pltpu.SemaphoreType.DMA((2,))
        return [pltpu.VMEM((2, *self.shape), BF16), sem, sem]

    def bind(self, refs, carry):
        self.into, self.ss, self.rs = refs
        self.carry = carry
        self.tok, self.ch = lax.axis_index("tok"), lax.axis_index("ch")
        place = self.tok // 2
        self.ranks = (place, self.chips - 1 - place)

    def hop(self, way):
        target = (self.tok + 2 - 4 * way + self.count) % self.count
        return pltpu.make_async_remote_copy(
            self.carry.at[way], self.into.at[way], self.ss.at[way], self.rs.at[way],
            (target, self.ch), MESH,
        )

    def launch(self):
        for way in range(2):

            @pl.when(self.ranks[1 - way] >= 1)
            def _():
                self.hop(way).start()

    def settle(self, result):
        for way in range(2):

            @pl.when(self.ranks[way] >= 1)
            def _():
                self.hop(way).wait_recv()

        def rows(at):
            span = pl.ds(pl.multiple_of(at, 16), 16)
            total = self.carry[2, span, :].astype(F32)
            for way in range(2):
                came = self.into[way, span, :].astype(F32)
                total = total + jnp.where(self.ranks[way] >= 1, came, 0.0)
            result[span, :] = total

        over_rows(0, self.shape[0], 16, rows, 2)
        for way in range(2):

            @pl.when(self.ranks[1 - way] >= 1)
            def _():
                self.hop(way).wait_send()


def block_columns(source, block, count):
    size = source.shape[1] // count
    return source[:, pl.ds(pl.multiple_of(block * size, 128), size)]


def fill(line, product):
    def far_side(z, _):
        line.put_away(z, product(line.away(z)))
        return 0

    def near_side(z, _):
        line.put_home(z, product(line.kept(z)))
        return 0

    lax.fori_loop(0, line.chips, far_side, 0)
    lax.fori_loop(0, line.chips, near_side, 0)


def end_kernel(
    ex, last, lines,
    g_rec, g_pre, wb_h, wg_h, stat, small, normed_h, carry, gate_blocks, x_own,
    scale, gain, mid_own,
    input_h, small_o, gain_o, mlp_o, taps_o, wb_o, wg_o, wo_o, gate_o,
    input_v, wide, w_branch, w_gelu, isem, lsem, stats, stat_sum, smalls, gains, gain_acc, st_s, st_r, sm_s, sm_r, gn_s, gn_r, *refs,
):
    held = len(lines[0].scratch())
    for i, line in enumerate(lines):
        line.bind(refs[i * held : (i + 1) * held])
    ahead = len(lines) * held
    last.bind(refs[ahead : ahead + 3], carry)
    ex.bind(refs[ahead + 3 :])
    n, width = ex.n, ex.width
    count = lax.axis_size("tok")
    across = [(ex.tok, ex.me ^ m) for m in range(1, n)]
    normed_load = pltpu.make_async_copy(normed_h, wide, lsem.at[0])
    loads = [
        pltpu.make_async_copy(wb_h, w_branch, lsem.at[1]),
        pltpu.make_async_copy(wg_h, w_gelu, lsem.at[2]),
    ]
    for load in [normed_load, *loads]:
        load.start()
    greet(across + tok_targets())
    last.launch()
    stats[ex.me] = stat[...]
    copies = []
    for m in range(1, n):
        copy = pltpu.make_async_remote_copy(
            stats.at[ex.me], stats.at[ex.me], st_s.at[m - 1], st_r.at[m - 1], across[m - 1], MESH
        )
        copy.start()
        copies.append(copy)

    def spread(buffer, send, recv):
        for o, target in enumerate(tok_targets()):
            copy = pltpu.make_async_remote_copy(
                buffer.at[ex.tok], buffer.at[ex.tok], send.at[o], recv.at[o], target, MESH
            )
            copy.start()
            copies.append(copy)

    def collect(buffer, send, recv):
        for o in range(count - 1):
            block = buffer.at[lax.rem(ex.tok + count - 1 - o, count)]
            pltpu.make_async_remote_copy(
                block, block, send.at[o], recv.at[o], tok_targets()[o], MESH
            ).wait_recv()

    smalls[ex.tok] = small[...]
    spread(smalls, sm_s, sm_r)
    wb_line, wg_line, gate_line = lines

    def start(line):
        line.join()
        if line.chips > 1:
            line.step(line.chips - 1)

    fill(gate_line, lambda d: gate_blocks[d].astype(F32))
    normed_load.wait()
    fill(wb_line, lambda d: tn_dot(block_columns(wide, d, count), g_rec[...]))
    start(gate_line)
    start(wb_line)
    fill(wg_line, lambda d: tn_dot(block_columns(wide, d, count), g_pre[...]))
    start(wg_line)
    for load in loads:
        load.wait()
    for m in range(1, n):
        block = stats.at[ex.me ^ m]
        pltpu.make_async_remote_copy(
            block, block, st_s.at[m - 1], st_r.at[m - 1], across[m - 1], MESH
        ).wait_recv()
    stat_sum[...] = jnp.sum(stats[...], axis=0)
    steps = ex.size // SEGS

    def input_store(c, part):
        source = input_v.at[pl.ds(c * steps, steps), part]
        target = input_h.at[pl.ds(part * (ex.rows // SEGS) + c * steps, steps)]
        return pltpu.make_async_copy(source, target, isem.at[part, c])

    gain_acc[...] = jnp.zeros_like(gain_acc)

    def first(c):
        span = ex.span(c)
        left, right = g_rec[span, :], g_pre[span, :]

        def block(mask):
            at = pl.ds(pl.multiple_of((ex.me ^ mask) * width, 128), width)
            return nt_dot(left, w_branch[at, :]) + nt_dot(right, w_gelu[at, :])

        ex.produce(c, block)

    def own(c):
        span = ex.span(c)
        grad = jnp.concatenate(ex.own_sum(c), axis=1)
        along = stat_sum[pl.ds(c, 1), :]
        square = (ex.size, ex.size)
        same = lax.broadcasted_iota(jnp.int32, square, 0) == lax.broadcasted_iota(
            jnp.int32, square, 1
        )
        term = jnp.sum(jnp.where(same, along, 0.0), axis=1, keepdims=True)
        s = scale[span, :]
        mine = x_own[span, :].astype(F32)
        value = (
            mid_own[span, :]
            + s * own_part(gain, ex) * grad
            - s * s * mine * (term * (1.0 / (n * width)))
        )
        input_v[pl.ds(c * steps, steps)] = eight(value)
        for part in range(SEGS):
            input_store(c, part).start()
        gain_acc[...] += jnp.sum((grad * mine * s).reshape(-1, 8, width), axis=0)
        ex.close_reduce(c)

    stages = [first]
    stages += [functools.partial(ex.pass_on, s) for s in range(1, ex.bits)]
    stages += [own]
    turns = ex.chunks + len(stages) - 1
    acts = [
        functools.partial(line.step, far)
        for far in range(wb_line.chips - 2, 0, -1)
        for line in (gate_line, wb_line, wg_line)
    ]

    def extra(t):
        for i, act in enumerate(acts):
            when = 2 + i * (turns - 2) // max(len(acts), 1)

            @pl.when(t == when)
            def _():
                act()

    ex.run(stages, extra)
    gains[ex.tok] = jnp.broadcast_to(jnp.sum(gain_acc[...], axis=0, keepdims=True), (8, width))
    spread(gains, gn_s, gn_r)
    collect(smalls, sm_s, sm_r)
    all_small = jnp.sum(smalls[...], axis=0)
    chans = g_rec.shape[1]
    small_o[...] = all_small[:8]
    taps_o[...] = all_small[4:8, :chans]
    mlp_o[...] = all_small[8:9, :width]
    last.settle(wo_o)
    gate_line.settle(gate_o)
    wb_line.settle(wb_o)
    wg_line.settle(wg_o)
    collect(gains, gn_s, gn_r)
    gain_o[...] = jnp.sum(gains[...], axis=0)[0:1]
    for c in range(ex.chunks):
        for part in range(SEGS):
            input_store(c, part).wait()
    for copy in copies:
        copy.wait_send()
    for line in lines:
        line.close()


def end_exchange(
    g_rec, g_pre, w_branch, w_gelu, stat, small, normed, carry, gate_blocks, x_own, scale, gain,
    mid_own, ident,
):
    n, count = lax.axis_size("ch"), lax.axis_size("tok")
    rows, width = x_own.shape
    chans, total = g_rec.shape[1], normed.shape[1]
    chunks = stat.shape[0]
    ex = Exchange(n, rows, width, chunks, False)
    lines = [
        Line(count, (total // count, chans)),
        Line(count, (total // count, chans)),
        Line(count, gate_blocks.shape[1:]),
    ]
    last = LastHop(count, carry.shape[1:])
    anywhere = pl.BlockSpec(memory_space=pl.ANY)
    vmem = pl.BlockSpec(memory_space=pltpu.VMEM)
    sem = pltpu.SemaphoreType.DMA
    return pl.pallas_call(
        functools.partial(end_kernel, ex, last, lines),
        out_shape=[
            jax.ShapeDtypeStruct((rows, width), F32),
            jax.ShapeDtypeStruct((8, small.shape[1]), F32),
            jax.ShapeDtypeStruct((1, width), F32),
            jax.ShapeDtypeStruct((1, width), F32),
            jax.ShapeDtypeStruct((4, chans), F32),
            jax.ShapeDtypeStruct(lines[0].shape, F32),
            jax.ShapeDtypeStruct(lines[1].shape, F32),
            jax.ShapeDtypeStruct(last.shape, F32),
            jax.ShapeDtypeStruct(lines[2].shape, F32),
        ],
        in_specs=[anywhere if i in (2, 3, 6) else vmem for i in range(13)],
        out_specs=[anywhere] + whole_vmem(8),
        scratch_shapes=[
            pltpu.VMEM((rows // SEGS, SEGS, width), F32),
            pltpu.VMEM((rows, total), BF16),
            pltpu.VMEM(w_branch.shape, BF16),
            pltpu.VMEM(w_gelu.shape, BF16),
            sem((SEGS, chunks)),
            sem((3,)),
            pltpu.VMEM((n, *stat.shape), F32),
            pltpu.VMEM(stat.shape, F32),
            pltpu.VMEM((count, *small.shape), F32),
            pltpu.VMEM((count, 8, width), F32),
            pltpu.VMEM((8, width), F32),
            sem((n - 1,)), sem((n - 1,)),
            sem((count - 1,)), sem((count - 1,)),
            sem((count - 1,)), sem((count - 1,)),
        ]
        + [shape for line in lines for shape in line.scratch()]
        + last.scratch()
        + ex.scratch(),
        compiler_params=pltpu.CompilerParams(
            collective_id=ident, has_side_effects=True, vmem_limit_bytes=63 << 20
        ),
    )(g_rec, g_pre, w_branch, w_gelu, stat, small, normed, carry, gate_blocks, x_own, scale, gain,
      mid_own)


def to_major(rows):
    count, width = rows.shape
    return rows.reshape(SEGS, count // SEGS, width).swapaxes(0, 1).reshape(count, width)


def from_major(rows):
    count, width = rows.shape
    return rows.reshape(count // SEGS, SEGS, width).swapaxes(0, 1).reshape(count, width)


def rows_kernel(a, b, out):
    out[...] = jnp.dot(a[...], b[...], preferred_element_type=F32).astype(BF16)


def rows_product(a, b):
    rows, inner = a.shape
    right = b.shape[1]
    size = min(256, rows)
    return pl.pallas_call(
        rows_kernel,
        grid=(rows // size,),
        out_shape=jax.ShapeDtypeStruct((rows, right), BF16),
        in_specs=[
            pl.BlockSpec((size, inner), lambda i: (i, 0)),
            pl.BlockSpec((inner, right), lambda i: (0, 0)),
        ],
        out_specs=pl.BlockSpec((size, right), lambda i: (i, 0)),
        compiler_params=pltpu.CompilerParams(vmem_limit_bytes=62 << 20),
    )(a, b)


def weight_kernel(plan, a, *refs):
    for out, parts in zip(refs[-len(plan) :], plan, strict=True):
        at = 0
        for i, first, last in parts:
            width = last - first
            out[:, at : at + width] = tn_dot(a[...], refs[i][:, first:last]).astype(BF16)
            at += width


def weight_products(a, sources, plan):
    rows, left = a.shape
    widths = [sum(last - first for _, first, last in parts) for parts in plan]
    size = next(t for t in (256, 128, left) if left % t == 0)
    return pl.pallas_call(
        functools.partial(weight_kernel, plan),
        grid=(left // size,),
        out_shape=[jax.ShapeDtypeStruct((left, width), BF16) for width in widths],
        in_specs=[pl.BlockSpec((rows, size), lambda i: (0, i))]
        + [pl.BlockSpec(b.shape, lambda i: (0, 0)) for b in sources],
        out_specs=[pl.BlockSpec((size, width), lambda i: (i, 0)) for width in widths],
        compiler_params=pltpu.CompilerParams(vmem_limit_bytes=62 << 20),
    )(a, *sources)


def tok_scatter(full, dim):
    return lax.psum_scatter(full, "tok", scatter_dimension=dim, tiled=True)


def close_kernel(
    input_in, wb_in, wg_in, wo_in, small, mlp, gain, taps, gate, wide, left_a, left_b, down,
    input_o, wb_o, wg_o, wo_o, gain_o, mlp_o, taps_o, convb_o, br_o, bi_o, decay_o, wr_o, wi_o,
    wgate_o, wup_o, wdown_o, sem,
):
    pairs = ((input_in, input_o), (wb_in, wb_o), (wg_in, wg_o), (wo_in, wo_o))
    copies = [pltpu.make_async_copy(a, b, sem.at[i]) for i, (a, b) in enumerate(pairs)]
    for copy in copies:
        copy.start()
    units = wgate_o.shape[1]
    cut = left_a.shape[1]

    def rows(at):
        span = pl.ds(at, 16)
        wgate_o[span, :] = wide[span, :units].astype(F32)
        wup_o[span, :cut] = left_a[span, :]
        wup_o[span, cut : 2 * cut] = left_b[span, :]
        wup_o[span, 2 * cut :] = wide[span, units:].astype(F32)

    over_rows(0, wgate_o.shape[0], 16, rows, 2)

    def tall_rows(at):
        span = pl.ds(at, 16)
        wdown_o[span, :] = down[span, :].astype(F32)

    over_rows(0, wdown_o.shape[0], 16, tall_rows, 4)
    for i, out in enumerate((decay_o, br_o, bi_o, convb_o)):
        out[...] = small[i, : out.shape[0]]
    gain_o[...] = gain[0, :]
    mlp_o[...] = mlp[0, :]
    taps_o[...] = taps[...]
    each, count = wr_o.shape[0], wr_o.shape[1]
    for half, out in enumerate((wr_o, wi_o)):
        for i in range(count):
            first = (half * count + i) * each
            out[:, i, :] = gate[first : first + each, :]
    for copy in copies:
        copy.wait()


def close(input_in, wb, wg, wo, small, mlp, gain, taps, gate, wide, left, down, chans, units, gates):
    width, block = gain.shape[1], gate.shape[1]
    each = gate.shape[0] // (2 * gates)
    anywhere = pl.BlockSpec(memory_space=pl.ANY)
    vmem = pl.BlockSpec(memory_space=pltpu.VMEM)

    def like(*shape):
        return jax.ShapeDtypeStruct(shape, F32)

    return pl.pallas_call(
        close_kernel,
        out_shape=[
            like(*input_in.shape), like(*wb.shape), like(*wg.shape), like(*wo.shape), like(width),
            like(width), like(*taps.shape), like(chans), like(chans), like(chans), like(chans),
            like(each, gates, block), like(each, gates, block), like(wide.shape[0], units),
            like(wide.shape[0], units), like(*down.shape),
        ],
        in_specs=[vmem] * 13,
        out_specs=[anywhere] * 4 + [vmem] * 12,
        scratch_shapes=[pltpu.SemaphoreType.DMA((4,))],
        compiler_params=pltpu.CompilerParams(vmem_limit_bytes=60 << 20),
    )(input_in, wb, wg, wo, small, mlp, gain, taps, gate, wide, *left, down)


def local(
    layer_in,
    positions,
    norm_gain,
    w_branch,
    w_gelu,
    conv_w,
    conv_b,
    w_rgate,
    b_rgate,
    w_igate,
    b_igate,
    decay_param,
    w_out,
    mlp_gain,
    w_gate,
    w_up,
    w_down,
    cotangent,
):
    rows, width = layer_in.shape
    ch_index = lax.axis_index("ch")
    column = ch_index * width
    chans = decay_param.shape[0]
    gates, gate_width = w_rgate.shape[0], w_rgate.shape[1]
    layer_in = to_major(layer_in)
    pos = positions.reshape(SEGS, rows // SEGS)
    (
        normed, scale_in, gate_pre, ext, conv, rate, igate, lru, branch, cot, vectors, dense_r,
        dense_i, pos_tall, cotangent,
    ) = front(
        layer_in, norm_gain[None], pos, w_branch, w_gelu, conv_w, conv_b, b_rgate, b_igate,
        decay_param, w_rgate.reshape(-1, gate_width), w_igate.reshape(-1, gate_width),
        cotangent, 0,
    )
    normed_mid, mid_full, mid_own, scale_mid, hidden, grad_gate, grad_up = mid_exchange(
        branch, w_out, layer_in, mlp_gain[None], w_gate, w_up, w_down, cot, 2
    )
    count = lax.axis_size("tok")
    total, units = cot.shape[1], hidden.shape[1]
    cut = units // 3
    (wdown_full,) = weight_products(hidden, (cot,), (((0, 0, total),),))
    grad_up, wdown_full = lax.optimization_barrier((grad_up, wdown_full))
    grad_wdown = tok_scatter(wdown_full, 1)
    wide_full, *wup_parts = weight_products(
        normed_mid,
        (grad_gate, grad_up),
        (((0, 0, units), (1, 2 * cut, units)), ((1, 0, cut),), ((1, cut, 2 * cut),)),
    )
    wide_sum = tok_scatter(wide_full, 0)
    hidden, wide_full = lax.optimization_barrier((hidden, wide_full))
    down = rows_product(hidden, w_down)
    grad_gate, down = lax.optimization_barrier((grad_gate, down))
    grad_block, grad_mid_own, gain_sum, *wup_left = back_exchange(
        grad_gate, grad_up, w_gate, w_up, mid_full, mid_own, cot, cotangent, scale_mid,
        mlp_gain[None], wup_parts, 3,
    )
    grad_rec, grad_gate_pre, gate_parts, sums, row_term, mlp_out, wout_carry = recur_bwd(
        grad_block, w_out, gate_pre, ext, conv, rate, igate, lru, pos_tall, conv_w, dense_r,
        dense_i, vectors, down, branch, gate_width, 4,
    )
    layer_out = from_major((mid_own + mlp_out).astype(BF16))
    grad_rec, layer_out = lax.optimization_barrier((grad_rec, layer_out))
    stat = row_term.reshape(8, rows // 8)
    small_width = max(chans, width)
    small = jnp.concatenate(
        [
            jnp.pad(sums, ((0, 0), (0, small_width - chans))),
            jnp.pad(
                jnp.sum(gain_sum, axis=0, keepdims=True), ((0, 7), (0, small_width - width))
            ),
        ],
        axis=0,
    )
    (
        input_grad, small_sum, norm_gain_sum, mlp_gain_sum, taps_sum, grad_wbranch, grad_wgelu,
        grad_wout, gate_sum,
    ) = end_exchange(
        grad_rec, grad_gate_pre, w_branch, w_gelu, stat, small, normed, wout_carry, gate_parts,
        layer_in, scale_in, norm_gain[None], grad_mid_own, 5,
    )
    (
        input_grad, grad_wbranch, grad_wgelu, grad_wout, own_norm_gain, own_mlp_gain, grad_taps,
        grad_convb, grad_brate, grad_binput, grad_decay, grad_wrate, grad_winput, grad_wgate,
        grad_wup, grad_wdown,
    ) = close(
        input_grad, grad_wbranch, grad_wgelu, grad_wout, small_sum, mlp_gain_sum, norm_gain_sum,
        taps_sum, gate_sum, wide_sum, wup_left, grad_wdown, chans, units, gates,
    )
    return (
        layer_out,
        input_grad,
        own_norm_gain,
        grad_wbranch,
        grad_wgelu,
        grad_taps,
        grad_convb,
        grad_wrate.swapaxes(0, 1),
        grad_brate,
        grad_winput.swapaxes(0, 1),
        grad_binput,
        grad_decay,
        grad_wout,
        own_mlp_gain,
        grad_wgate,
        grad_wup,
        grad_wdown,
    )


def solution(mesh):
    placed = (
        P("tok", "ch"),
        P("tok"),
        P(),
        P(None, "ch"),
        P(None, "ch"),
        P(None, "ch"),
        P("ch"),
        P("ch", None, None),
        P("ch"),
        P("ch", None, None),
        P("ch"),
        P("ch"),
        P("ch", None),
        P(),
        P(None, "ch"),
        P(None, "ch"),
        P("ch", None),
        P("tok", "ch"),
    )
    return jax.shard_map(
        local,
        mesh=mesh,
        in_specs=placed,
        out_specs=(
            P("tok", "ch"),
            P("tok", "ch"),
            P("ch"),
            P("tok", "ch"),
            P("tok", "ch"),
            P(None, "ch"),
            P("ch"),
            P("ch", "tok", None),
            P("ch"),
            P("ch", "tok", None),
            P("ch"),
            P("ch"),
            P("ch", "tok"),
            P("ch"),
            P("tok", "ch"),
            P("tok", "ch"),
            P("ch", "tok"),
        ),
        check_vma=False,
    )
```
